256 devices in a mesh: tm: 4 (over y), space: 64 (over x, z, core).
Axes of the slice: x: 4, y: 4, z: 8, core: 2. Of those that a mesh axis runs over, the one named last changes fastest.
Arguments:
- initial_state: float32 [3, 128, 128, 128], P(None, 'space'), may hold values from -6 to 6
- end_states: float32 [4, 3, 128, 128, 128], P('tm', None, 'space'), may hold values from -6 to 6
- old_tendencies: float32 [4, 3, 3, 128, 128, 128], P('tm', None, None, 'space'), may hold values from -6 to 6
Outputs:
- node_states: float32 [4, 3, 3, 128, 128, 128], P('tm', None, None, 'space')
- q_field: float32 [4, 128, 128, 128], P('tm', 'space')
The draws below stay inside these ranges and needn't reach their ends.
All inputs are finite; a program needn't handle non-finite values.
Results may differ from the reference program's by a relative error of at most 0.00014.
Values sent between devices are 32-bit elements; how exact they have to be, the bound alone decides.
A program may use at most 128 MiB of HBM per device.

```python
import math
import jax
import jax.numpy as jnp
from jax import lax

NX = 128
NY = 128
NZ = 128
SLICES = 4


def block_levels(key, shape, shards, least, top_value):
    def one(dim, parts):
        heights = jax.random.uniform(jax.random.fold_in(jax.random.fold_in(key, 6), dim), (parts,), jnp.float32, least / len(shards), top_value / len(shards))
        return jnp.repeat(jnp.exp(heights), shape[dim] // parts).reshape((-1,) + (1,) * (len(shape) - dim - 1))

    factor_of = one(*shards[0])
    for cut in shards[1:]:
        factor_of = factor_of * one(*cut)
    return factor_of


def gaussian(own_key, dims, deviation, limit, pieces=(), kind=jnp.bfloat16):
    loudness = block_levels(own_key, dims, pieces, -0.22, 0.18) if pieces else 1.0
    result = jax.random.normal(own_key, dims, jnp.float32) * deviation * loudness
    return jnp.minimum(jnp.maximum(result, -limit), limit).astype(kind)


def setup_inputs(seed: int = 0) -> dict:
    streams_of = jax.random.split(jax.random.key(seed), 4)
    initial_state = gaussian(streams_of[0], (3, NZ, NX, NY), 1.0, 6.0, ((1, 64),), jnp.float32)
    end_states = gaussian(streams_of[1], (SLICES, 3, NZ, NX, NY), 1.0, 6.0, ((0, 4), (2, 64)), jnp.float32)
    old_tendencies = gaussian(streams_of[2], (SLICES, 3, 3, NZ, NX, NY), 1.0, 6.0, ((0, 4), (3, 64)), jnp.float32)
    return dict(initial_state=initial_state, end_states=end_states, old_tendencies=old_tendencies)


slice_time = 0.4
viscosity = 0.1
exact_mode = lax.Precision.HIGHEST
two_pi = 2.0 * math.pi


def trig_tables(point_count, mode_count):
    points = jnp.arange(point_count, dtype=jnp.int32)[:, None]
    wave_ids = jnp.arange(mode_count, dtype=jnp.int32)[None, :]
    angles = (two_pi / point_count) * ((points * wave_ids) % point_count).astype(jnp.float32)
    return jnp.cos(angles), jnp.sin(angles)


def restrict_table(point_count):
    coarse_count = point_count // 2
    kept_count = coarse_count // 2
    cos_coarse, sin_coarse = trig_tables(coarse_count, kept_count)
    cos_fine, sin_fine = trig_tables(point_count, kept_count)
    weight = jnp.where(jnp.arange(kept_count) == 0, 1.0, 2.0).astype(jnp.float32)
    trig_sum = jnp.dot(cos_coarse * weight, cos_fine.T, precision=exact_mode) + jnp.dot(sin_coarse * weight, sin_fine.T, precision=exact_mode)
    return trig_sum / point_count


def restrict(values):
    row_table = restrict_table(values.shape[-2])
    col_table = restrict_table(values.shape[-1])
    return jnp.einsum("jx,...xy,ly->...jl", row_table, values, col_table, precision=exact_mode)


def prolong(values):
    row_table = restrict_table(2 * values.shape[-2])
    col_table = restrict_table(2 * values.shape[-1])
    return 4.0 * jnp.einsum("jx,...jl,ly->...xy", row_table, values, col_table, precision=exact_mode)


def first_roll(values, axis_dim, spacing):
    return (jnp.roll(values, 2, axis_dim) - 8.0 * jnp.roll(values, 1, axis_dim) + 8.0 * jnp.roll(values, -1, axis_dim) - jnp.roll(values, -2, axis_dim)) / (12.0 * spacing)


def second_roll(values, axis_dim, spacing):
    return (16.0 * (jnp.roll(values, 1, axis_dim) + jnp.roll(values, -1, axis_dim)) - (jnp.roll(values, 2, axis_dim) + jnp.roll(values, -2, axis_dim)) - 30.0 * values) / (12.0 * spacing * spacing)


def signed_ids(point_count):
    plain = jnp.arange(point_count, dtype=jnp.int32)
    return jnp.where(plain < point_count // 2, plain, plain - point_count)


def biot_savart(vort, spacing):
    slab_depth, row_count, col_count = vort.shape[1], vort.shape[2], vort.shape[3]
    spectrum = jnp.fft.rfftn(vort, axes=(1, 2, 3))
    signed_z = signed_ids(slab_depth)
    signed_x = signed_ids(row_count)
    plain_y = jnp.arange(col_count // 2 + 1, dtype=jnp.int32)
    wave_z = ((two_pi / slab_depth) * signed_z.astype(jnp.float32))[:, None, None]
    wave_x = ((two_pi / (row_count * spacing)) * signed_x.astype(jnp.float32))[None, :, None]
    wave_y = ((two_pi / (col_count * spacing)) * plain_y.astype(jnp.float32))[None, None, :]
    squared = wave_x * wave_x + wave_y * wave_y + wave_z * wave_z
    kept_modes = (signed_z != -(slab_depth // 2))[:, None, None] & (signed_x != -(row_count // 2))[None, :, None] & (plain_y < col_count // 2)[None, None, :] & (squared > 0)
    inverse = jnp.where(kept_modes, 1.0 / jnp.where(kept_modes, squared, 1.0), 0.0)
    cross_x = wave_y * spectrum[2] - wave_z * spectrum[1]
    cross_y = wave_z * spectrum[0] - wave_x * spectrum[2]
    cross_z = wave_x * spectrum[1] - wave_y * spectrum[0]
    hat_field = 1j * jnp.stack([cross_x, cross_y, cross_z]) * inverse
    return jnp.fft.irfftn(hat_field, s=(slab_depth, row_count, col_count), axes=(1, 2, 3)).astype(jnp.float32)


def tendency(vort, spacing):
    velocity = biot_savart(vort, spacing)
    flux_x = velocity[1] * vort[2] - velocity[2] * vort[1]
    flux_y = velocity[2] * vort[0] - velocity[0] * vort[2]
    flux_z = velocity[0] * vort[1] - velocity[1] * vort[0]
    curl_vec = jnp.stack([
        first_roll(flux_z, -1, spacing) - first_roll(flux_y, -3, 1.0),
        first_roll(flux_x, -3, 1.0) - first_roll(flux_z, -2, spacing),
        first_roll(flux_y, -2, spacing) - first_roll(flux_x, -1, spacing)])
    laplacian = second_roll(vort, -2, spacing) + second_roll(vort, -1, spacing) + second_roll(vort, -3, 1.0)
    return curl_vec + viscosity * laplacian


def criterion(velocity):
    gradient = []
    for comp_num in range(3):
        gradient.append([first_roll(velocity[comp_num], -2, 1.0), first_roll(velocity[comp_num], -1, 1.0), first_roll(velocity[comp_num], -3, 1.0)])
    accum = jnp.zeros(velocity.shape[1:], jnp.float32)
    for first_axis in range(3):
        for second_axis in range(3):
            accum = accum + gradient[first_axis][second_axis] * gradient[second_axis][first_axis]
    return -0.5 * accum


def reference(initial_state, end_states, old_tendencies):
    half_step = 0.5 * slice_time
    chain_value = restrict(initial_state)
    all_nodes = []
    all_fields = []
    for slice_num in range(SLICES):
        if slice_num == 0:
            start_node = initial_state
        else:
            start_node = end_states[slice_num - 1]
        previous = old_tendencies[slice_num]
        tend_zero = tendency(start_node, 1.0)
        middle_node = start_node + half_step * (tend_zero - previous[0]) + slice_time * ((5.0 / 24.0) * previous[0] + (1.0 / 3.0) * previous[1] - (1.0 / 24.0) * previous[2])
        tend_one = tendency(middle_node, 1.0)
        end_node = middle_node + half_step * (tend_one - previous[1]) + slice_time * (-(1.0 / 24.0) * previous[0] + (1.0 / 3.0) * previous[1] + (5.0 / 24.0) * previous[2])
        tend_two = tendency(end_node, 1.0)
        coarse_zero = restrict(start_node)
        coarse_two = restrict(end_node)
        base_zero = tendency(coarse_zero, 2.0)
        base_two = tendency(coarse_two, 2.0)
        correction = restrict(slice_time * (tend_zero / 6.0 + (2.0 / 3.0) * tend_one + tend_two / 6.0)) - half_step * (base_zero + base_two)
        coarse_start = chain_value
        early_tend = tendency(coarse_start, 2.0)
        coarse_end = coarse_start + slice_time * (early_tend - base_zero) + half_step * (base_zero + base_two) + correction
        later_tend = tendency(coarse_end, 2.0)
        coarse_end = coarse_start + half_step * (early_tend + later_tend) + correction
        chain_value = coarse_end
        delta_zero = prolong(coarse_start - coarse_zero)
        delta_one = prolong(coarse_end - coarse_two)
        new_zero = start_node + delta_zero
        new_one = middle_node + 0.5 * (delta_zero + delta_one)
        new_two = end_node + delta_one
        all_nodes.append(jnp.stack([new_zero, new_one, new_two]))
        all_fields.append(criterion(biot_savart(new_two, 1.0)))
    return jnp.stack(all_nodes), jnp.stack(all_fields)
```

```python
import math

import jax
import jax.numpy as jnp
import numpy as np
from jax import lax
from jax.experimental import pallas as pl
from jax.experimental.pallas import tpu as pltpu
from jax.sharding import PartitionSpec as P

DT = 0.4
HALF = 0.2
NU = 0.1
PARTS = 64
ROWS = 4
N = 128
M = 64
FINE = 12
COARSE = 3
f32 = jnp.float32
MESH = pl.DeviceIdType.MESH


def angle_tables(left, right, count):
    angles = (2.0 * math.pi / count) * (np.outer(left, right) % count)
    return np.cos(angles), np.sin(angles)


def restriction_table(count):
    cos_c, sin_c = angle_tables(np.arange(count // 2), np.arange(count // 4), count // 2)
    cos_f, sin_f = angle_tables(np.arange(count), np.arange(count // 4), count)
    weight = np.where(np.arange(count // 4) == 0, 1.0, 2.0)
    return ((cos_c * weight) @ cos_f.T + (sin_c * weight) @ sin_f.T) / count


def twice(block):
    zero = np.zeros_like(block)
    return np.block([[block, zero], [zero, block]])


def wave_symbols(ids, count, spacing):
    theta = 2.0 * math.pi * ids / count
    kappa = theta / spacing
    first = (8.0 * np.sin(theta) - np.sin(2.0 * theta)) / (6.0 * spacing)
    second = (-2.0 * np.cos(2.0 * theta) + 32.0 * np.cos(theta) - 30.0) / (12.0 * spacing**2)
    return kappa, first, second


def signed(ids, count):
    return np.where(ids < count // 2, ids, ids - count)


def build_tables():
    t = {}
    grid = np.arange(N)
    owner = np.concatenate([2 * np.arange(PARTS), 2 * np.arange(PARTS) + 1])
    cos_y, sin_y = angle_tables(grid, np.arange(M), N)
    t["f_y"] = np.hstack([cos_y, -sin_y, -sin_y, -cos_y])
    t["f_x"] = np.hstack(angle_tables(owner, grid, N))
    t["f_z"] = np.hstack(angle_tables(grid, owner, N))
    t["i_z"] = np.hstack(angle_tables(owner, grid, N))
    t["i_x"] = np.hstack(angle_tables(grid, owner, N))
    weight = np.where(np.arange(M) == 0, 1.0, 2.0) / float(N**3)
    wc, ws = (cos_y * weight).T, (sin_y * weight).T
    t["i_y"] = np.hstack([np.vstack([wc, -ws]), np.vstack([-ws, -wc])])
    half = np.arange(M // 2)
    cos_y, sin_y = angle_tables(np.arange(M), half, M)
    t["cf_y"] = np.hstack([twice(np.hstack([cos_y, -sin_y])), twice(np.hstack([-sin_y, -cos_y]))])
    t["c_x"] = np.hstack(angle_tables(np.arange(M), np.arange(M), M))
    weight = np.where(half == 0, 1.0, 2.0) / float(M * M * N)
    wc, ws = (cos_y * weight).T, (sin_y * weight).T
    t["ci_y"] = np.hstack([twice(np.vstack([wc, -ws])), twice(np.vstack([-ws, -wc]))])
    table = restriction_table(N)
    t["r_x"] = table
    t["r_y"] = twice(table.T)
    t["p_x"] = 4.0 * table.T
    t["p_y"] = twice(table)
    kx, _, _ = wave_symbols(signed(grid, N), N, 1.0)
    ky = np.tile(kx[:M], 2)[None, :]
    ones = np.ones((1, N))
    t["f_kx"] = kx[:, None] * ones
    t["f_mx"] = (grid != M)[:, None] * ones
    t["f_ky"] = np.repeat(ky, 8, axis=0)
    t["f_kz"] = kx[:, None] * ones
    t["f_kk"] = ky**2 + kx[:, None] ** 2
    t["f_mz"] = t["f_mx"]
    ckx, sx, lx = wave_symbols(signed(np.arange(M), M), M, 2.0)
    t["c_kx"] = ckx[:, None] * ones
    t["c_mx"] = (np.arange(M) != M // 2)[:, None] * ones
    t["c_sx"] = sx[:, None] * ones
    t["c_lx"] = lx[:, None] * ones
    lane = lambda v: np.tile(v[: M // 2], 4)[None, :]
    cky, sy, ly = lane(ckx), lane(sx), lane(lx)
    zid = np.hstack([np.repeat(np.arange(M)[:, None], M, 1), np.repeat(np.arange(M)[:, None] + M, M, 1)])
    ckz, sz, lz = wave_symbols(signed(zid, N), N, 1.0)
    t["c_ky"] = np.repeat(cky, 8, axis=0)
    t["c_sy"] = np.repeat(sy, 8, axis=0)
    t["c_kz"] = ckz
    t["c_sz"] = sz
    t["c_kk"] = cky**2 + ckz**2
    t["c_mz"] = (zid != M) * 1.0
    t["c_ll"] = ly + lz
    turn = 2.0 * math.pi * np.arange(M)[:, None] / N
    first = (np.arange(N) < M)[None, :]
    t["tw_c"] = np.where(first, 1.0, np.cos(turn))
    t["tw_s"] = np.where(first, 0.0, np.sin(turn))
    made = {}
    for name, value in t.items():
        value = np.asarray(value, np.float32)
        if name in SPLIT:
            high = value.astype(jnp.bfloat16)
            made[name + "_h"] = high
            made[name + "_l"] = (value - high.astype(np.float32)).astype(jnp.bfloat16)
        else:
            made[name] = value
    return made


SPLIT = ("f_x", "f_y", "f_z", "i_x", "i_y", "i_z", "cf_y", "c_x", "ci_y")
TABLES = build_tables()
NAMES = tuple(sorted(TABLES))


def exact(a, b):
    return jnp.dot(a, b, precision=lax.Precision.HIGHEST, preferred_element_type=f32)


def dot(a, b):
    return jnp.dot(a, b, preferred_element_type=f32)


def split(x):
    high = x.astype(jnp.bfloat16)
    return high, (x - high.astype(f32)).astype(jnp.bfloat16)


def by_table(x, t, name):
    high, low = split(x)
    table = t[name + "_h"][...]
    return dot(high, table) + (dot(low, table) + dot(high, t[name + "_l"][...]))


def table_by(t, name, x):
    high, low = split(x)
    table = t[name + "_h"][...]
    return dot(table, high) + (dot(table, low) + dot(t[name + "_l"][...], high))


def roll(x, shift, axis):
    return pltpu.roll(x, shift % x.shape[axis], axis)


def lanes(shape):
    return lax.broadcasted_iota(jnp.int32, shape, 1)


def stacked(a, b):
    return jnp.concatenate([a, b], axis=0)


def both_halves(wide):
    return stacked(wide[:, :N], wide[:, N:])


def turn_back(x):
    swapped = roll(x, M, 1)
    return jnp.where(lanes(x.shape) < M, swapped, -swapped)


def turn_back_c(x):
    is_real = (lanes(x.shape) % M) < M // 2
    return jnp.where(is_real, roll(x, -M // 2, 1), -roll(x, M // 2, 1))


def butterfly(x):
    return jnp.where(lanes(x.shape) < M, x, -x) + roll(x, M, 1)


def cross(a, b):
    return (
        a[1] * b[2] - a[2] * b[1],
        a[2] * b[0] - a[0] * b[2],
        a[0] * b[1] - a[1] * b[0],
    )


def first_fine(f, axis):
    return (roll(f, 2, axis) - roll(f, -2, axis) + 8.0 * (roll(f, -1, axis) - roll(f, 1, axis))) * (
        1.0 / 12.0
    )


def second_fine_xy(f):
    near = (roll(f, 1, 0) + roll(f, -1, 0)) + (roll(f, 1, 1) + roll(f, -1, 1))
    far = (roll(f, 2, 0) + roll(f, -2, 0)) + (roll(f, 2, 1) + roll(f, -2, 1))
    return (16.0 * near - far - 60.0 * f) * (1.0 / 12.0)


def roll_half(f, shift):
    place = lanes(f.shape) % M
    keep = place >= shift if shift > 0 else place < M + shift
    return jnp.where(keep, roll(f, shift, 1), roll(f, shift - M if shift > 0 else shift + M, 1))


def first_coarse(f, along_x):
    go = (lambda s: roll(f, s, 0)) if along_x else (lambda s: roll_half(f, s))
    return (go(2) - go(-2) + 8.0 * (go(-1) - go(1))) * (1.0 / 24.0)


def second_coarse_xy(f):
    near = (roll(f, 1, 0) + roll(f, -1, 0)) + (roll_half(f, 1) + roll_half(f, -1))
    far = (roll(f, 2, 0) + roll(f, -2, 0)) + (roll_half(f, 2) + roll_half(f, -2))
    return (16.0 * near - far - 60.0 * f) * (1.0 / 48.0)


def first_next(a, b):
    return (a - 8.0 * b) * (1.0 / 12.0), b * (1.0 / 12.0)


def first_prev(a, b):
    return a * (-1.0 / 12.0), (8.0 * a - b) * (1.0 / 12.0)


def first_own(a, b):
    return b * (8.0 / 12.0), a * (-8.0 / 12.0)


def second_next(a, b):
    return (16.0 * b - a) * (1.0 / 12.0), b * (-1.0 / 12.0)


def second_prev(a, b):
    return a * (-1.0 / 12.0), (16.0 * a - b) * (1.0 / 12.0)


def second_own(a, b):
    return (16.0 * b - 30.0 * a) * (1.0 / 12.0), (16.0 * a - 30.0 * b) * (1.0 / 12.0)


def lane_pair(f, low, high):
    is_low = lanes(f.shape) < M
    own = jnp.where(is_low, low[0], high[0]).astype(f32)
    other = jnp.where(is_low, low[1], high[1]).astype(f32)
    return f * own + roll(f, M, 1) * other


T12 = 1.0 / 12.0


def c_first_next(f):
    return lane_pair(f, (T12, -8 * T12), (T12, 0.0))


def c_first_prev(f):
    return lane_pair(f, (-T12, 0.0), (-T12, 8 * T12))


def c_first_own(f):
    return lane_pair(f, (0.0, 8 * T12), (0.0, -8 * T12))


def c_second_next(f):
    return lane_pair(f, (-T12, 16 * T12), (-T12, 0.0))


def c_second_prev(f):
    return lane_pair(f, (-T12, 0.0), (-T12, 16 * T12))


def c_second_own(f):
    return lane_pair(f, (-30 * T12, 16 * T12), (-30 * T12, 16 * T12))


def forward_fine(plane, t):
    return table_by(t, "f_x", both_halves(by_table(plane, t, "f_y")))


def inverse_fine(modes, t):
    return table_by(t, "i_x", both_halves(by_table(modes, t, "i_y")))


def forward_coarse(pair, t):
    return table_by(t, "c_x", both_halves(by_table(pair, t, "cf_y")))


def inverse_coarse(modes, t):
    return table_by(t, "c_x", both_halves(by_table(modes, t, "ci_y")))


def solve_fine(planes, kx, mx, t):
    hat = [table_by(t, "f_z", stacked(p, turn_back(p))) for p in planes]
    kz = t["f_kz"][...]
    ky = jnp.broadcast_to(t["f_ky"][0:1, :], kz.shape)
    squared = t["f_kk"][...] + kx * kx
    live = squared > 0.0
    inverse = jnp.where(live, t["f_mz"][...] * mx / jnp.where(live, squared, 1.0), 0.0)
    out = []
    for r in cross((kx, ky, kz), hat):
        r = r * inverse
        out.append(table_by(t, "i_z", stacked(-turn_back(r), -r)))
    return out


def z_coarse(x, t):
    d = table_by(t, "c_x", stacked(x, turn_back_c(x)))
    return butterfly(t["tw_c"][...] * d + t["tw_s"][...] * turn_back_c(d))


def z_coarse_back(a, t):
    b = butterfly(a)
    b = t["tw_c"][...] * b - t["tw_s"][...] * turn_back_c(b)
    return table_by(t, "c_x", stacked(b, -turn_back_c(b)))


def velocity_modes(hat, kx, mx, t):
    kz = t["c_kz"][...]
    ky = jnp.broadcast_to(t["c_ky"][0:1, :], kz.shape)
    squared = t["c_kk"][...] + kx * kx
    live = squared > 0.0
    inverse = jnp.where(live, t["c_mz"][...] * mx / jnp.where(live, squared, 1.0), 0.0)
    return [-turn_back_c(r * inverse) for r in cross((kx, ky, kz), hat)]


def tendency_modes(flux, w, sx, lx, t):
    sz = t["c_sz"][...]
    sy = jnp.broadcast_to(t["c_sy"][0:1, :], sz.shape)
    spread = NU * (t["c_ll"][...] + lx)
    return [-turn_back_c(r) + spread * w[i] for i, r in enumerate(cross((sx, sy, sz), flux))]


def restrict(a, b, t):
    return exact(t["r_x"][...], exact(jnp.concatenate([a, b], axis=1), t["r_y"][...]))


def prolong(pair, t):
    wide = exact(exact(t["p_x"][...], pair), t["p_y"][...])
    return wide[:, :N], wide[:, N:]


SCRATCH = dict(
    node=pltpu.VMEM((3, 3, 2, N, N), f32),
    speed=pltpu.VMEM((3, 2, N, N), f32),
    flux=pltpu.VMEM((3, 2, N, N), f32),
    total=pltpu.VMEM((3, 2, N, N), f32),
    slope=pltpu.VMEM((3, 2, N, N), f32),
    fs=pltpu.VMEM((6, PARTS * FINE, N), f32),
    fr=pltpu.VMEM((6, PARTS * FINE, N), f32),
    cs=pltpu.VMEM((6, PARTS * COARSE, N), f32),
    cr=pltpu.VMEM((6, PARTS * COARSE, N), f32),
    fh_next=pltpu.VMEM((4, 3, 2, N, N), f32),
    fh_prev=pltpu.VMEM((4, 3, 2, N, N), f32),
    fh_low=pltpu.VMEM((4, 3, 2, N, N), f32),
    fh_high=pltpu.VMEM((4, 3, 2, N, N), f32),
    ch_next=pltpu.VMEM((5, 3, M, N), f32),
    ch_prev=pltpu.VMEM((5, 3, M, N), f32),
    ch_low=pltpu.VMEM((5, 3, M, N), f32),
    ch_high=pltpu.VMEM((5, 3, M, N), f32),
    hand_v=pltpu.VMEM((3, M, N), f32),
    hand_u=pltpu.VMEM((3, M, N), f32),
    hand_m=pltpu.VMEM((3, M, N), f32),
    send_v=pltpu.VMEM((3, M, N), f32),
    send_u=pltpu.VMEM((3, M, N), f32),
    send_m=pltpu.VMEM((3, M, N), f32),
    co=pltpu.VMEM((14, 3, M, N), f32),
    f_ssem=pltpu.SemaphoreType.DMA((6,)),
    f_rsem=pltpu.SemaphoreType.DMA((6,)),
    c_ssem=pltpu.SemaphoreType.DMA((6,)),
    c_rsem=pltpu.SemaphoreType.DMA((6,)),
    h_ssem=pltpu.SemaphoreType.DMA((9, 2)),
    h_rsem=pltpu.SemaphoreType.DMA((9, 2)),
    y_ssem=pltpu.SemaphoreType.DMA((4,)),
    y_rsem=pltpu.SemaphoreType.DMA((4,)),
)
A0, A2, UA0, UA2, G0, G2, C1, C2, CM1, CM2, B1, S1, BM1, SM1 = range(14)


def kernel(*refs):
    count = len(NAMES)
    init, end, old = refs[:3]
    t = dict(zip(NAMES, refs[3 : 3 + count]))
    nodes, q_out = refs[3 + count : 5 + count]
    s = dict(zip(SCRATCH, refs[5 + count :]))
    co = s["co"]
    row = lax.axis_index("tm")
    me = lax.axis_index("space")
    ahead = lax.rem(me + 1, PARTS)
    behind = lax.rem(me + PARTS - 1, PARTS)
    up = lax.rem(row + 1, ROWS)
    down = lax.rem(row + ROWS - 1, ROWS)

    barrier = pltpu.get_barrier_semaphore()

    def greet(k, carry):
        pl.semaphore_signal(barrier, inc=1, device_id=(row, lax.rem(me + k, PARTS)), device_id_type=MESH)
        return carry

    lax.fori_loop(1, PARTS, greet, 0)
    pl.semaphore_signal(barrier, inc=1, device_id=(up, me), device_id_type=MESH)
    pl.semaphore_signal(barrier, inc=1, device_id=(down, me), device_id_type=MESH)
    pl.semaphore_wait(barrier, PARTS + 1)


    def transpose_start(send, recv, depth, ssem, rsem):
        mine = pl.ds(me * depth, depth)
        pltpu.make_async_copy(send.at[mine], recv.at[mine], rsem).start()

        def step(k, carry):
            to = lax.rem(me + k, PARTS)
            pltpu.make_async_remote_copy(
                src_ref=send.at[pl.ds(to * depth, depth)],
                dst_ref=recv.at[mine],
                send_sem=ssem,
                recv_sem=rsem,
                device_id=(row, to),
                device_id_type=MESH,
            ).start()
            return carry

        lax.fori_loop(1, PARTS, step, 0)

    def arrived(ref, sem):
        pltpu.make_async_copy(ref, ref, sem).wait()

    def left(ref, depth, sem):
        part = ref.at[pl.ds(0, (PARTS - 1) * depth)]
        pltpu.make_async_copy(part, part, sem).wait()

    def fine_start(i):
        transpose_start(s["fs"].at[i], s["fr"].at[i], FINE, s["f_ssem"].at[i], s["f_rsem"].at[i])

    def coarse_start(i):
        transpose_start(s["cs"].at[i], s["cr"].at[i], COARSE, s["c_ssem"].at[i], s["c_rsem"].at[i])

    def fine_wait(i):
        arrived(s["fr"].at[i], s["f_rsem"].at[i])

    def coarse_wait(i):
        arrived(s["cr"].at[i], s["c_rsem"].at[i])

    def halo_copies(kind, i, sem):
        return (
            pltpu.make_async_remote_copy(
                src_ref=s[kind + "h_next"].at[i],
                dst_ref=s[kind + "h_low"].at[i],
                send_sem=s["h_ssem"].at[sem, 0],
                recv_sem=s["h_rsem"].at[sem, 0],
                device_id=(row, ahead),
                device_id_type=MESH,
            ),
            pltpu.make_async_remote_copy(
                src_ref=s[kind + "h_prev"].at[i],
                dst_ref=s[kind + "h_high"].at[i],
                send_sem=s["h_ssem"].at[sem, 1],
                recv_sem=s["h_rsem"].at[sem, 1],
                device_id=(row, behind),
                device_id_type=MESH,
            ),
        )

    def halo_start(kind, i, sem):
        for copy in halo_copies(kind, i, sem):
            copy.start()

    def halo_wait(kind, i, sem):
        for copy in halo_copies(kind, i, sem):
            copy.wait_recv()

    def halo_left(kind, i, sem):
        for copy in halo_copies(kind, i, sem):
            copy.wait_send()

    def hand_copy(src, dst, sem):
        return pltpu.make_async_remote_copy(
            src_ref=src,
            dst_ref=dst,
            send_sem=s["y_ssem"].at[sem],
            recv_sem=s["y_rsem"].at[sem],
            device_id=(up, me),
            device_id_type=MESH,
        )

    start_copy = hand_copy(end.at[0], s["node"].at[0], 0)
    v_copy = hand_copy(s["send_v"], s["hand_v"], 1)
    u_copy = hand_copy(s["send_u"], s["hand_u"], 2)
    m_copy = hand_copy(s["send_m"], s["hand_m"], 3)
    is_first = row == 0
    has_next = row < ROWS - 1


    def fine_send(get, i):
        for c in range(3):
            for z in range(2):
                out = forward_fine(get(c, z), t)
                for low in range(2):
                    s["fs"][i, pl.ds((c * 2 + z) * 2 + low, PARTS, stride=FINE), :] = out[low * M : low * M + M]

    def fine_modes(i):
        for low in range(2):
            planes = [
                stacked(
                    s["fr"][i, pl.ds((c * 2) * 2 + low, PARTS, stride=FINE), :],
                    s["fr"][i, pl.ds((c * 2 + 1) * 2 + low, PARTS, stride=FINE), :],
                )
                for c in range(3)
            ]
            at = pl.ds(me * 2 + low, 1)
            kx = jnp.broadcast_to(t["f_kx"][at, :], (N, N))
            mx = jnp.broadcast_to(t["f_mx"][at, :], (N, N))
            for c, out in enumerate(solve_fine(planes, kx, mx, t)):
                for z in range(2):
                    s["fs"][i + 1, pl.ds((c * 2 + z) * 2 + low, PARTS, stride=FINE), :] = out[z * M : z * M + M]

    def fine_velocity(i):
        for c in range(3):
            for z in range(2):
                at = (c * 2 + z) * 2
                modes = stacked(
                    s["fr"][i, pl.ds(at, PARTS, stride=FINE), :],
                    s["fr"][i, pl.ds(at + 1, PARTS, stride=FINE), :],
                )
                s["speed"][c, z] = inverse_fine(modes, t)

    node, speed, flux, total = s["node"], s["speed"], s["flux"], s["total"]

    def fine_flux(m):
        for z in range(2):
            parts = cross([speed[c, z] for c in range(3)], [node[m, c, z] for c in range(3)])
            for c in range(3):
                flux[c, z] = parts[c]
        for c in range(3):
            w0, w1 = node[m, c, 0], node[m, c, 1]
            ahead0, ahead1 = second_next(w0, w1)
            back0, back1 = second_prev(w0, w1)
            ahead0, ahead1, back0, back1 = NU * ahead0, NU * ahead1, NU * back0, NU * back1
            if c < 2:
                sign = -1.0 if c == 0 else 1.0
                g0, g1 = sign * flux[1 - c, 0], sign * flux[1 - c, 1]
                d0, d1 = first_next(g0, g1)
                e0, e1 = first_prev(g0, g1)
                ahead0, ahead1, back0, back1 = ahead0 + d0, ahead1 + d1, back0 + e0, back1 + e1
            s["fh_next"][m, c, 0] = ahead0
            s["fh_next"][m, c, 1] = ahead1
            s["fh_prev"][m, c, 0] = back0
            s["fh_prev"][m, c, 1] = back1
        halo_start("f", m, m)

    def fine_local(m, c):
        w0, w1 = node[m, c, 0], node[m, c, 1]
        own = [NU * v for v in second_own(w0, w1)]
        if c < 2:
            sign = -1.0 if c == 0 else 1.0
            extra = first_own(sign * flux[1 - c, 0], sign * flux[1 - c, 1])
            own = [own[z] + extra[z] for z in range(2)]
        out = []
        for z in range(2):
            if c == 0:
                curl = first_fine(flux[2, z], 1)
            elif c == 1:
                curl = -first_fine(flux[2, z], 0)
            else:
                curl = first_fine(flux[1, z], 0) - first_fine(flux[0, z], 1)
            out.append(curl + NU * second_fine_xy((w0, w1)[z]) + own[z])
        return out


    def coarse_send(values, i):
        for c in range(3):
            s["cs"][i, pl.ds(c, PARTS, stride=COARSE), :] = forward_coarse(values[c], t)

    def coarse_recv(i):
        return [s["cr"][i, pl.ds(c, PARTS, stride=COARSE), :] for c in range(3)]

    def coarse_modes(i):
        return [z_coarse(x, t) for x in coarse_recv(i)]

    def coarse_velocity(i):
        return [inverse_coarse(x, t) for x in coarse_recv(i)]

    mine = pl.ds(me, 1)
    wide = lambda name: jnp.broadcast_to(t[name][mine, :], (M, N))

    def coarse_back(hat, i):
        modes = velocity_modes(hat, wide("c_kx"), wide("c_mx"), t)
        for c in range(3):
            s["cs"][i, pl.ds(c, PARTS, stride=COARSE), :] = z_coarse_back(modes[c], t)

    def coarse_flux(u, w, i):
        f = cross(u, w)
        g = (-f[1], f[0], None)
        for c in range(3):
            nxt, prv = NU * c_second_next(w[c]), NU * c_second_prev(w[c])
            if g[c] is not None:
                nxt, prv = nxt + c_first_next(g[c]), prv + c_first_prev(g[c])
            s["ch_next"][i, c] = nxt
            s["ch_prev"][i, c] = prv
        halo_start("c", i, 4 + i)
        return f

    def coarse_tendency(f, w, i):
        own = [NU * (second_coarse_xy(w[c]) + c_second_own(w[c])) for c in range(3)]
        parts = [
            first_coarse(f[2], False) - c_first_own(f[1]),
            c_first_own(f[0]) - first_coarse(f[2], True),
            first_coarse(f[1], True) - first_coarse(f[0], False),
        ]
        halo_wait("c", i, 4 + i)
        return [own[c] + parts[c] + (s["ch_low"][i, c] + s["ch_high"][i, c]) for c in range(3)]

    def keep(i, values):
        for c in range(3):
            co[i, c] = values[c]

    def kept(i):
        return [co[i, c] for c in range(3)]

    def restricted(get):
        return [restrict(get(c, 0), get(c, 1), t) for c in range(3)]


    @pl.when(has_next)
    def _():
        start_copy.start()

    @pl.when(is_first)
    def _():
        for c in range(3):
            for z in range(2):
                node[0, c, z] = init[c, z]

    @pl.when(jnp.logical_not(is_first))
    def _():
        start_copy.wait_recv()

    f0 = lambda c, z: old[0, 0, c, z]
    f1 = lambda c, z: old[0, 1, c, z]
    f2 = lambda c, z: old[0, 2, c, z]

    for m in range(3):
        fine_send(lambda c, z: node[m, c, z], 2 * m)
        fine_start(2 * m)
        if m == 0:
            keep(A0, restricted(lambda c, z: node[0, c, z]))
        if m == 1:
            keep(UA0, restricted(lambda c, z: speed[c, z]))
            flux_g0 = coarse_flux(kept(UA0), kept(A0), 0)
            keep(G0, coarse_tendency(flux_g0, kept(A0), 0))
        if m == 2:
            keep(A2, restricted(lambda c, z: node[2, c, z]))
        fine_wait(2 * m)
        fine_modes(2 * m)
        fine_start(2 * m + 1)
        fine_wait(2 * m + 1)
        fine_velocity(2 * m + 1)
        fine_flux(m)
        if m == 2:
            keep(UA2, restricted(lambda c, z: speed[c, z]))
            flux_g2 = coarse_flux(kept(UA2), kept(A2), 1)
        weight = (DT / 6.0, DT * 2.0 / 3.0, DT / 6.0)[m]
        if m < 2:
            for c in range(3):
                local = fine_local(m, c)
                for z in range(2):
                    total[c, z] = weight * local[z] if m == 0 else total[c, z] + weight * local[z]
                    if m == 0:
                        old_part = (
                            (DT * 5.0 / 24.0 - HALF) * f0(c, z)
                            + (DT / 3.0) * f1(c, z)
                            - (DT / 24.0) * f2(c, z)
                        )
                    else:
                        old_part = (
                            (-DT / 24.0) * f0(c, z)
                            + (DT / 3.0 - HALF) * f1(c, z)
                            + (DT * 5.0 / 24.0) * f2(c, z)
                        )
                    node[m + 1, c, z] = node[m, c, z] + HALF * local[z] + old_part
            halo_wait("f", m, m)
            for c in range(3):
                for z in range(2):
                    share = s["fh_low"][m, c, z] + s["fh_high"][m, c, z]
                    total[c, z] = total[c, z] + weight * share
                    node[m + 1, c, z] = node[m + 1, c, z] + HALF * share
        else:
            for c in range(3):
                local = fine_local(m, c)
                for z in range(2):
                    total[c, z] = total[c, z] + weight * local[z]
            halo_wait("f", m, m)
            for c in range(3):
                for z in range(2):
                    share = s["fh_low"][m, c, z] + s["fh_high"][m, c, z]
                    total[c, z] = total[c, z] + weight * share

    rest = restricted(lambda c, z: total[c, z])
    keep(C1, [rest[c] + jnp.where(is_first, co[A0, c], -DT * co[G0, c]) for c in range(3)])
    coarse_send(kept(C1), 0)
    coarse_start(0)
    keep(G2, coarse_tendency(flux_g2, kept(A2), 1))
    keep(
        C2,
        [
            rest[c] - HALF * co[G2, c] + jnp.where(is_first, co[A0, c], -HALF * co[G0, c])
            for c in range(3)
        ],
    )
    coarse_send(kept(C2), 1)
    coarse_start(1)

    for c in range(3):
        a, b = speed[c, 0], speed[c, 1]
        s["fh_next"][3, c, 0], s["fh_next"][3, c, 1] = first_next(a, b)
        s["fh_prev"][3, c, 0], s["fh_prev"][3, c, 1] = first_prev(a, b)
    halo_start("f", 3, 3)

    coarse_wait(0)
    keep(CM1, coarse_modes(0))
    sx, lx = wide("c_sx"), wide("c_lx")

    @pl.when(is_first)
    def _():
        keep(BM1, kept(CM1))
        keep(B1, kept(C1))
        keep(S1, kept(C2))
        for c in range(3):
            s["hand_v"][c] = co[A0, c]

    @pl.when(jnp.logical_not(is_first))
    def _():
        coarse_wait(1)
        keep(CM2, coarse_modes(1))
        v_copy.wait_recv()
        u_copy.wait_recv()
        start = [s["hand_v"][c] for c in range(3)]
        f = coarse_flux([s["hand_u"][c] for c in range(3)], start, 2)
        coarse_send(f, 2)
        coarse_start(2)
        early = coarse_tendency(f, start, 2)
        keep(B1, [start[c] + DT * early[c] + co[C1, c] for c in range(3)])
        keep(S1, [start[c] + HALF * early[c] + co[C2, c] for c in range(3)])
        m_copy.wait_recv()
        coarse_wait(2)
        held = [s["hand_m"][c] for c in range(3)]
        early = tendency_modes(coarse_modes(2), held, sx, lx, t)
        keep(BM1, [held[c] + DT * early[c] + co[CM1, c] for c in range(3)])
        keep(SM1, [held[c] + HALF * early[c] + co[CM2, c] for c in range(3)])

    coarse_back(kept(BM1), 3)
    coarse_start(3)

    @pl.when(is_first)
    def _():
        coarse_wait(1)
        keep(SM1, coarse_modes(1))

    coarse_wait(3)
    middle = kept(B1)
    f = coarse_flux(coarse_velocity(3), middle, 3)
    coarse_send(f, 4)
    coarse_start(4)
    later = coarse_tendency(f, middle, 3)
    for c in range(3):
        s["send_v"][c] = co[S1, c] + HALF * later[c]

    @pl.when(has_next)
    def _():
        v_copy.start()

    coarse_wait(4)
    later = tendency_modes(coarse_modes(4), kept(BM1), sx, lx, t)
    for c in range(3):
        s["send_m"][c] = co[SM1, c] + HALF * later[c]
    coarse_back([s["send_m"][c] for c in range(3)], 5)
    coarse_start(5)

    @pl.when(has_next)
    def _():
        m_copy.start()

    for c in range(3):
        zero = prolong(s["hand_v"][c] - co[A0, c], t)
        two = prolong(s["send_v"][c] - co[A2, c], t)
        for z in range(2):
            nodes[0, 0, c, z] = node[0, c, z] + zero[z]
            nodes[0, 1, c, z] = node[1, c, z] + 0.5 * (zero[z] + two[z])
            nodes[0, 2, c, z] = node[2, c, z] + two[z]

    halo_wait("f", 3, 3)
    slope = s["slope"]
    for c in range(3):
        own = first_own(speed[c, 0], speed[c, 1])
        for z in range(2):
            slope[c, z] = own[z] + (s["fh_low"][3, c, z] + s["fh_high"][3, c, z])

    coarse_wait(5)
    out = coarse_velocity(5)
    for c in range(3):
        s["send_u"][c] = out[c]

    @pl.when(has_next)
    def _():
        u_copy.start()

    change = [out[c] - co[UA2, c] for c in range(3)]
    for c in range(3):
        s["ch_next"][4, c] = c_first_next(change[c])
        s["ch_prev"][4, c] = c_first_prev(change[c])
    halo_start("c", 4, 8)
    for c in range(3):
        put = prolong(change[c], t)
        for z in range(2):
            speed[c, z] = speed[c, z] + put[z]
    own = [c_first_own(change[c]) for c in range(3)]
    halo_wait("c", 4, 8)
    for c in range(3):
        put = prolong(own[c] + (s["ch_low"][4, c] + s["ch_high"][4, c]), t)
        for z in range(2):
            slope[c, z] = slope[c, z] + put[z]
    for z in range(2):
        gx = [first_fine(speed[c, z], 0) for c in range(3)]
        gy = [first_fine(speed[c, z], 1) for c in range(3)]
        gz = [slope[c, z] for c in range(3)]
        diagonal = gx[0] * gx[0] + gy[1] * gy[1] + gz[2] * gz[2]
        mixed = gx[1] * gy[0] + gx[2] * gz[0] + gy[2] * gz[1]
        q_out[0, z] = -0.5 * diagonal - mixed

    for i in range(6):
        left(s["fs"].at[i], FINE, s["f_ssem"].at[i])
    for i in (0, 1, 3, 4, 5):
        left(s["cs"].at[i], COARSE, s["c_ssem"].at[i])

    @pl.when(jnp.logical_not(is_first))
    def _():
        left(s["cs"].at[2], COARSE, s["c_ssem"].at[2])
        halo_left("c", 2, 6)

    for i in range(4):
        halo_left("f", i, i)
    for i in (0, 1, 3, 4):
        halo_left("c", i, 4 + i)

    @pl.when(has_next)
    def _():
        for copy in (start_copy, v_copy, u_copy, m_copy):
            copy.wait_send()


def body(initial_state, end_states, old_tendencies):
    vmem = pl.BlockSpec(memory_space=pltpu.VMEM)
    return pl.pallas_call(
        kernel,
        out_shape=(
            jax.ShapeDtypeStruct((1, 3, 3, 2, N, N), f32),
            jax.ShapeDtypeStruct((1, 2, N, N), f32),
        ),
        in_specs=[vmem] * (3 + len(NAMES)),
        out_specs=(vmem, vmem),
        scratch_shapes=list(SCRATCH.values()),
        compiler_params=pltpu.CompilerParams(
            collective_id=0, has_side_effects=True, vmem_limit_bytes=56 * 1024 * 1024
        ),
    )(initial_state, end_states, old_tendencies, *[jnp.asarray(TABLES[name]) for name in NAMES])


def solution(mesh):
    in_specs = (
        P(None, "space", None, None),
        P("tm", None, "space", None, None),
        P("tm", None, None, "space", None, None),
    )
    out_specs = (P("tm", None, None, "space", None, None), P("tm", "space", None, None))
    return jax.shard_map(body, mesh=mesh, in_specs=in_specs, out_specs=out_specs, check_vma=False)
```

```python
import math

import jax
import jax.numpy as jnp
import numpy as np
from jax import lax
from jax.experimental import pallas as pl
from jax.experimental.pallas import tpu as pltpu
from jax.sharding import PartitionSpec as P

DT = 0.4
HALF = 0.2
NU = 0.1
PARTS = 64
ROWS = 4
N = 128
M = 64
FINE = 12
COARSE = 3
f32 = jnp.float32
MESH = pl.DeviceIdType.MESH


def angle_tables(left, right, count):
    angles = (2.0 * math.pi / count) * (np.outer(left, right) % count)
    return np.cos(angles), np.sin(angles)


def restriction_table(count):
    cos_c, sin_c = angle_tables(np.arange(count // 2), np.arange(count // 4), count // 2)
    cos_f, sin_f = angle_tables(np.arange(count), np.arange(count // 4), count)
    weight = np.where(np.arange(count // 4) == 0, 1.0, 2.0)
    return ((cos_c * weight) @ cos_f.T + (sin_c * weight) @ sin_f.T) / count


def twice(block):
    zero = np.zeros_like(block)
    return np.block([[block, zero], [zero, block]])


def wave_symbols(ids, count, spacing):
    theta = 2.0 * math.pi * ids / count
    kappa = theta / spacing
    first = (8.0 * np.sin(theta) - np.sin(2.0 * theta)) / (6.0 * spacing)
    second = (-2.0 * np.cos(2.0 * theta) + 32.0 * np.cos(theta) - 30.0) / (12.0 * spacing**2)
    return kappa, first, second


def signed(ids, count):
    return np.where(ids < count // 2, ids, ids - count)


def build_tables():
    t = {}
    grid = np.arange(N)
    owner = np.concatenate([2 * np.arange(PARTS), 2 * np.arange(PARTS) + 1])
    cos_y, sin_y = angle_tables(grid, np.arange(M), N)
    t["f_y"] = np.hstack([cos_y, -sin_y, -sin_y, -cos_y])
    t["f_x"] = np.hstack(angle_tables(owner, grid, N))
    t["f_z"] = np.hstack(angle_tables(grid, owner, N))
    t["i_z"] = np.hstack(angle_tables(owner, grid, N))
    t["i_x"] = np.hstack(angle_tables(grid, owner, N))
    weight = np.where(np.arange(M) == 0, 1.0, 2.0) / float(N**3)
    wc, ws = (cos_y * weight).T, (sin_y * weight).T
    t["i_y"] = np.hstack([np.vstack([wc, -ws]), np.vstack([-ws, -wc])])
    half = np.arange(M // 2)
    cos_y, sin_y = angle_tables(np.arange(M), half, M)
    t["cf_y"] = np.hstack([twice(np.hstack([cos_y, -sin_y])), twice(np.hstack([-sin_y, -cos_y]))])
    t["c_x"] = np.hstack(angle_tables(np.arange(M), np.arange(M), M))
    weight = np.where(half == 0, 1.0, 2.0) / float(M * M * N)
    wc, ws = (cos_y * weight).T, (sin_y * weight).T
    t["ci_y"] = np.hstack([twice(np.vstack([wc, -ws])), twice(np.vstack([-ws, -wc]))])
    table = restriction_table(N)
    t["r_x"] = table
    t["r_y"] = twice(table.T)
    t["p_x"] = 4.0 * table.T
    t["p_y0"], t["p_y1"] = np.hsplit(twice(table), 2)
    kx, _, _ = wave_symbols(signed(grid, N), N, 1.0)
    ky = np.tile(kx[:M], 2)[None, :]
    ones = np.ones((1, N))
    t["f_kx"] = kx[:, None] * ones
    t["f_mx"] = (grid != M)[:, None] * ones
    t["f_ky"] = np.repeat(ky, 8, axis=0)
    t["f_kz"] = kx[:, None] * ones
    t["f_kk"] = ky**2 + kx[:, None] ** 2
    t["f_mz"] = t["f_mx"]
    ckx, sx, lx = wave_symbols(signed(np.arange(M), M), M, 2.0)
    t["c_kx"] = ckx[:, None] * ones
    t["c_mx"] = (np.arange(M) != M // 2)[:, None] * ones
    t["c_sx"] = sx[:, None] * ones
    t["c_lx"] = lx[:, None] * ones
    lane = lambda v: np.tile(v[: M // 2], 4)[None, :]
    cky, sy, ly = lane(ckx), lane(sx), lane(lx)
    zid = np.hstack([np.repeat(np.arange(M)[:, None], M, 1), np.repeat(np.arange(M)[:, None] + M, M, 1)])
    ckz, sz, lz = wave_symbols(signed(zid, N), N, 1.0)
    t["c_ky"] = np.repeat(cky, 8, axis=0)
    t["c_sy"] = np.repeat(sy, 8, axis=0)
    t["c_kz"] = ckz
    t["c_sz"] = sz
    t["c_kk"] = cky**2 + ckz**2
    t["c_mz"] = (zid != M) * 1.0
    t["c_ll"] = ly + lz
    turn = 2.0 * math.pi * np.arange(M)[:, None] / N
    first = (np.arange(N) < M)[None, :]
    t["tw_c"] = np.where(first, 1.0, np.cos(turn))
    t["tw_s"] = np.where(first, 0.0, np.sin(turn))
    made = {}
    for name, value in t.items():
        value = np.asarray(value, np.float32)
        if name in SPLIT:
            high = value.astype(jnp.bfloat16)
            made[name + "_h"] = high
            made[name + "_l"] = (value - high.astype(np.float32)).astype(jnp.bfloat16)
        else:
            made[name] = value
    return made


SPLIT = ("f_x", "f_y", "f_z", "i_x", "i_y", "i_z", "cf_y", "c_x", "ci_y")
TABLES = build_tables()


def pack(kind, width):
    places, blocks, top = {}, [], 0
    for name in sorted(TABLES):
        value = TABLES[name]
        if value.dtype == kind:
            block = np.zeros((value.shape[0], width), kind)
            block[:, : value.shape[1]] = value
            places[name] = (top, value.shape)
            blocks.append(block)
            top += value.shape[0]
    return places, np.concatenate(blocks)


PLACES_32, PACKED_32 = pack(np.float32, N)
PLACES_16, PACKED_16 = pack(jnp.bfloat16, 2 * N)
OPERANDS = 5


def exact(a, b):
    return jnp.dot(a, b, precision=lax.Precision.HIGHEST, preferred_element_type=f32)


def dot(a, b):
    return jnp.dot(a, b, preferred_element_type=f32)


def split(x):
    high = x.astype(jnp.bfloat16)
    return high, (x - high.astype(f32)).astype(jnp.bfloat16)


def by_table(x, t, name):
    high, low = split(x)
    table = t[name + "_h"][...]
    return dot(high, table) + (dot(low, table) + dot(high, t[name + "_l"][...]))


def table_by(t, name, x):
    high, low = split(x)
    table = t[name + "_h"][...]
    return dot(table, high) + (dot(table, low) + dot(t[name + "_l"][...], high))


def roll(x, shift, axis):
    return pltpu.roll(x, shift % x.shape[axis], axis)


def lanes(shape):
    return lax.broadcasted_iota(jnp.int32, shape, 1)


def stacked(a, b):
    return jnp.concatenate([a, b], axis=0)


def both_halves(wide):
    return stacked(wide[:, :N], wide[:, N:])


def turn_back(x):
    swapped = roll(x, M, 1)
    return jnp.where(lanes(x.shape) < M, swapped, -swapped)


def turn_back_c(x):
    is_real = (lanes(x.shape) % M) < M // 2
    return jnp.where(is_real, roll(x, -M // 2, 1), -roll(x, M // 2, 1))


def butterfly(x):
    return jnp.where(lanes(x.shape) < M, x, -x) + roll(x, M, 1)


def cross(a, b):
    return (
        a[1] * b[2] - a[2] * b[1],
        a[2] * b[0] - a[0] * b[2],
        a[0] * b[1] - a[1] * b[0],
    )


def first_fine(f, axis):
    return (roll(f, 2, axis) - roll(f, -2, axis) + 8.0 * (roll(f, -1, axis) - roll(f, 1, axis))) * (
        1.0 / 12.0
    )


def second_fine_xy(f):
    near = (roll(f, 1, 0) + roll(f, -1, 0)) + (roll(f, 1, 1) + roll(f, -1, 1))
    far = (roll(f, 2, 0) + roll(f, -2, 0)) + (roll(f, 2, 1) + roll(f, -2, 1))
    return (16.0 * near - far - 60.0 * f) * (1.0 / 12.0)


def roll_half(f, shift):
    place = lanes(f.shape) % M
    keep = place >= shift if shift > 0 else place < M + shift
    return jnp.where(keep, roll(f, shift, 1), roll(f, shift - M if shift > 0 else shift + M, 1))


def first_coarse(f, along_x):
    go = (lambda s: roll(f, s, 0)) if along_x else (lambda s: roll_half(f, s))
    return (go(2) - go(-2) + 8.0 * (go(-1) - go(1))) * (1.0 / 24.0)


def second_coarse_xy(f):
    near = (roll(f, 1, 0) + roll(f, -1, 0)) + (roll_half(f, 1) + roll_half(f, -1))
    far = (roll(f, 2, 0) + roll(f, -2, 0)) + (roll_half(f, 2) + roll_half(f, -2))
    return (16.0 * near - far - 60.0 * f) * (1.0 / 48.0)


def first_next(a, b):
    return (a - 8.0 * b) * (1.0 / 12.0), b * (1.0 / 12.0)


def first_prev(a, b):
    return a * (-1.0 / 12.0), (8.0 * a - b) * (1.0 / 12.0)


def first_own(a, b):
    return b * (8.0 / 12.0), a * (-8.0 / 12.0)


def second_next(a, b):
    return (16.0 * b - a) * (1.0 / 12.0), b * (-1.0 / 12.0)


def second_prev(a, b):
    return a * (-1.0 / 12.0), (16.0 * a - b) * (1.0 / 12.0)


def second_own(a, b):
    return (16.0 * b - 30.0 * a) * (1.0 / 12.0), (16.0 * a - 30.0 * b) * (1.0 / 12.0)


def lane_pair(f, low, high):
    is_low = lanes(f.shape) < M
    own = jnp.where(is_low, low[0], high[0]).astype(f32)
    other = jnp.where(is_low, low[1], high[1]).astype(f32)
    return f * own + roll(f, M, 1) * other


T12 = 1.0 / 12.0


def c_first_next(f):
    return lane_pair(f, (T12, -8 * T12), (T12, 0.0))


def c_first_prev(f):
    return lane_pair(f, (-T12, 0.0), (-T12, 8 * T12))


def c_first_own(f):
    return lane_pair(f, (0.0, 8 * T12), (0.0, -8 * T12))


def c_second_next(f):
    return lane_pair(f, (-T12, 16 * T12), (-T12, 0.0))


def c_second_prev(f):
    return lane_pair(f, (-T12, 0.0), (-T12, 16 * T12))


def c_second_own(f):
    return lane_pair(f, (-30 * T12, 16 * T12), (-30 * T12, 16 * T12))


def forward_fine(plane, t):
    return table_by(t, "f_x", both_halves(by_table(plane, t, "f_y")))


def inverse_fine(modes, t):
    return table_by(t, "i_x", both_halves(by_table(modes, t, "i_y")))


def forward_coarse(pair, t):
    return table_by(t, "c_x", both_halves(by_table(pair, t, "cf_y")))


def inverse_coarse(modes, t):
    return table_by(t, "c_x", both_halves(by_table(modes, t, "ci_y")))


def inverse_square(kk, kx, mask):
    squared = kk + kx * kx
    live = squared > 0.0
    return jnp.where(live, mask / jnp.where(live, squared, 1.0), 0.0)


def solve_fine(planes, kx, inverse, t):
    hat = [table_by(t, "f_z", stacked(p, turn_back(p))) for p in planes]
    kz = t["f_kz"][...]
    ky = jnp.broadcast_to(t["f_ky"][0:1, :], kz.shape)
    out = []
    for r in cross((kx, ky, kz), hat):
        r = r * inverse
        out.append(table_by(t, "i_z", stacked(-turn_back(r), -r)))
    return out


def z_coarse(x, t):
    d = table_by(t, "c_x", stacked(x, turn_back_c(x)))
    return butterfly(t["tw_c"][...] * d + t["tw_s"][...] * turn_back_c(d))


def z_coarse_back(a, t):
    b = butterfly(a)
    b = t["tw_c"][...] * b - t["tw_s"][...] * turn_back_c(b)
    return table_by(t, "c_x", stacked(b, -turn_back_c(b)))


def velocity_modes(hat, kx, inverse, t):
    kz = t["c_kz"][...]
    ky = jnp.broadcast_to(t["c_ky"][0:1, :], kz.shape)
    return [-turn_back_c(r * inverse) for r in cross((kx, ky, kz), hat)]


def tendency_modes(flux, w, sx, lx, t):
    sz = t["c_sz"][...]
    sy = jnp.broadcast_to(t["c_sy"][0:1, :], sz.shape)
    spread = NU * (t["c_ll"][...] + lx)
    return [-turn_back_c(r) + spread * w[i] for i, r in enumerate(cross((sx, sy, sz), flux))]


def restrict(a, b, t):
    return exact(t["r_x"][...], exact(jnp.concatenate([a, b], axis=1), t["r_y"][...]))


def prolong(pair, t):
    wide = exact(exact(t["p_x"][...], pair), jnp.concatenate([t["p_y0"][...], t["p_y1"][...]], axis=1))
    return wide[:, :N], wide[:, N:]


SCRATCH = dict(
    node=pltpu.VMEM((3, 3, 2, N, N), f32),
    speed=pltpu.VMEM((3, 2, N, N), f32),
    flux=pltpu.VMEM((3, 2, N, N), f32),
    total=pltpu.VMEM((3, 2, N, N), f32),
    slope=pltpu.VMEM((3, 2, N, N), f32),
    fs=pltpu.VMEM((6, PARTS * FINE, N), f32),
    fr=pltpu.VMEM((6, PARTS * FINE, N), f32),
    cs=pltpu.VMEM((6, PARTS * COARSE, N), f32),
    cr=pltpu.VMEM((7, PARTS * COARSE, N), f32),
    fh_next=pltpu.VMEM((4, 3, 2, N, N), f32),
    fh_prev=pltpu.VMEM((4, 3, 2, N, N), f32),
    fh_low=pltpu.VMEM((4, 3, 2, N, N), f32),
    fh_high=pltpu.VMEM((4, 3, 2, N, N), f32),
    ch_next=pltpu.VMEM((5, 3, M, N), f32),
    ch_prev=pltpu.VMEM((5, 3, M, N), f32),
    ch_low=pltpu.VMEM((5, 3, M, N), f32),
    ch_high=pltpu.VMEM((5, 3, M, N), f32),
    hand_v=pltpu.VMEM((3, M, N), f32),
    hand_m=pltpu.VMEM((3, M, N), f32),
    send_v=pltpu.VMEM((3, M, N), f32),
    send_m=pltpu.VMEM((3, M, N), f32),
    co=pltpu.VMEM((14, 3, M, N), f32),
    inv_f=pltpu.VMEM((2, N, N), f32),
    inv_c=pltpu.VMEM((M, N), f32),
    f_ssem=pltpu.SemaphoreType.DMA((6,)),
    f_rsem=pltpu.SemaphoreType.DMA((6,)),
    c_ssem=pltpu.SemaphoreType.DMA((7,)),
    c_rsem=pltpu.SemaphoreType.DMA((7,)),
    h_ssem=pltpu.SemaphoreType.DMA((9, 2)),
    h_rsem=pltpu.SemaphoreType.DMA((9, 2)),
    y_ssem=pltpu.SemaphoreType.DMA((3,)),
    y_rsem=pltpu.SemaphoreType.DMA((3,)),
    in_sem=pltpu.SemaphoreType.DMA((OPERANDS,)),
)
A0, A2, UA0, UA2, G0, G2, C1, C2, CM1, CM2, B1, S1, BM1, SM1 = range(14)


def kernel(*refs):
    nodes, q_out = refs[OPERANDS : OPERANDS + 2]
    staged = refs[OPERANDS + 2 : 2 * OPERANDS + 2]
    init, end, old = staged[:3]
    s = dict(zip(SCRATCH, refs[2 * OPERANDS + 2 :]))
    t = {}
    for places, packed in ((PLACES_32, staged[3]), (PLACES_16, staged[4])):
        for name, (top, shape) in places.items():
            t[name] = packed.at[pl.ds(top, shape[0]), pl.ds(0, shape[1])]
    loads = [
        pltpu.make_async_copy(source, target, s["in_sem"].at[i])
        for i, (source, target) in enumerate(zip(refs[:OPERANDS], staged))
    ]
    co = s["co"]
    row = lax.axis_index("tm")
    me = lax.axis_index("space")
    ahead = lax.rem(me + 1, PARTS)
    behind = lax.rem(me + PARTS - 1, PARTS)
    up = lax.rem(row + 1, ROWS)
    down = lax.rem(row + ROWS - 1, ROWS)

    barrier = pltpu.get_barrier_semaphore()

    def greet(k, carry):
        pl.semaphore_signal(barrier, inc=1, device_id=(row, lax.rem(me + k, PARTS)), device_id_type=MESH)
        return carry

    def greet_rows(k, carry):
        for other in (up, down):
            pl.semaphore_signal(barrier, inc=1, device_id=(other, lax.rem(me + k, PARTS)), device_id_type=MESH)
        return carry

    for i in (0, 1, 4, 3, 2):
        loads[i].start()
    lax.fori_loop(0, PARTS, greet_rows, 0)
    lax.fori_loop(1, PARTS, greet, 0)
    for i in (0, 1, 3, 4):
        loads[i].wait()


    place_x, place_z, core = me // 16, lax.rem(me // 2, 8), lax.rem(me, 2)

    def transpose_start(send, recv, depth, ssem, rsem, to_row=None):
        mine = pl.ds(me * depth, depth)

        def post(z, x, c):
            to = (lax.rem(place_x + x, 4) * 8 + lax.rem(place_z + z, 8)) * 2 + lax.rem(core + c, 2)
            pltpu.make_async_remote_copy(
                src_ref=send.at[pl.ds(to * depth, depth)],
                dst_ref=recv.at[mine],
                send_sem=ssem,
                recv_sem=rsem,
                device_id=(row if to_row is None else to_row, to),
                device_id_type=MESH,
            ).start()

        def step(j, carry):
            z = 4 + ((j + 1) // 2) * (1 - 2 * lax.rem(j, 2))
            for x in (2, 1, 3, 0):
                for c in (1, 0):
                    post(z, x, c)
            return carry

        lax.fori_loop(0, 7, step, 0)
        for x in (2, 1, 3, 0):
            for c in (1, 0):
                if x or c or to_row is not None:
                    post(0, x, c)
        if to_row is None:
            pltpu.make_async_copy(send.at[mine], recv.at[mine], rsem).start()

    def arrived(ref, sem):
        pltpu.make_async_copy(ref, ref, sem).wait()

    def left(ref, depth, sem, parts=PARTS - 1):
        part = ref.at[pl.ds(0, parts * depth)]
        pltpu.make_async_copy(part, part, sem).wait()

    def fine_start(i, to_row=None):
        transpose_start(s["fs"].at[i], s["fr"].at[i], FINE, s["f_ssem"].at[i], s["f_rsem"].at[i], to_row)

    def coarse_start(i):
        transpose_start(s["cs"].at[i], s["cr"].at[i], COARSE, s["c_ssem"].at[i], s["c_rsem"].at[i])

    def fine_wait(i):
        arrived(s["fr"].at[i], s["f_rsem"].at[i])

    def coarse_wait(i):
        arrived(s["cr"].at[i], s["c_rsem"].at[i])

    def halo_copies(kind, i, sem):
        return (
            pltpu.make_async_remote_copy(
                src_ref=s[kind + "h_next"].at[i],
                dst_ref=s[kind + "h_low"].at[i],
                send_sem=s["h_ssem"].at[sem, 0],
                recv_sem=s["h_rsem"].at[sem, 0],
                device_id=(row, ahead),
                device_id_type=MESH,
            ),
            pltpu.make_async_remote_copy(
                src_ref=s[kind + "h_prev"].at[i],
                dst_ref=s[kind + "h_high"].at[i],
                send_sem=s["h_ssem"].at[sem, 1],
                recv_sem=s["h_rsem"].at[sem, 1],
                device_id=(row, behind),
                device_id_type=MESH,
            ),
        )

    def halo_start(kind, i, sem):
        for copy in halo_copies(kind, i, sem):
            copy.start()

    def halo_wait(kind, i, sem):
        for copy in halo_copies(kind, i, sem):
            copy.wait_recv()

    def halo_left(kind, i, sem):
        for copy in halo_copies(kind, i, sem):
            copy.wait_send()

    def hand_copy(src, dst, sem):
        return pltpu.make_async_remote_copy(
            src_ref=src,
            dst_ref=dst,
            send_sem=s["y_ssem"].at[sem],
            recv_sem=s["y_rsem"].at[sem],
            device_id=(up, me),
            device_id_type=MESH,
        )

    start_copy = hand_copy(end.at[0], s["node"].at[0], 0)
    v_copy = hand_copy(s["send_v"], s["hand_v"], 1)
    m_copy = hand_copy(s["send_m"], s["hand_m"], 2)
    is_first = row == 0
    has_next = row < ROWS - 1


    def fine_send(get, i):
        for c in range(3):
            for z in range(2):
                out = forward_fine(get(c, z), t)
                for low in range(2):
                    s["fs"][i, pl.ds((c * 2 + z) * 2 + low, PARTS, stride=FINE), :] = out[low * M : low * M + M]

    def fine_modes(i):
        for low in range(2):
            planes = [
                stacked(
                    s["fr"][i, pl.ds((c * 2) * 2 + low, PARTS, stride=FINE), :],
                    s["fr"][i, pl.ds((c * 2 + 1) * 2 + low, PARTS, stride=FINE), :],
                )
                for c in range(3)
            ]
            at = pl.ds(me * 2 + low, 1)
            kx = jnp.broadcast_to(t["f_kx"][at, :], (N, N))
            for c, out in enumerate(solve_fine(planes, kx, s["inv_f"][low], t)):
                for z in range(2):
                    s["fs"][i + 1, pl.ds((c * 2 + z) * 2 + low, PARTS, stride=FINE), :] = out[z * M : z * M + M]

    def fine_velocity(i):
        for c in range(3):
            for z in range(2):
                at = (c * 2 + z) * 2
                modes = stacked(
                    s["fr"][i, pl.ds(at, PARTS, stride=FINE), :],
                    s["fr"][i, pl.ds(at + 1, PARTS, stride=FINE), :],
                )
                s["speed"][c, z] = inverse_fine(modes, t)

    node, speed, flux, total = s["node"], s["speed"], s["flux"], s["total"]

    def fine_flux(m):
        for z in range(2):
            parts = cross([speed[c, z] for c in range(3)], [node[m, c, z] for c in range(3)])
            for c in range(3):
                flux[c, z] = parts[c]
        for c in range(3):
            w0, w1 = node[m, c, 0], node[m, c, 1]
            ahead0, ahead1 = second_next(w0, w1)
            back0, back1 = second_prev(w0, w1)
            ahead0, ahead1, back0, back1 = NU * ahead0, NU * ahead1, NU * back0, NU * back1
            if c < 2:
                sign = -1.0 if c == 0 else 1.0
                g0, g1 = sign * flux[1 - c, 0], sign * flux[1 - c, 1]
                d0, d1 = first_next(g0, g1)
                e0, e1 = first_prev(g0, g1)
                ahead0, ahead1, back0, back1 = ahead0 + d0, ahead1 + d1, back0 + e0, back1 + e1
            s["fh_next"][m, c, 0] = ahead0
            s["fh_next"][m, c, 1] = ahead1
            s["fh_prev"][m, c, 0] = back0
            s["fh_prev"][m, c, 1] = back1
        halo_start("f", m, m)

    def fine_local(m, c):
        w0, w1 = node[m, c, 0], node[m, c, 1]
        own = [NU * v for v in second_own(w0, w1)]
        if c < 2:
            sign = -1.0 if c == 0 else 1.0
            extra = first_own(sign * flux[1 - c, 0], sign * flux[1 - c, 1])
            own = [own[z] + extra[z] for z in range(2)]
        out = []
        for z in range(2):
            if c == 0:
                curl = first_fine(flux[2, z], 1)
            elif c == 1:
                curl = -first_fine(flux[2, z], 0)
            else:
                curl = first_fine(flux[1, z], 0) - first_fine(flux[0, z], 1)
            out.append(curl + NU * second_fine_xy((w0, w1)[z]) + own[z])
        return out


    def coarse_send(values, i):
        for c in range(3):
            s["cs"][i, pl.ds(c, PARTS, stride=COARSE), :] = forward_coarse(values[c], t)

    def coarse_recv(i):
        return [s["cr"][i, pl.ds(c, PARTS, stride=COARSE), :] for c in range(3)]

    def coarse_modes(i):
        return [z_coarse(x, t) for x in coarse_recv(i)]

    def coarse_velocity(i):
        return [inverse_coarse(x, t) for x in coarse_recv(i)]

    mine = pl.ds(me, 1)
    wide = lambda name: jnp.broadcast_to(t[name][mine, :], (M, N))

    def coarse_back(hat, i):
        modes = velocity_modes(hat, wide("c_kx"), s["inv_c"][...], t)
        for c in range(3):
            s["cs"][i, pl.ds(c, PARTS, stride=COARSE), :] = z_coarse_back(modes[c], t)

    def coarse_halo(f, w, i):
        g = (-f[1], f[0], None)
        for c in range(3):
            nxt, prv = NU * c_second_next(w[c]), NU * c_second_prev(w[c])
            if g[c] is not None:
                nxt, prv = nxt + c_first_next(g[c]), prv + c_first_prev(g[c])
            s["ch_next"][i, c] = nxt
            s["ch_prev"][i, c] = prv
        halo_start("c", i, 4 + i)

    def coarse_tendency(f, w, i):
        own = [NU * (second_coarse_xy(w[c]) + c_second_own(w[c])) for c in range(3)]
        parts = [
            first_coarse(f[2], False) - c_first_own(f[1]),
            c_first_own(f[0]) - first_coarse(f[2], True),
            first_coarse(f[1], True) - first_coarse(f[0], False),
        ]
        halo_wait("c", i, 4 + i)
        return [own[c] + parts[c] + (s["ch_low"][i, c] + s["ch_high"][i, c]) for c in range(3)]

    def keep(i, values):
        for c in range(3):
            co[i, c] = values[c]

    def kept(i):
        return [co[i, c] for c in range(3)]

    def restricted(get):
        return [restrict(get(c, 0), get(c, 1), t) for c in range(3)]

    for low in range(2):
        at = pl.ds(me * 2 + low, 1)
        kx = jnp.broadcast_to(t["f_kx"][at, :], (N, N))
        mask = t["f_mz"][...] * jnp.broadcast_to(t["f_mx"][at, :], (N, N))
        s["inv_f"][low] = inverse_square(t["f_kk"][...], kx, mask)
    s["inv_c"][...] = inverse_square(t["c_kk"][...], wide("c_kx"), t["c_mz"][...] * wide("c_mx"))

    f0 = lambda c, z: old[0, 0, c, z]
    f1 = lambda c, z: old[0, 1, c, z]
    f2 = lambda c, z: old[0, 2, c, z]

    for m in range(3):
        if m == 0:
            fine_send(lambda c, z: jnp.where(has_next, end[0, c, z], init[c, z]), 0)
            pl.semaphore_wait(barrier, 3 * PARTS - 1)
            fine_start(0, up)
        else:
            fine_send(lambda c, z: node[m, c, z], 2 * m)
            fine_start(2 * m)
        if m == 1:
            keep(UA0, restricted(lambda c, z: speed[c, z]))
            flux_g0 = cross(kept(UA0), kept(A0))
            coarse_halo(flux_g0, kept(A0), 0)
            keep(G0, coarse_tendency(flux_g0, kept(A0), 0))
        if m == 2:
            keep(A2, restricted(lambda c, z: node[2, c, z]))
        fine_wait(2 * m)
        fine_modes(2 * m)
        fine_start(2 * m + 1)
        if m == 0:

            @pl.when(has_next)
            def _():
                start_copy.start()

            @pl.when(is_first)
            def _():
                for c in range(3):
                    for z in range(2):
                        node[0, c, z] = init[c, z]

            @pl.when(jnp.logical_not(is_first))
            def _():
                start_copy.wait_recv()

            keep(A0, restricted(lambda c, z: node[0, c, z]))
            loads[2].wait()
        fine_wait(2 * m + 1)
        fine_velocity(2 * m + 1)
        fine_flux(m)
        if m == 2:
            keep(UA2, restricted(lambda c, z: speed[c, z]))
            flux_g2 = cross(kept(UA2), kept(A2))
            coarse_halo(flux_g2, kept(A2), 1)
        weight = (DT / 6.0, DT * 2.0 / 3.0, DT / 6.0)[m]
        if m < 2:
            for c in range(3):
                local = fine_local(m, c)
                for z in range(2):
                    total[c, z] = weight * local[z] if m == 0 else total[c, z] + weight * local[z]
                    if m == 0:
                        old_part = (
                            (DT * 5.0 / 24.0 - HALF) * f0(c, z)
                            + (DT / 3.0) * f1(c, z)
                            - (DT / 24.0) * f2(c, z)
                        )
                    else:
                        old_part = (
                            (-DT / 24.0) * f0(c, z)
                            + (DT / 3.0 - HALF) * f1(c, z)
                            + (DT * 5.0 / 24.0) * f2(c, z)
                        )
                    node[m + 1, c, z] = node[m, c, z] + HALF * local[z] + old_part
            halo_wait("f", m, m)
            for c in range(3):
                for z in range(2):
                    share = s["fh_low"][m, c, z] + s["fh_high"][m, c, z]
                    total[c, z] = total[c, z] + weight * share
                    node[m + 1, c, z] = node[m + 1, c, z] + HALF * share
        else:
            for c in range(3):
                local = fine_local(m, c)
                for z in range(2):
                    total[c, z] = total[c, z] + weight * local[z]
            halo_wait("f", m, m)
            for c in range(3):
                for z in range(2):
                    share = s["fh_low"][m, c, z] + s["fh_high"][m, c, z]
                    total[c, z] = total[c, z] + weight * share

    rest = restricted(lambda c, z: total[c, z])
    keep(C1, [rest[c] + jnp.where(is_first, co[A0, c], -DT * co[G0, c]) for c in range(3)])
    coarse_send(kept(C1), 0)
    coarse_start(0)
    keep(G2, coarse_tendency(flux_g2, kept(A2), 1))
    keep(
        C2,
        [
            rest[c] - HALF * co[G2, c] + jnp.where(is_first, co[A0, c], -HALF * co[G0, c])
            for c in range(3)
        ],
    )
    coarse_send(kept(C2), 1)
    coarse_start(1)

    for c in range(3):
        a, b = speed[c, 0], speed[c, 1]
        s["fh_next"][3, c, 0], s["fh_next"][3, c, 1] = first_next(a, b)
        s["fh_prev"][3, c, 0], s["fh_prev"][3, c, 1] = first_prev(a, b)
    halo_start("f", 3, 3)

    coarse_wait(0)
    keep(CM1, coarse_modes(0))
    sx, lx = wide("c_sx"), wide("c_lx")

    @pl.when(is_first)
    def _():
        keep(BM1, kept(CM1))
        keep(B1, kept(C1))
        keep(S1, kept(C2))
        for c in range(3):
            s["hand_v"][c] = co[A0, c]

    @pl.when(jnp.logical_not(is_first))
    def _():
        coarse_wait(1)
        keep(CM2, coarse_modes(1))
        v_copy.wait_recv()
        start = [s["hand_v"][c] for c in range(3)]
        coarse_wait(6)
        f = cross(coarse_velocity(6), start)
        coarse_send(f, 2)
        coarse_start(2)
        coarse_halo(f, start, 2)
        early = coarse_tendency(f, start, 2)
        keep(B1, [start[c] + DT * early[c] + co[C1, c] for c in range(3)])
        keep(S1, [start[c] + HALF * early[c] + co[C2, c] for c in range(3)])
        m_copy.wait_recv()
        coarse_wait(2)
        held = [s["hand_m"][c] for c in range(3)]
        early = tendency_modes(coarse_modes(2), held, sx, lx, t)
        keep(BM1, [held[c] + DT * early[c] + co[CM1, c] for c in range(3)])
        keep(SM1, [held[c] + HALF * early[c] + co[CM2, c] for c in range(3)])

    coarse_back(kept(BM1), 3)
    coarse_start(3)

    @pl.when(is_first)
    def _():
        coarse_wait(1)
        keep(SM1, coarse_modes(1))

    coarse_wait(3)
    middle = kept(B1)
    f = cross(coarse_velocity(3), middle)
    coarse_send(f, 4)
    coarse_start(4)
    coarse_halo(f, middle, 3)
    later = coarse_tendency(f, middle, 3)
    for c in range(3):
        s["send_v"][c] = co[S1, c] + HALF * later[c]

    @pl.when(has_next)
    def _():
        v_copy.start()

    coarse_wait(4)
    later = tendency_modes(coarse_modes(4), kept(BM1), sx, lx, t)
    for c in range(3):
        s["send_m"][c] = co[SM1, c] + HALF * later[c]
    coarse_back([s["send_m"][c] for c in range(3)], 5)

    @pl.when(has_next)
    def _():
        transpose_start(s["cs"].at[5], s["cr"].at[6], COARSE, s["c_ssem"].at[6], s["c_rsem"].at[6], up)
        m_copy.start()

    coarse_start(5)

    for c in range(3):
        zero = prolong(s["hand_v"][c] - co[A0, c], t)
        two = prolong(s["send_v"][c] - co[A2, c], t)
        for z in range(2):
            nodes[0, 0, c, z] = node[0, c, z] + zero[z]
            nodes[0, 1, c, z] = node[1, c, z] + 0.5 * (zero[z] + two[z])
            nodes[0, 2, c, z] = node[2, c, z] + two[z]

    halo_wait("f", 3, 3)
    slope = s["slope"]
    for c in range(3):
        own = first_own(speed[c, 0], speed[c, 1])
        for z in range(2):
            slope[c, z] = own[z] + (s["fh_low"][3, c, z] + s["fh_high"][3, c, z])

    coarse_wait(5)
    out = coarse_velocity(5)

    change = [out[c] - co[UA2, c] for c in range(3)]
    for c in range(3):
        s["ch_next"][4, c] = c_first_next(change[c])
        s["ch_prev"][4, c] = c_first_prev(change[c])
    halo_start("c", 4, 8)
    for c in range(3):
        put = prolong(change[c], t)
        for z in range(2):
            speed[c, z] = speed[c, z] + put[z]
    own = [c_first_own(change[c]) for c in range(3)]
    halo_wait("c", 4, 8)
    for c in range(3):
        put = prolong(own[c] + (s["ch_low"][4, c] + s["ch_high"][4, c]), t)
        for z in range(2):
            slope[c, z] = slope[c, z] + put[z]
    for z in range(2):
        gx = [first_fine(speed[c, z], 0) for c in range(3)]
        gy = [first_fine(speed[c, z], 1) for c in range(3)]
        gz = [slope[c, z] for c in range(3)]
        diagonal = gx[0] * gx[0] + gy[1] * gy[1] + gz[2] * gz[2]
        mixed = gx[1] * gy[0] + gx[2] * gz[0] + gy[2] * gz[1]
        q_out[0, z] = -0.5 * diagonal - mixed

    for i in range(6):
        left(s["fs"].at[i], FINE, s["f_ssem"].at[i], PARTS if i == 0 else PARTS - 1)
    for i in (0, 1, 3, 4, 5):
        left(s["cs"].at[i], COARSE, s["c_ssem"].at[i])

    @pl.when(jnp.logical_not(is_first))
    def _():
        left(s["cs"].at[2], COARSE, s["c_ssem"].at[2])
        halo_left("c", 2, 6)

    for i in range(4):
        halo_left("f", i, i)
    for i in (0, 1, 3, 4):
        halo_left("c", i, 4 + i)

    @pl.when(has_next)
    def _():
        left(s["cs"].at[5], COARSE, s["c_ssem"].at[6], PARTS)
        for copy in (start_copy, v_copy, m_copy):
            copy.wait_send()


def body(initial_state, end_states, old_tendencies):
    vmem = pl.BlockSpec(memory_space=pltpu.VMEM)
    operands = [initial_state, end_states, old_tendencies, jnp.asarray(PACKED_32), jnp.asarray(PACKED_16)]
    return pl.pallas_call(
        kernel,
        out_shape=(
            jax.ShapeDtypeStruct((1, 3, 3, 2, N, N), f32),
            jax.ShapeDtypeStruct((1, 2, N, N), f32),
        ),
        in_specs=[pl.BlockSpec(memory_space=pl.ANY)] * len(operands),
        out_specs=(vmem, vmem),
        scratch_shapes=[pltpu.VMEM(x.shape, x.dtype) for x in operands] + list(SCRATCH.values()),
        compiler_params=pltpu.CompilerParams(
            collective_id=0, has_side_effects=True, vmem_limit_bytes=56 * 1024 * 1024
        ),
    )(*operands)


def solution(mesh):
    in_specs = (
        P(None, "space", None, None),
        P("tm", None, "space", None, None),
        P("tm", None, None, "space", None, None),
    )
    out_specs = (P("tm", None, None, "space", None, None), P("tm", "space", None, None))
    return jax.shard_map(body, mesh=mesh, in_specs=in_specs, out_specs=out_specs, check_vma=False)
```

```python
import math

import jax
import jax.numpy as jnp
import numpy as np
from jax import lax
from jax.experimental import pallas as pl
from jax.experimental.pallas import tpu as pltpu
from jax.sharding import PartitionSpec as P

DT = 0.4
HALF = 0.2
NU = 0.1
PARTS = 64
ROWS = 4
N = 128
M = 64
FINE = 6
THIRD = 4
COARSE = 3
f32 = jnp.float32
MESH = pl.DeviceIdType.MESH


def angle_tables(left, right, count):
    angles = (2.0 * math.pi / count) * (np.outer(left, right) % count)
    return np.cos(angles), np.sin(angles)


def restriction_table(count):
    cos_c, sin_c = angle_tables(np.arange(count // 2), np.arange(count // 4), count // 2)
    cos_f, sin_f = angle_tables(np.arange(count), np.arange(count // 4), count)
    weight = np.where(np.arange(count // 4) == 0, 1.0, 2.0)
    return ((cos_c * weight) @ cos_f.T + (sin_c * weight) @ sin_f.T) / count


def twice(block):
    zero = np.zeros_like(block)
    return np.block([[block, zero], [zero, block]])


def wave_symbols(ids, count, spacing):
    theta = 2.0 * math.pi * ids / count
    kappa = theta / spacing
    first = (8.0 * np.sin(theta) - np.sin(2.0 * theta)) / (6.0 * spacing)
    second = (-2.0 * np.cos(2.0 * theta) + 32.0 * np.cos(theta) - 30.0) / (12.0 * spacing**2)
    return kappa, first, second


def signed(ids, count):
    return np.where(ids < count // 2, ids, ids - count)


def build_tables():
    t = {}
    grid = np.arange(N)
    owner = np.concatenate([2 * np.arange(PARTS), 2 * np.arange(PARTS) + 1])
    cos_y, sin_y = angle_tables(grid, np.arange(M), N)
    t["f_y"] = np.hstack([cos_y, -sin_y, -sin_y, -cos_y])
    t["f_x"] = np.hstack(angle_tables(owner, grid, N))
    t["f_z"] = np.hstack(angle_tables(grid, owner, N))
    t["i_z"] = np.hstack(angle_tables(owner, grid, N))
    t["i_x"] = np.hstack(angle_tables(grid, owner, N))
    weight = np.where(np.arange(M) == 0, 1.0, 2.0) / float(N**3)
    wc, ws = (cos_y * weight).T, (sin_y * weight).T
    t["i_y"] = np.hstack([np.vstack([wc, -ws]), np.vstack([-ws, -wc])])
    half = np.arange(M // 2)
    cos_y, sin_y = angle_tables(np.arange(M), half, M)
    t["cf_y"] = np.hstack([twice(np.hstack([cos_y, -sin_y])), twice(np.hstack([-sin_y, -cos_y]))])
    t["c_x"] = np.hstack(angle_tables(np.arange(M), np.arange(M), M))
    weight = np.where(half == 0, 1.0, 2.0) / float(M * M * N)
    wc, ws = (cos_y * weight).T, (sin_y * weight).T
    t["ci_y"] = np.hstack([twice(np.vstack([wc, -ws])), twice(np.vstack([-ws, -wc]))])
    table = restriction_table(N)
    t["r_x"] = table
    t["r_y"] = twice(table.T)
    t["p_x"] = 4.0 * table.T
    t["p_y0"], t["p_y1"] = np.hsplit(twice(table), 2)
    kx, _, _ = wave_symbols(signed(grid, N), N, 1.0)
    ky = np.tile(kx[:M], 2)[None, :]
    ones = np.ones((1, N))
    t["f_kx"] = kx[:, None] * ones
    t["f_mx"] = (grid != M)[:, None] * ones
    t["f_ky"] = np.repeat(ky, 8, axis=0)
    t["f_kz"] = kx[:, None] * ones
    t["f_kk"] = ky**2 + kx[:, None] ** 2
    t["f_mz"] = t["f_mx"]
    ckx, sx, lx = wave_symbols(signed(np.arange(M), M), M, 2.0)
    t["c_kx"] = ckx[:, None] * ones
    t["c_mx"] = (np.arange(M) != M // 2)[:, None] * ones
    t["c_sx"] = sx[:, None] * ones
    t["c_lx"] = lx[:, None] * ones
    lane = lambda v: np.tile(v[: M // 2], 4)[None, :]
    cky, sy, ly = lane(ckx), lane(sx), lane(lx)
    zid = np.hstack([np.repeat(np.arange(M)[:, None], M, 1), np.repeat(np.arange(M)[:, None] + M, M, 1)])
    ckz, sz, lz = wave_symbols(signed(zid, N), N, 1.0)
    t["c_ky"] = np.repeat(cky, 8, axis=0)
    t["c_sy"] = np.repeat(sy, 8, axis=0)
    t["c_kz"] = ckz
    t["c_sz"] = sz
    t["c_kk"] = cky**2 + ckz**2
    t["c_mz"] = (zid != M) * 1.0
    t["c_ll"] = ly + lz
    turn = 2.0 * math.pi * np.arange(M)[:, None] / N
    first = (np.arange(N) < M)[None, :]
    t["tw_c"] = np.where(first, 1.0, np.cos(turn))
    t["tw_s"] = np.where(first, 0.0, np.sin(turn))
    made = {}
    for name, value in t.items():
        value = np.asarray(value, np.float32)
        if name in SPLIT:
            high = value.astype(jnp.bfloat16)
            made[name + "_h"] = high
            made[name + "_l"] = (value - high.astype(np.float32)).astype(jnp.bfloat16)
        else:
            made[name] = value
    return made


SPLIT = ("f_x", "f_y", "f_z", "i_x", "i_y", "i_z", "cf_y", "c_x", "ci_y")
TABLES = build_tables()


def pack(kind, width):
    places, blocks, top = {}, [], 0
    for name in sorted(TABLES):
        value = TABLES[name]
        if value.dtype == kind:
            block = np.zeros((value.shape[0], width), kind)
            block[:, : value.shape[1]] = value
            places[name] = (top, value.shape)
            blocks.append(block)
            top += value.shape[0]
    return places, np.concatenate(blocks)


PLACES_32, PACKED_32 = pack(np.float32, N)
PLACES_16, PACKED_16 = pack(jnp.bfloat16, 2 * N)
OPERANDS = 5


def exact(a, b):
    return jnp.dot(a, b, precision=lax.Precision.HIGHEST, preferred_element_type=f32)


def dot(a, b):
    return jnp.dot(a, b, preferred_element_type=f32)


def split(x):
    high = x.astype(jnp.bfloat16)
    return high, (x - high.astype(f32)).astype(jnp.bfloat16)


def by_table(x, t, name):
    high, low = split(x)
    table = t[name + "_h"][...]
    return dot(high, table) + (dot(low, table) + dot(high, t[name + "_l"][...]))


def table_by(t, name, x, rows=slice(None)):
    high, low = split(x)
    table = t[name + "_h"][rows, :]
    return dot(table, high) + (dot(table, low) + dot(t[name + "_l"][rows, :], high))


def roll(x, shift, axis):
    return pltpu.roll(x, shift % x.shape[axis], axis)


def lanes(shape):
    return lax.broadcasted_iota(jnp.int32, shape, 1)


def stacked(a, b):
    return jnp.concatenate([a, b], axis=0)


def both_halves(wide):
    return stacked(wide[:, :N], wide[:, N:])


def turn_back(x):
    swapped = roll(x, M, 1)
    return jnp.where(lanes(x.shape) < M, swapped, -swapped)


def turn_back_c(x):
    is_real = (lanes(x.shape) % M) < M // 2
    return jnp.where(is_real, roll(x, -M // 2, 1), -roll(x, M // 2, 1))


def butterfly(x):
    return jnp.where(lanes(x.shape) < M, x, -x) + roll(x, M, 1)


def cross(a, b):
    return (
        a[1] * b[2] - a[2] * b[1],
        a[2] * b[0] - a[0] * b[2],
        a[0] * b[1] - a[1] * b[0],
    )


def first_fine(f, axis):
    return (roll(f, 2, axis) - roll(f, -2, axis) + 8.0 * (roll(f, -1, axis) - roll(f, 1, axis))) * (
        1.0 / 12.0
    )


def second_fine_xy(f):
    near = (roll(f, 1, 0) + roll(f, -1, 0)) + (roll(f, 1, 1) + roll(f, -1, 1))
    far = (roll(f, 2, 0) + roll(f, -2, 0)) + (roll(f, 2, 1) + roll(f, -2, 1))
    return (16.0 * near - far - 60.0 * f) * (1.0 / 12.0)


def roll_half(f, shift):
    place = lanes(f.shape) % M
    keep = place >= shift if shift > 0 else place < M + shift
    return jnp.where(keep, roll(f, shift, 1), roll(f, shift - M if shift > 0 else shift + M, 1))


def first_coarse(f, along_x):
    go = (lambda s: roll(f, s, 0)) if along_x else (lambda s: roll_half(f, s))
    return (go(2) - go(-2) + 8.0 * (go(-1) - go(1))) * (1.0 / 24.0)


def second_coarse_xy(f):
    near = (roll(f, 1, 0) + roll(f, -1, 0)) + (roll_half(f, 1) + roll_half(f, -1))
    far = (roll(f, 2, 0) + roll(f, -2, 0)) + (roll_half(f, 2) + roll_half(f, -2))
    return (16.0 * near - far - 60.0 * f) * (1.0 / 48.0)


def first_next(a, b):
    return (a - 8.0 * b) * (1.0 / 12.0), b * (1.0 / 12.0)


def first_prev(a, b):
    return a * (-1.0 / 12.0), (8.0 * a - b) * (1.0 / 12.0)


def first_own(a, b):
    return b * (8.0 / 12.0), a * (-8.0 / 12.0)


def second_next(a, b):
    return (16.0 * b - a) * (1.0 / 12.0), b * (-1.0 / 12.0)


def second_prev(a, b):
    return a * (-1.0 / 12.0), (16.0 * a - b) * (1.0 / 12.0)


def second_own(a, b):
    return (16.0 * b - 30.0 * a) * (1.0 / 12.0), (16.0 * a - 30.0 * b) * (1.0 / 12.0)


def lane_pair(f, low, high):
    is_low = lanes(f.shape) < M
    own = jnp.where(is_low, low[0], high[0]).astype(f32)
    other = jnp.where(is_low, low[1], high[1]).astype(f32)
    return f * own + roll(f, M, 1) * other


T12 = 1.0 / 12.0


def c_first_next(f):
    return lane_pair(f, (T12, -8 * T12), (T12, 0.0))


def c_first_prev(f):
    return lane_pair(f, (-T12, 0.0), (-T12, 8 * T12))


def c_first_own(f):
    return lane_pair(f, (0.0, 8 * T12), (0.0, -8 * T12))


def c_second_next(f):
    return lane_pair(f, (-T12, 16 * T12), (-T12, 0.0))


def c_second_prev(f):
    return lane_pair(f, (-T12, 0.0), (-T12, 16 * T12))


def c_second_own(f):
    return lane_pair(f, (-30 * T12, 16 * T12), (-30 * T12, 16 * T12))


def along_both(fields, t, name):
    wide = by_table(jnp.concatenate(fields, axis=0), t, name)
    return [table_by(t, "c_x", both_halves(wide[c * M : c * M + M])) for c in range(len(fields))]


def inverse_square(kk, kx, mask):
    squared = kk + kx * kx
    live = squared > 0.0
    return jnp.where(live, mask / jnp.where(live, squared, 1.0), 0.0)


def solve_fine(planes, kx, inverse, t):
    hat = [table_by(t, "f_z", stacked(p, turn_back(p))) for p in planes]
    kz = t["f_kz"][...]
    ky = jnp.broadcast_to(t["f_ky"][0:1, :], kz.shape)
    out = []
    for r in cross((kx, ky, kz), hat):
        r = r * inverse
        out.append(table_by(t, "i_z", stacked(-turn_back(r), -r)))
    return out


def z_coarse(x, t):
    d = table_by(t, "c_x", stacked(x, turn_back_c(x)))
    return butterfly(t["tw_c"][...] * d + t["tw_s"][...] * turn_back_c(d))


def z_coarse_back(a, t):
    b = butterfly(a)
    b = t["tw_c"][...] * b - t["tw_s"][...] * turn_back_c(b)
    return table_by(t, "c_x", stacked(b, -turn_back_c(b)))


def velocity_modes(hat, kx, inverse, t):
    kz = t["c_kz"][...]
    ky = jnp.broadcast_to(t["c_ky"][0:1, :], kz.shape)
    return [-turn_back_c(r * inverse) for r in cross((kx, ky, kz), hat)]


def tendency_modes(flux, w, sx, lx, t):
    sz = t["c_sz"][...]
    sy = jnp.broadcast_to(t["c_sy"][0:1, :], sz.shape)
    spread = NU * (t["c_ll"][...] + lx)
    return [-turn_back_c(r) + spread * w[i] for i, r in enumerate(cross((sx, sy, sz), flux))]


def restrict(a, b, t):
    return exact(t["r_x"][...], exact(jnp.concatenate([a, b], axis=1), t["r_y"][...]))


def prolong(pair, t):
    wide = exact(exact(t["p_x"][...], pair), jnp.concatenate([t["p_y0"][...], t["p_y1"][...]], axis=1))
    return wide[:, :N], wide[:, N:]


SCRATCH = dict(
    node=pltpu.VMEM((3, 3, 2, N, N), f32),
    speed=pltpu.VMEM((3, 2, N, N), f32),
    flux=pltpu.VMEM((3, 2, N, N), f32),
    total=pltpu.VMEM((3, 2, N, N), f32),
    slope=pltpu.VMEM((3, 2, N, N), f32),
    half=pltpu.VMEM((3, 2, 2 * N, N), f32),
    gs=pltpu.VMEM((9, PARTS * THIRD, N), f32),
    gr=pltpu.VMEM((9, PARTS * THIRD, N), f32),
    fs=pltpu.VMEM((6, PARTS * FINE, N), f32),
    fr=pltpu.VMEM((6, PARTS * FINE, N), f32),
    cs=pltpu.VMEM((6, PARTS * COARSE, N), f32),
    cr=pltpu.VMEM((7, PARTS * COARSE, N), f32),
    fh_next=pltpu.VMEM((4, 3, 2, N, N), f32),
    fh_prev=pltpu.VMEM((4, 3, 2, N, N), f32),
    fh_low=pltpu.VMEM((4, 3, 2, N, N), f32),
    fh_high=pltpu.VMEM((4, 3, 2, N, N), f32),
    ch_next=pltpu.VMEM((5, 3, M, N), f32),
    ch_prev=pltpu.VMEM((5, 3, M, N), f32),
    ch_low=pltpu.VMEM((5, 3, M, N), f32),
    ch_high=pltpu.VMEM((5, 3, M, N), f32),
    hand_v=pltpu.VMEM((3, M, N), f32),
    hand_m=pltpu.VMEM((3, M, N), f32),
    send_v=pltpu.VMEM((3, M, N), f32),
    send_m=pltpu.VMEM((3, M, N), f32),
    co=pltpu.VMEM((14, 3, M, N), f32),
    inv_f=pltpu.VMEM((2, N, N), f32),
    inv_c=pltpu.VMEM((M, N), f32),
    g_ssem=pltpu.SemaphoreType.DMA((9,)),
    g_rsem=pltpu.SemaphoreType.DMA((9,)),
    f_ssem=pltpu.SemaphoreType.DMA((6,)),
    f_rsem=pltpu.SemaphoreType.DMA((6,)),
    c_ssem=pltpu.SemaphoreType.DMA((7,)),
    c_rsem=pltpu.SemaphoreType.DMA((7,)),
    h_ssem=pltpu.SemaphoreType.DMA((17, 2)),
    h_rsem=pltpu.SemaphoreType.DMA((17, 2)),
    y_ssem=pltpu.SemaphoreType.DMA((3,)),
    y_rsem=pltpu.SemaphoreType.DMA((3,)),
    in_sem=pltpu.SemaphoreType.DMA((OPERANDS,)),
)
A0, A2, UA0, UA2, G0, G2, C1, C2, CM1, CM2, B1, S1, BM1, SM1 = range(14)


def kernel(*refs):
    nodes, q_out = refs[OPERANDS : OPERANDS + 2]
    staged = refs[OPERANDS + 2 : 2 * OPERANDS + 2]
    init, end, old = staged[:3]
    s = dict(zip(SCRATCH, refs[2 * OPERANDS + 2 :]))
    t = {}
    for places, packed in ((PLACES_32, staged[3]), (PLACES_16, staged[4])):
        for name, (top, shape) in places.items():
            t[name] = packed.at[pl.ds(top, shape[0]), pl.ds(0, shape[1])]
    loads = [
        pltpu.make_async_copy(source, target, s["in_sem"].at[i])
        for i, (source, target) in enumerate(zip(refs[:OPERANDS], staged))
    ]
    co = s["co"]
    row = lax.axis_index("tm")
    me = lax.axis_index("space")
    ahead = lax.rem(me + 1, PARTS)
    behind = lax.rem(me + PARTS - 1, PARTS)
    up = lax.rem(row + 1, ROWS)
    down = lax.rem(row + ROWS - 1, ROWS)

    barrier = pltpu.get_barrier_semaphore()

    place_x, place_z, core = me // 16, lax.rem(me // 2, 8), lax.rem(me, 2)

    def partner(z, x, c):
        return (lax.rem(place_x + x, 4) * 8 + lax.rem(place_z + z, 8)) * 2 + lax.rem(core + c, 2)

    def greet(z, x, c, rows):
        for other in rows:
            pl.semaphore_signal(barrier, inc=1, device_id=(other, partner(z, x, c)), device_id_type=MESH)

    def greet_far(j, carry):
        z = 4 + ((j + 1) // 2) * (1 - 2 * lax.rem(j, 2))
        for x in (2, 1, 3, 0):
            for c in (1, 0):
                greet(z, x, c, (up, down, row))
        return carry

    for i in (0, 1, 4, 3, 2):
        loads[i].start()
    lax.fori_loop(0, 7, greet_far, 0)
    for x in (2, 1, 3, 0):
        for c in (1, 0):
            greet(0, x, c, (up, down, row) if x or c else (up, down))
    for i in (0, 1, 3, 4):
        loads[i].wait()


    def transpose_start(send, recv, depth, ssem, rsem, to_row=None):
        mine = pl.ds(me * depth, depth)

        def post(z, x, c):
            to = partner(z, x, c)
            pltpu.make_async_remote_copy(
                src_ref=send.at[pl.ds(to * depth, depth)],
                dst_ref=recv.at[mine],
                send_sem=ssem,
                recv_sem=rsem,
                device_id=(row if to_row is None else to_row, to),
                device_id_type=MESH,
            ).start()

        def step(j, carry):
            z = 4 + ((j + 1) // 2) * (1 - 2 * lax.rem(j, 2))
            for x in (2, 1, 3, 0):
                for c in (1, 0):
                    post(z, x, c)
            return carry

        lax.fori_loop(0, 7, step, 0)
        for x in (2, 1, 3, 0):
            for c in (1, 0):
                if x or c or to_row is not None:
                    post(0, x, c)
        if to_row is None:
            pltpu.make_async_copy(send.at[mine], recv.at[mine], rsem).start()

    def arrived(ref, sem):
        pltpu.make_async_copy(ref, ref, sem).wait()

    def left(ref, depth, sem, parts=PARTS - 1):
        part = ref.at[pl.ds(0, parts * depth)]
        pltpu.make_async_copy(part, part, sem).wait()

    def third_start(i, to_row):
        transpose_start(s["gs"].at[i], s["gr"].at[i], THIRD, s["g_ssem"].at[i], s["g_rsem"].at[i], to_row)

    def third_wait(i):
        arrived(s["gr"].at[i], s["g_rsem"].at[i])

    def fine_start(i):
        transpose_start(s["fs"].at[i], s["fr"].at[i], FINE, s["f_ssem"].at[i], s["f_rsem"].at[i])

    def coarse_start(i):
        transpose_start(s["cs"].at[i], s["cr"].at[i], COARSE, s["c_ssem"].at[i], s["c_rsem"].at[i])

    def fine_wait(i):
        arrived(s["fr"].at[i], s["f_rsem"].at[i])

    def coarse_wait(i):
        arrived(s["cr"].at[i], s["c_rsem"].at[i])

    def halo_copies(kind, at, sem):
        def copy(out, into, side, to):
            return pltpu.make_async_remote_copy(
                src_ref=s[kind + out].at[at],
                dst_ref=s[kind + into].at[at],
                send_sem=s["h_ssem"].at[sem, side],
                recv_sem=s["h_rsem"].at[sem, side],
                device_id=(row, to),
                device_id_type=MESH,
            )

        return copy("h_next", "h_low", 0, ahead), copy("h_prev", "h_high", 1, behind)

    def fine_halo(m, c):
        return halo_copies("f", (m, c), 3 * m + c)

    def coarse_halo_copies(i):
        return halo_copies("c", i, 12 + i)

    def begin(copies):
        for copy in copies:
            copy.start()

    def landed(copies):
        for copy in copies:
            copy.wait_recv()

    def gone(copies):
        for copy in copies:
            copy.wait_send()

    def hand_copy(src, dst, sem):
        return pltpu.make_async_remote_copy(
            src_ref=src,
            dst_ref=dst,
            send_sem=s["y_ssem"].at[sem],
            recv_sem=s["y_rsem"].at[sem],
            device_id=(up, me),
            device_id_type=MESH,
        )

    start_copy = hand_copy(end.at[0], s["node"].at[0], 0)
    v_copy = hand_copy(s["send_v"], s["hand_v"], 1)
    m_copy = hand_copy(s["send_m"], s["hand_m"], 2)
    is_first = row == 0
    has_next = row < ROWS - 1


    def fine_spread(c, z, plane):
        s["half"][c, z] = both_halves(by_table(plane, t, "f_y"))


    def send_z(m, to_row=None):
        for z in range(2):
            out = table_by(t, "f_x", s["half"][2, z])
            for low in range(2):
                s["gs"][3 * m, pl.ds(2 * low + z, PARTS, stride=THIRD), :] = out[low * M : low * M + M]
        third_start(3 * m, to_row)

    def send_xy(m, to_row=None):
        for low in range(2):
            for c in range(2):
                for z in range(2):
                    s["gs"][3 * m + 1 + low, pl.ds(2 * c + z, PARTS, stride=THIRD), :] = table_by(
                        t, "f_x", s["half"][c, z], slice(low * M, low * M + M)
                    )
            third_start(3 * m + 1 + low, to_row)

    def fine_modes(m):
        third_wait(3 * m)
        for low in range(2):
            third_wait(3 * m + 1 + low)
            places = [(1 + low, 0), (1 + low, 2), (0, 2 * low)]
            planes = [
                stacked(*[s["gr"][3 * m + part, pl.ds(at + z, PARTS, stride=THIRD), :] for z in range(2)])
                for part, at in places
            ]
            kx = jnp.broadcast_to(t["f_kx"][pl.ds(me * 2 + low, 1), :], (N, N))
            for c, out in enumerate(solve_fine(planes, kx, s["inv_f"][low], t)):
                for z in range(2):
                    s["fs"][2 * m + low, pl.ds(c * 2 + z, PARTS, stride=FINE), :] = out[z * M : z * M + M]
            fine_start(2 * m + low)

    def fine_velocity(m):
        for low in range(2):
            fine_wait(2 * m + low)
            for c in range(3):
                modes = stacked(*[s["fr"][2 * m + low, pl.ds(c * 2 + z, PARTS, stride=FINE), :] for z in range(2)])
                wide = by_table(modes, t, "i_y")
                for z in range(2):
                    part = wide[z * M : z * M + M]
                    s["half"][c, z, low * M : low * M + M, :] = part[:, :N]
                    s["half"][c, z, N + low * M : N + low * M + M, :] = part[:, N:]
        for c in range(3):
            for z in range(2):
                s["speed"][c, z] = table_by(t, "i_x", s["half"][c, z])

    node, speed, flux, total = s["node"], s["speed"], s["flux"], s["total"]

    def fine_flux(m):
        for z in range(2):
            parts = cross([speed[c, z] for c in range(3)], [node[m, c, z] for c in range(3)])
            for c in range(3):
                flux[c, z] = parts[c]
        for c in range(2):
            fine_shares(m, c)

    def fine_shares(m, c):
        w0, w1 = node[m, c, 0], node[m, c, 1]
        ahead0, ahead1 = second_next(w0, w1)
        back0, back1 = second_prev(w0, w1)
        ahead0, ahead1, back0, back1 = NU * ahead0, NU * ahead1, NU * back0, NU * back1
        if c < 2:
            sign = -1.0 if c == 0 else 1.0
            g0, g1 = sign * flux[1 - c, 0], sign * flux[1 - c, 1]
            d0, d1 = first_next(g0, g1)
            e0, e1 = first_prev(g0, g1)
            ahead0, ahead1, back0, back1 = ahead0 + d0, ahead1 + d1, back0 + e0, back1 + e1
        s["fh_next"][m, c, 0] = ahead0
        s["fh_next"][m, c, 1] = ahead1
        s["fh_prev"][m, c, 0] = back0
        s["fh_prev"][m, c, 1] = back1
        begin(fine_halo(m, c))

    def fine_local(m, c):
        w0, w1 = node[m, c, 0], node[m, c, 1]
        own = [NU * v for v in second_own(w0, w1)]
        if c < 2:
            sign = -1.0 if c == 0 else 1.0
            extra = first_own(sign * flux[1 - c, 0], sign * flux[1 - c, 1])
            own = [own[z] + extra[z] for z in range(2)]
        out = []
        for z in range(2):
            if c == 0:
                curl = first_fine(flux[2, z], 1)
            elif c == 1:
                curl = -first_fine(flux[2, z], 0)
            else:
                curl = first_fine(flux[1, z], 0) - first_fine(flux[0, z], 1)
            out.append(curl + NU * second_fine_xy((w0, w1)[z]) + own[z])
        return out


    def coarse_send(values, i):
        for c, out in enumerate(along_both(values, t, "cf_y")):
            s["cs"][i, pl.ds(c, PARTS, stride=COARSE), :] = out

    def coarse_recv(i):
        return [s["cr"][i, pl.ds(c, PARTS, stride=COARSE), :] for c in range(3)]

    def coarse_modes(i):
        return [z_coarse(x, t) for x in coarse_recv(i)]

    def coarse_velocity(i):
        return along_both(coarse_recv(i), t, "ci_y")

    mine = pl.ds(me, 1)
    wide = lambda name: jnp.broadcast_to(t[name][mine, :], (M, N))

    def coarse_back(hat, i):
        modes = velocity_modes(hat, wide("c_kx"), s["inv_c"][...], t)
        for c in range(3):
            s["cs"][i, pl.ds(c, PARTS, stride=COARSE), :] = z_coarse_back(modes[c], t)

    def coarse_halo(f, w, i):
        g = (-f[1], f[0], None)
        for c in range(3):
            nxt, prv = NU * c_second_next(w[c]), NU * c_second_prev(w[c])
            if g[c] is not None:
                nxt, prv = nxt + c_first_next(g[c]), prv + c_first_prev(g[c])
            s["ch_next"][i, c] = nxt
            s["ch_prev"][i, c] = prv
        begin(coarse_halo_copies(i))

    def coarse_tendency(f, w, i):
        own = [NU * (second_coarse_xy(w[c]) + c_second_own(w[c])) for c in range(3)]
        parts = [
            first_coarse(f[2], False) - c_first_own(f[1]),
            c_first_own(f[0]) - first_coarse(f[2], True),
            first_coarse(f[1], True) - first_coarse(f[0], False),
        ]
        landed(coarse_halo_copies(i))
        return [own[c] + parts[c] + (s["ch_low"][i, c] + s["ch_high"][i, c]) for c in range(3)]

    def keep(i, values):
        for c in range(3):
            co[i, c] = values[c]

    def kept(i):
        return [co[i, c] for c in range(3)]

    def restricted(get):
        return [restrict(get(c, 0), get(c, 1), t) for c in range(3)]

    for low in range(2):
        at = pl.ds(me * 2 + low, 1)
        kx = jnp.broadcast_to(t["f_kx"][at, :], (N, N))
        mask = t["f_mz"][...] * jnp.broadcast_to(t["f_mx"][at, :], (N, N))
        s["inv_f"][low] = inverse_square(t["f_kk"][...], kx, mask)
    s["inv_c"][...] = inverse_square(t["c_kk"][...], wide("c_kx"), t["c_mz"][...] * wide("c_mx"))

    f0 = lambda c, z: old[0, 0, c, z]
    f1 = lambda c, z: old[0, 1, c, z]
    f2 = lambda c, z: old[0, 2, c, z]

    for c in range(3):
        for z in range(2):
            fine_spread(c, z, jnp.where(has_next, end[0, c, z], init[c, z]))
    pl.semaphore_wait(barrier, 3 * PARTS - 1)

    for m in range(3):
        if m == 0:
            send_z(0, up)
            send_xy(0, up)
        else:
            send_xy(m)
            fine_shares(m, 2)
        if m == 1:
            keep(UA0, restricted(lambda c, z: speed[c, z]))
            flux_g0 = cross(kept(UA0), kept(A0))
            coarse_halo(flux_g0, kept(A0), 0)
            keep(G0, coarse_tendency(flux_g0, kept(A0), 0))
        if m == 2:
            keep(A2, restricted(lambda c, z: node[2, c, z]))
        fine_modes(m)
        if m == 0:

            @pl.when(has_next)
            def _():
                start_copy.start()

            @pl.when(is_first)
            def _():
                for c in range(3):
                    for z in range(2):
                        node[0, c, z] = init[c, z]

            @pl.when(jnp.logical_not(is_first))
            def _():
                start_copy.wait_recv()

            fine_shares(0, 2)
            keep(A0, restricted(lambda c, z: node[0, c, z]))
            loads[2].wait()
        fine_velocity(m)
        fine_flux(m)
        if m == 2:
            keep(UA2, restricted(lambda c, z: speed[c, z]))
            flux_g2 = cross(kept(UA2), kept(A2))
            coarse_halo(flux_g2, kept(A2), 1)
        weight = (DT / 6.0, DT * 2.0 / 3.0, DT / 6.0)[m]
        if m < 2:
            def advance(c):
                local = fine_local(m, c)
                for z in range(2):
                    total[c, z] = weight * local[z] if m == 0 else total[c, z] + weight * local[z]
                    if m == 0:
                        old_part = (
                            (DT * 5.0 / 24.0 - HALF) * f0(c, z)
                            + (DT / 3.0) * f1(c, z)
                            - (DT / 24.0) * f2(c, z)
                        )
                    else:
                        old_part = (
                            (-DT / 24.0) * f0(c, z)
                            + (DT / 3.0 - HALF) * f1(c, z)
                            + (DT * 5.0 / 24.0) * f2(c, z)
                        )
                    node[m + 1, c, z] = node[m, c, z] + HALF * local[z] + old_part

            def finish(c):
                landed(fine_halo(m, c))
                for z in range(2):
                    share = s["fh_low"][m, c, z] + s["fh_high"][m, c, z]
                    total[c, z] = total[c, z] + weight * share
                    fresh = node[m + 1, c, z] + HALF * share
                    node[m + 1, c, z] = fresh
                    fine_spread(c, z, fresh)

            advance(2)
            finish(2)
            send_z(m + 1)
            for c in range(2):
                advance(c)
            for c in range(2):
                finish(c)
        else:
            for c in range(3):
                local = fine_local(m, c)
                for z in range(2):
                    total[c, z] = total[c, z] + weight * local[z]
            for c in (2, 0, 1):
                landed(fine_halo(m, c))
                for z in range(2):
                    share = s["fh_low"][m, c, z] + s["fh_high"][m, c, z]
                    total[c, z] = total[c, z] + weight * share

    rest = restricted(lambda c, z: total[c, z])
    keep(C1, [rest[c] + jnp.where(is_first, co[A0, c], -DT * co[G0, c]) for c in range(3)])
    coarse_send(kept(C1), 0)
    coarse_start(0)
    keep(G2, coarse_tendency(flux_g2, kept(A2), 1))
    keep(
        C2,
        [
            rest[c] - HALF * co[G2, c] + jnp.where(is_first, co[A0, c], -HALF * co[G0, c])
            for c in range(3)
        ],
    )
    coarse_send(kept(C2), 1)
    coarse_start(1)

    coarse_wait(0)
    keep(CM1, coarse_modes(0))
    sx, lx = wide("c_sx"), wide("c_lx")

    def end_shares():
        for c in range(3):
            a, b = speed[c, 0], speed[c, 1]
            s["fh_next"][3, c, 0], s["fh_next"][3, c, 1] = first_next(a, b)
            s["fh_prev"][3, c, 0], s["fh_prev"][3, c, 1] = first_prev(a, b)
            begin(fine_halo(3, c))

    @pl.when(is_first)
    def _():
        keep(BM1, kept(CM1))
        keep(B1, kept(C1))
        keep(S1, kept(C2))
        for c in range(3):
            s["hand_v"][c] = co[A0, c]

    @pl.when(jnp.logical_not(is_first))
    def _():
        coarse_wait(1)
        keep(CM2, coarse_modes(1))
        end_shares()
        v_copy.wait_recv()
        start = [s["hand_v"][c] for c in range(3)]
        coarse_wait(6)
        f = cross(coarse_velocity(6), start)
        coarse_send(f, 2)
        coarse_start(2)
        coarse_halo(f, start, 2)
        early = coarse_tendency(f, start, 2)
        keep(B1, [start[c] + DT * early[c] + co[C1, c] for c in range(3)])
        keep(S1, [start[c] + HALF * early[c] + co[C2, c] for c in range(3)])
        m_copy.wait_recv()
        coarse_wait(2)
        held = [s["hand_m"][c] for c in range(3)]
        early = tendency_modes(coarse_modes(2), held, sx, lx, t)
        keep(BM1, [held[c] + DT * early[c] + co[CM1, c] for c in range(3)])
        keep(SM1, [held[c] + HALF * early[c] + co[CM2, c] for c in range(3)])

    coarse_back(kept(BM1), 3)
    coarse_start(3)

    @pl.when(is_first)
    def _():
        coarse_wait(1)
        keep(SM1, coarse_modes(1))

    coarse_wait(3)
    middle = kept(B1)
    f = cross(coarse_velocity(3), middle)
    coarse_send(f, 4)
    coarse_start(4)
    coarse_halo(f, middle, 3)
    later = coarse_tendency(f, middle, 3)
    for c in range(3):
        s["send_v"][c] = co[S1, c] + HALF * later[c]

    @pl.when(has_next)
    def _():
        v_copy.start()

    coarse_wait(4)
    later = tendency_modes(coarse_modes(4), kept(BM1), sx, lx, t)
    for c in range(3):
        s["send_m"][c] = co[SM1, c] + HALF * later[c]
    coarse_back([s["send_m"][c] for c in range(3)], 5)

    @pl.when(has_next)
    def _():
        transpose_start(s["cs"].at[5], s["cr"].at[6], COARSE, s["c_ssem"].at[6], s["c_rsem"].at[6], up)
        m_copy.start()

    @pl.when(jnp.logical_not(has_next))
    def _():
        coarse_start(5)

    @pl.when(is_first)
    def _():
        end_shares()

    for c in range(3):
        zero = prolong(s["hand_v"][c] - co[A0, c], t)
        two = prolong(s["send_v"][c] - co[A2, c], t)
        for z in range(2):
            nodes[0, 0, c, z] = node[0, c, z] + zero[z]
            nodes[0, 1, c, z] = node[1, c, z] + 0.5 * (zero[z] + two[z])
            nodes[0, 2, c, z] = node[2, c, z] + two[z]

    @pl.when(has_next)
    def _():
        coarse_start(5)

    slope = s["slope"]
    for c in range(3):
        landed(fine_halo(3, c))
        own = first_own(speed[c, 0], speed[c, 1])
        for z in range(2):
            slope[c, z] = own[z] + (s["fh_low"][3, c, z] + s["fh_high"][3, c, z])

    coarse_wait(5)
    out = coarse_velocity(5)

    change = [out[c] - co[UA2, c] for c in range(3)]
    for c in range(3):
        s["ch_next"][4, c] = c_first_next(change[c])
        s["ch_prev"][4, c] = c_first_prev(change[c])
    begin(coarse_halo_copies(4))
    for c in range(3):
        put = prolong(change[c], t)
        for z in range(2):
            speed[c, z] = speed[c, z] + put[z]
    own = [c_first_own(change[c]) for c in range(3)]
    landed(coarse_halo_copies(4))
    for c in range(3):
        put = prolong(own[c] + (s["ch_low"][4, c] + s["ch_high"][4, c]), t)
        for z in range(2):
            slope[c, z] = slope[c, z] + put[z]
    for z in range(2):
        gx = [first_fine(speed[c, z], 0) for c in range(3)]
        gy = [first_fine(speed[c, z], 1) for c in range(3)]
        gz = [slope[c, z] for c in range(3)]
        diagonal = gx[0] * gx[0] + gy[1] * gy[1] + gz[2] * gz[2]
        mixed = gx[1] * gy[0] + gx[2] * gz[0] + gy[2] * gz[1]
        q_out[0, z] = -0.5 * diagonal - mixed

    for i in range(9):
        left(s["gs"].at[i], THIRD, s["g_ssem"].at[i], PARTS if i < 3 else PARTS - 1)
    for i in range(6):
        left(s["fs"].at[i], FINE, s["f_ssem"].at[i])
    for i in (0, 1, 3, 4, 5):
        left(s["cs"].at[i], COARSE, s["c_ssem"].at[i])

    @pl.when(jnp.logical_not(is_first))
    def _():
        left(s["cs"].at[2], COARSE, s["c_ssem"].at[2])
        gone(coarse_halo_copies(2))

    for i in range(4):
        for c in range(3):
            gone(fine_halo(i, c))
    for i in (0, 1, 3, 4):
        gone(coarse_halo_copies(i))

    @pl.when(has_next)
    def _():
        left(s["cs"].at[5], COARSE, s["c_ssem"].at[6], PARTS)
        for copy in (start_copy, v_copy, m_copy):
            copy.wait_send()


def body(initial_state, end_states, old_tendencies):
    vmem = pl.BlockSpec(memory_space=pltpu.VMEM)
    operands = [initial_state, end_states, old_tendencies, jnp.asarray(PACKED_32), jnp.asarray(PACKED_16)]
    return pl.pallas_call(
        kernel,
        out_shape=(
            jax.ShapeDtypeStruct((1, 3, 3, 2, N, N), f32),
            jax.ShapeDtypeStruct((1, 2, N, N), f32),
        ),
        in_specs=[pl.BlockSpec(memory_space=pl.ANY)] * len(operands),
        out_specs=(vmem, vmem),
        scratch_shapes=[pltpu.VMEM(x.shape, x.dtype) for x in operands] + list(SCRATCH.values()),
        compiler_params=pltpu.CompilerParams(
            collective_id=0, has_side_effects=True, vmem_limit_bytes=56 * 1024 * 1024
        ),
    )(*operands)


def solution(mesh):
    in_specs = (
        P(None, "space", None, None),
        P("tm", None, "space", None, None),
        P("tm", None, None, "space", None, None),
    )
    out_specs = (P("tm", None, None, "space", None, None), P("tm", "space", None, None))
    return jax.shard_map(body, mesh=mesh, in_specs=in_specs, out_specs=out_specs, check_vma=False)
```

```python
import math

import jax
import jax.numpy as jnp
import numpy as np
from jax import lax
from jax.experimental import pallas as pl
from jax.experimental.pallas import tpu as pltpu
from jax.sharding import PartitionSpec as P

DT = 0.4
HALF = 0.2
NU = 0.1
PARTS = 64
ROWS = 4
N = 128
M = 64
FINE = 6
THIRD = 4
COARSE = 3
f32 = jnp.float32
MESH = pl.DeviceIdType.MESH


def angle_tables(left, right, count):
    angles = (2.0 * math.pi / count) * (np.outer(left, right) % count)
    return np.cos(angles), np.sin(angles)


def restriction_table(count):
    cos_c, sin_c = angle_tables(np.arange(count // 2), np.arange(count // 4), count // 2)
    cos_f, sin_f = angle_tables(np.arange(count), np.arange(count // 4), count)
    weight = np.where(np.arange(count // 4) == 0, 1.0, 2.0)
    return ((cos_c * weight) @ cos_f.T + (sin_c * weight) @ sin_f.T) / count


def twice(block):
    zero = np.zeros_like(block)
    return np.block([[block, zero], [zero, block]])


def wave_symbols(ids, count, spacing):
    theta = 2.0 * math.pi * ids / count
    kappa = theta / spacing
    first = (8.0 * np.sin(theta) - np.sin(2.0 * theta)) / (6.0 * spacing)
    second = (-2.0 * np.cos(2.0 * theta) + 32.0 * np.cos(theta) - 30.0) / (12.0 * spacing**2)
    return kappa, first, second


def signed(ids, count):
    return np.where(ids < count // 2, ids, ids - count)


def build_tables():
    t = {}
    grid = np.arange(N)
    owner = np.concatenate([2 * np.arange(PARTS), 2 * np.arange(PARTS) + 1])
    cos_y, sin_y = angle_tables(grid, np.arange(M), N)
    t["f_y"] = np.hstack([cos_y, -sin_y, -sin_y, -cos_y])
    t["f_x"] = np.hstack(angle_tables(owner, grid, N))
    t["f_z"] = np.hstack(angle_tables(grid, owner, N))
    t["i_z"] = np.hstack(angle_tables(owner, grid, N))
    t["i_x"] = np.hstack(angle_tables(grid, owner, N))
    weight = np.where(np.arange(M) == 0, 1.0, 2.0) / float(N**3)
    wc, ws = (cos_y * weight).T, (sin_y * weight).T
    t["i_y"] = np.hstack([np.vstack([wc, -ws]), np.vstack([-ws, -wc])])
    half = np.arange(M // 2)
    cos_y, sin_y = angle_tables(np.arange(M), half, M)
    t["cf_y"] = np.hstack([twice(np.hstack([cos_y, -sin_y])), twice(np.hstack([-sin_y, -cos_y]))])
    t["c_x"] = np.hstack(angle_tables(np.arange(M), np.arange(M), M))
    weight = np.where(half == 0, 1.0, 2.0) / float(M * M * N)
    wc, ws = (cos_y * weight).T, (sin_y * weight).T
    t["ci_y"] = np.hstack([twice(np.vstack([wc, -ws])), twice(np.vstack([-ws, -wc]))])
    table = restriction_table(N)
    t["r_x"] = table
    t["r_y"] = twice(table.T)
    t["p_x"] = 4.0 * table.T
    t["p_y"] = twice(table)
    kx, _, _ = wave_symbols(signed(grid, N), N, 1.0)
    ky = np.tile(kx[:M], 2)[None, :]
    ones = np.ones((1, N))
    t["f_kx"] = kx[:, None] * ones
    t["f_mx"] = (grid != M)[:, None] * ones
    t["f_ky"] = np.repeat(ky, 8, axis=0)
    t["f_kz"] = kx[:, None] * ones
    t["f_kk"] = ky**2 + kx[:, None] ** 2
    t["f_mz"] = t["f_mx"]
    ckx, sx, lx = wave_symbols(signed(np.arange(M), M), M, 2.0)
    t["c_kx"] = ckx[:, None] * ones
    t["c_mx"] = (np.arange(M) != M // 2)[:, None] * ones
    t["c_sx"] = sx[:, None] * ones
    t["c_lx"] = lx[:, None] * ones
    lane = lambda v: np.tile(v[: M // 2], 4)[None, :]
    cky, sy, ly = lane(ckx), lane(sx), lane(lx)
    zid = np.hstack([np.repeat(np.arange(M)[:, None], M, 1), np.repeat(np.arange(M)[:, None] + M, M, 1)])
    ckz, sz, lz = wave_symbols(signed(zid, N), N, 1.0)
    t["c_ky"] = np.repeat(cky, 8, axis=0)
    t["c_sy"] = np.repeat(sy, 8, axis=0)
    t["c_kz"] = ckz
    t["c_sz"] = sz
    t["c_kk"] = cky**2 + ckz**2
    t["c_mz"] = (zid != M) * 1.0
    t["c_ll"] = ly + lz
    turn = 2.0 * math.pi * np.arange(M)[:, None] / N
    first = (np.arange(N) < M)[None, :]
    t["tw_c"] = np.where(first, 1.0, np.cos(turn))
    t["tw_s"] = np.where(first, 0.0, np.sin(turn))
    made = {}
    for name, value in t.items():
        value = np.asarray(value, np.float32)
        if name in SPLIT:
            high = value.astype(jnp.bfloat16)
            made[name + "_h"] = high
            if name in RIGHT:
                made[name + "_h"] = np.vstack([high, high])
            if name in LEFT:
                made[name + "_h"] = np.hstack([high, high])
            low = (value - high.astype(np.float32)).astype(jnp.bfloat16)
            made[name + "_l"] = np.hstack([low, np.zeros_like(low)]) if name in LEFT else low
        else:
            made[name] = value
    return made


RIGHT = ("f_y", "i_y", "cf_y", "ci_y", "p_y")
LEFT = ("c_x", "r_x", "p_x")
SPLIT = ("r_x", "r_y", "p_x", "p_y", "f_x", "f_y", "f_z", "i_x", "i_y", "i_z", "cf_y", "c_x", "ci_y")
TABLES = build_tables()


def pack(kind, width):
    places, blocks, top = {}, [], 0
    for name in sorted(TABLES):
        value = TABLES[name]
        if value.dtype == kind:
            block = np.zeros((value.shape[0], width), kind)
            block[:, : value.shape[1]] = value
            places[name] = (top, value.shape)
            blocks.append(block)
            top += value.shape[0]
    return places, np.concatenate(blocks)


PLACES_32, PACKED_32 = pack(np.float32, N)
PLACES_16, PACKED_16 = pack(jnp.bfloat16, 2 * N)
OPERANDS = 5


def dot(a, b):
    return jnp.dot(a, b, preferred_element_type=f32)


def split(x):
    high = x.astype(jnp.bfloat16)
    return high, (x - high.astype(f32)).astype(jnp.bfloat16)


def by_table(x, t, name):
    high, low = split(x)
    table = t[name + "_h"][...]
    rest = dot(high, t[name + "_l"][...])
    if name in RIGHT:
        return dot(jnp.concatenate([high, low], axis=1), table) + rest
    return dot(high, table) + (dot(low, table) + rest)


def table_by(t, name, x, rows=slice(None)):
    high, low = split(x)
    table = t[name + "_h"][rows, :]
    if name in LEFT:
        both = jnp.concatenate([high, low], axis=0)
        return dot(table, both) + dot(t[name + "_l"][...], both)
    return dot(table, high) + (dot(table, low) + dot(t[name + "_l"][rows, :], high))


def roll(x, shift, axis):
    return pltpu.roll(x, shift % x.shape[axis], axis)


def lanes(shape):
    return lax.broadcasted_iota(jnp.int32, shape, 1)


def stacked(a, b):
    return jnp.concatenate([a, b], axis=0)


def both_halves(wide):
    return stacked(wide[:, :N], wide[:, N:])


def turn_back(x):
    swapped = roll(x, M, 1)
    return jnp.where(lanes(x.shape) < M, swapped, -swapped)


def turn_back_c(x):
    is_real = (lanes(x.shape) % M) < M // 2
    return jnp.where(is_real, roll(x, -M // 2, 1), -roll(x, M // 2, 1))


def butterfly(x):
    return jnp.where(lanes(x.shape) < M, x, -x) + roll(x, M, 1)


def cross(a, b):
    return (
        a[1] * b[2] - a[2] * b[1],
        a[2] * b[0] - a[0] * b[2],
        a[0] * b[1] - a[1] * b[0],
    )


def first_fine(f, axis):
    return (roll(f, 2, axis) - roll(f, -2, axis) + 8.0 * (roll(f, -1, axis) - roll(f, 1, axis))) * (
        1.0 / 12.0
    )


def second_fine_xy(f):
    near = (roll(f, 1, 0) + roll(f, -1, 0)) + (roll(f, 1, 1) + roll(f, -1, 1))
    far = (roll(f, 2, 0) + roll(f, -2, 0)) + (roll(f, 2, 1) + roll(f, -2, 1))
    return (16.0 * near - far - 60.0 * f) * (1.0 / 12.0)


def roll_half(f, shift):
    place = lanes(f.shape) % M
    keep = place >= shift if shift > 0 else place < M + shift
    return jnp.where(keep, roll(f, shift, 1), roll(f, shift - M if shift > 0 else shift + M, 1))


def first_coarse(f, along_x):
    go = (lambda s: roll(f, s, 0)) if along_x else (lambda s: roll_half(f, s))
    return (go(2) - go(-2) + 8.0 * (go(-1) - go(1))) * (1.0 / 24.0)


def second_coarse_xy(f):
    near = (roll(f, 1, 0) + roll(f, -1, 0)) + (roll_half(f, 1) + roll_half(f, -1))
    far = (roll(f, 2, 0) + roll(f, -2, 0)) + (roll_half(f, 2) + roll_half(f, -2))
    return (16.0 * near - far - 60.0 * f) * (1.0 / 48.0)


def first_next(a, b):
    return (a - 8.0 * b) * (1.0 / 12.0), b * (1.0 / 12.0)


def first_prev(a, b):
    return a * (-1.0 / 12.0), (8.0 * a - b) * (1.0 / 12.0)


def first_own(a, b):
    return b * (8.0 / 12.0), a * (-8.0 / 12.0)


def second_next(a, b):
    return (16.0 * b - a) * (1.0 / 12.0), b * (-1.0 / 12.0)


def second_prev(a, b):
    return a * (-1.0 / 12.0), (16.0 * a - b) * (1.0 / 12.0)


def second_own(a, b):
    return (16.0 * b - 30.0 * a) * (1.0 / 12.0), (16.0 * a - 30.0 * b) * (1.0 / 12.0)


def lane_pair(f, low, high):
    is_low = lanes(f.shape) < M
    own = jnp.where(is_low, low[0], high[0]).astype(f32)
    other = jnp.where(is_low, low[1], high[1]).astype(f32)
    return f * own + roll(f, M, 1) * other


T12 = 1.0 / 12.0


def c_first_next(f):
    return lane_pair(f, (T12, -8 * T12), (T12, 0.0))


def c_first_prev(f):
    return lane_pair(f, (-T12, 0.0), (-T12, 8 * T12))


def c_first_own(f):
    return lane_pair(f, (0.0, 8 * T12), (0.0, -8 * T12))


def c_second_next(f):
    return lane_pair(f, (-T12, 16 * T12), (-T12, 0.0))


def c_second_prev(f):
    return lane_pair(f, (-T12, 0.0), (-T12, 16 * T12))


def c_second_own(f):
    return lane_pair(f, (-30 * T12, 16 * T12), (-30 * T12, 16 * T12))


def along_both(fields, t, name):
    wide = by_table(jnp.concatenate(fields, axis=0), t, name)
    return [table_by(t, "c_x", both_halves(wide[c * M : c * M + M])) for c in range(len(fields))]


def inverse_square(kk, kx, mask):
    squared = kk + kx * kx
    live = squared > 0.0
    return jnp.where(live, mask / jnp.where(live, squared, 1.0), 0.0)


def solve_fine(planes, kx, inverse, t):
    hat = [table_by(t, "f_z", stacked(p, turn_back(p))) for p in planes]
    kz = t["f_kz"][...]
    ky = jnp.broadcast_to(t["f_ky"][0:1, :], kz.shape)
    out = []
    for r in cross((kx, ky, kz), hat):
        r = r * inverse
        out.append(table_by(t, "i_z", stacked(-turn_back(r), -r)))
    return out


def z_coarse(x, t):
    d = table_by(t, "c_x", stacked(x, turn_back_c(x)))
    return butterfly(t["tw_c"][...] * d + t["tw_s"][...] * turn_back_c(d))


def z_coarse_back(a, t):
    b = butterfly(a)
    b = t["tw_c"][...] * b - t["tw_s"][...] * turn_back_c(b)
    return table_by(t, "c_x", stacked(b, -turn_back_c(b)))


def velocity_modes(hat, kx, inverse, t):
    kz = t["c_kz"][...]
    ky = jnp.broadcast_to(t["c_ky"][0:1, :], kz.shape)
    return [-turn_back_c(r * inverse) for r in cross((kx, ky, kz), hat)]


def tendency_modes(flux, w, sx, lx, t):
    sz = t["c_sz"][...]
    sy = jnp.broadcast_to(t["c_sy"][0:1, :], sz.shape)
    spread = NU * (t["c_ll"][...] + lx)
    return [-turn_back_c(r) + spread * w[i] for i, r in enumerate(cross((sx, sy, sz), flux))]


def restrict(pairs, t):
    wide = by_table(jnp.concatenate([jnp.concatenate(pair, axis=1) for pair in pairs], axis=0), t, "r_y")
    return [table_by(t, "r_x", wide[c * N : c * N + N]) for c in range(len(pairs))]


def prolong(pairs, t):
    wide = by_table(jnp.concatenate([table_by(t, "p_x", pair) for pair in pairs], axis=0), t, "p_y")
    return [(wide[c * N : c * N + N, :N], wide[c * N : c * N + N, N:]) for c in range(len(pairs))]


SCRATCH = dict(
    node=pltpu.VMEM((3, 3, 2, N, N), f32),
    speed=pltpu.VMEM((3, 2, N, N), f32),
    flux=pltpu.VMEM((3, 2, N, N), f32),
    total=pltpu.VMEM((3, 2, N, N), f32),
    slope=pltpu.VMEM((3, 2, N, N), f32),
    half=pltpu.VMEM((3, 2, 2 * N, N), f32),
    gs=pltpu.VMEM((9, PARTS * THIRD, N), f32),
    gr=pltpu.VMEM((9, PARTS * THIRD, N), f32),
    fs=pltpu.VMEM((6, PARTS * FINE, N), f32),
    fr=pltpu.VMEM((6, PARTS * FINE, N), f32),
    cs=pltpu.VMEM((6, PARTS * COARSE, N), f32),
    cr=pltpu.VMEM((7, PARTS * COARSE, N), f32),
    fh_next=pltpu.VMEM((4, 3, 2, N, N), f32),
    fh_prev=pltpu.VMEM((4, 3, 2, N, N), f32),
    fh_low=pltpu.VMEM((4, 3, 2, N, N), f32),
    fh_high=pltpu.VMEM((4, 3, 2, N, N), f32),
    es=pltpu.VMEM((PARTS * 2 * COARSE, N), f32),
    er=pltpu.VMEM((PARTS * 2 * COARSE, N), f32),
    ch_next=pltpu.VMEM((5, 3, M, N), f32),
    ch_prev=pltpu.VMEM((5, 3, M, N), f32),
    ch_low=pltpu.VMEM((5, 3, M, N), f32),
    ch_high=pltpu.VMEM((5, 3, M, N), f32),
    hand_v=pltpu.VMEM((3, M, N), f32),
    hand_m=pltpu.VMEM((3, M, N), f32),
    send_v=pltpu.VMEM((3, M, N), f32),
    send_m=pltpu.VMEM((3, M, N), f32),
    co=pltpu.VMEM((14, 3, M, N), f32),
    inv_f=pltpu.VMEM((2, N, N), f32),
    inv_c=pltpu.VMEM((M, N), f32),
    g_ssem=pltpu.SemaphoreType.DMA((9,)),
    g_rsem=pltpu.SemaphoreType.DMA((9,)),
    f_ssem=pltpu.SemaphoreType.DMA((6,)),
    f_rsem=pltpu.SemaphoreType.DMA((6,)),
    c_ssem=pltpu.SemaphoreType.DMA((7,)),
    c_rsem=pltpu.SemaphoreType.DMA((7,)),
    h_ssem=pltpu.SemaphoreType.DMA((17, 2)),
    h_rsem=pltpu.SemaphoreType.DMA((17, 2)),
    y_ssem=pltpu.SemaphoreType.DMA((3,)),
    y_rsem=pltpu.SemaphoreType.DMA((3,)),
    in_sem=pltpu.SemaphoreType.DMA((OPERANDS,)),
)
A0, A2, UA0, UA2, G0, G2, C1, C2, CM1, CM2, B1, S1, BM1, SM1 = range(14)


def kernel(*refs):
    nodes, q_out = refs[OPERANDS : OPERANDS + 2]
    staged = refs[OPERANDS + 2 : 2 * OPERANDS + 2]
    init, end, old = staged[:3]
    s = dict(zip(SCRATCH, refs[2 * OPERANDS + 2 :]))
    t = {}
    for places, packed in ((PLACES_32, staged[3]), (PLACES_16, staged[4])):
        for name, (top, shape) in places.items():
            t[name] = packed.at[pl.ds(top, shape[0]), pl.ds(0, shape[1])]
    loads = [
        pltpu.make_async_copy(source, target, s["in_sem"].at[i])
        for i, (source, target) in enumerate(zip(refs[:OPERANDS], staged))
    ]
    co = s["co"]
    row = lax.axis_index("tm")
    me = lax.axis_index("space")
    ahead = lax.rem(me + 1, PARTS)
    behind = lax.rem(me + PARTS - 1, PARTS)
    up = lax.rem(row + 1, ROWS)
    down = lax.rem(row + ROWS - 1, ROWS)

    barrier = pltpu.get_barrier_semaphore()

    place_x, place_z, core = me // 16, lax.rem(me // 2, 8), lax.rem(me, 2)

    def partner(z, x, c):
        return (lax.rem(place_x + x, 4) * 8 + lax.rem(place_z + z, 8)) * 2 + lax.rem(core + c, 2)

    def greet(z, x, c, rows):
        for other in rows:
            pl.semaphore_signal(barrier, inc=1, device_id=(other, partner(z, x, c)), device_id_type=MESH)

    def greet_far(j, carry):
        z = 4 + ((j + 1) // 2) * (1 - 2 * lax.rem(j, 2))
        for x in (2, 1, 3, 0):
            for c in (1, 0):
                greet(z, x, c, (up, down, row))
        return carry

    for i in (0, 1, 4, 3, 2):
        loads[i].start()
    lax.fori_loop(0, 7, greet_far, 0)
    for x in (2, 1, 3, 0):
        for c in (1, 0):
            greet(0, x, c, (up, down, row) if x or c else (up, down))
    for i in (0, 1, 3, 4):
        loads[i].wait()


    def transpose_start(send, recv, depth, ssem, rsem, to_row=None):
        mine = pl.ds(me * depth, depth)

        def post(z, x, c):
            to = partner(z, x, c)
            pltpu.make_async_remote_copy(
                src_ref=send.at[pl.ds(to * depth, depth)],
                dst_ref=recv.at[mine],
                send_sem=ssem,
                recv_sem=rsem,
                device_id=(row if to_row is None else to_row, to),
                device_id_type=MESH,
            ).start()

        def step(j, carry):
            z = 4 + ((j + 1) // 2) * (1 - 2 * lax.rem(j, 2))
            for x in (2, 1, 3, 0):
                for c in (1, 0):
                    post(z, x, c)
            return carry

        lax.fori_loop(0, 7, step, 0)
        for x in (2, 1, 3, 0):
            for c in (1, 0):
                if x or c or to_row is not None:
                    post(0, x, c)
        if to_row is None:
            pltpu.make_async_copy(send.at[mine], recv.at[mine], rsem).start()

    def arrived(ref, sem):
        pltpu.make_async_copy(ref, ref, sem).wait()

    def left(ref, depth, sem, parts=PARTS - 1):
        part = ref.at[pl.ds(0, parts * depth)]
        pltpu.make_async_copy(part, part, sem).wait()

    def third_start(i, to_row):
        transpose_start(s["gs"].at[i], s["gr"].at[i], THIRD, s["g_ssem"].at[i], s["g_rsem"].at[i], to_row)

    def third_wait(i):
        arrived(s["gr"].at[i], s["g_rsem"].at[i])

    def fine_start(i):
        transpose_start(s["fs"].at[i], s["fr"].at[i], FINE, s["f_ssem"].at[i], s["f_rsem"].at[i])

    def coarse_start(i):
        transpose_start(s["cs"].at[i], s["cr"].at[i], COARSE, s["c_ssem"].at[i], s["c_rsem"].at[i])

    def fine_wait(i):
        arrived(s["fr"].at[i], s["f_rsem"].at[i])

    def coarse_wait(i):
        arrived(s["cr"].at[i], s["c_rsem"].at[i])

    def halo_copies(kind, at, sem):
        def copy(out, into, side, to):
            return pltpu.make_async_remote_copy(
                src_ref=s[kind + out].at[at],
                dst_ref=s[kind + into].at[at],
                send_sem=s["h_ssem"].at[sem, side],
                recv_sem=s["h_rsem"].at[sem, side],
                device_id=(row, to),
                device_id_type=MESH,
            )

        return copy("h_next", "h_low", 0, ahead), copy("h_prev", "h_high", 1, behind)

    def fine_halo(m, c):
        return halo_copies("f", (m, c), 3 * m + c)

    def coarse_halo_copies(i):
        return halo_copies("c", i, 12 + i)

    def begin(copies):
        for copy in copies:
            copy.start()

    def landed(copies):
        for copy in copies:
            copy.wait_recv()

    def gone(copies):
        for copy in copies:
            copy.wait_send()

    def hand_copy(src, dst, sem):
        return pltpu.make_async_remote_copy(
            src_ref=src,
            dst_ref=dst,
            send_sem=s["y_ssem"].at[sem],
            recv_sem=s["y_rsem"].at[sem],
            device_id=(up, me),
            device_id_type=MESH,
        )

    start_copy = hand_copy(end.at[0], s["node"].at[0], 0)
    v_copy = hand_copy(s["send_v"], s["hand_v"], 1)
    m_copy = hand_copy(s["send_m"], s["hand_m"], 2)
    is_first = row == 0
    has_next = row < ROWS - 1


    def fine_spread(c, z, plane):
        s["half"][c, z] = both_halves(by_table(plane, t, "f_y"))


    def send_z(m, to_row=None):
        for z in range(2):
            out = table_by(t, "f_x", s["half"][2, z])
            for low in range(2):
                s["gs"][3 * m, pl.ds(2 * low + z, PARTS, stride=THIRD), :] = out[low * M : low * M + M]
        third_start(3 * m, to_row)

    def send_xy(m, to_row=None):
        for low in range(2):
            for c in range(2):
                for z in range(2):
                    s["gs"][3 * m + 1 + low, pl.ds(2 * c + z, PARTS, stride=THIRD), :] = table_by(
                        t, "f_x", s["half"][c, z], slice(low * M, low * M + M)
                    )
            third_start(3 * m + 1 + low, to_row)

    def fine_modes(m):
        third_wait(3 * m)
        for low in range(2):
            third_wait(3 * m + 1 + low)
            places = [(1 + low, 0), (1 + low, 2), (0, 2 * low)]
            planes = [
                stacked(*[s["gr"][3 * m + part, pl.ds(at + z, PARTS, stride=THIRD), :] for z in range(2)])
                for part, at in places
            ]
            kx = jnp.broadcast_to(t["f_kx"][pl.ds(me * 2 + low, 1), :], (N, N))
            for c, out in enumerate(solve_fine(planes, kx, s["inv_f"][low], t)):
                for z in range(2):
                    s["fs"][2 * m + low, pl.ds(c * 2 + z, PARTS, stride=FINE), :] = out[z * M : z * M + M]
            fine_start(2 * m + low)

    def fine_velocity(m):
        for low in range(2):
            fine_wait(2 * m + low)
            for c in range(3):
                modes = stacked(*[s["fr"][2 * m + low, pl.ds(c * 2 + z, PARTS, stride=FINE), :] for z in range(2)])
                wide = by_table(modes, t, "i_y")
                for z in range(2):
                    part = wide[z * M : z * M + M]
                    s["half"][c, z, low * M : low * M + M, :] = part[:, :N]
                    s["half"][c, z, N + low * M : N + low * M + M, :] = part[:, N:]
        for c in range(3):
            for z in range(2):
                s["speed"][c, z] = table_by(t, "i_x", s["half"][c, z])

    node, speed, flux, total = s["node"], s["speed"], s["flux"], s["total"]

    def fine_flux(m):
        for z in range(2):
            parts = cross([speed[c, z] for c in range(3)], [node[m, c, z] for c in range(3)])
            for c in range(3):
                flux[c, z] = parts[c]
        if m < 2:
            for c in range(2):
                fine_shares(m, c)

    def fine_shares(m, c):
        w0, w1 = node[m, c, 0], node[m, c, 1]
        ahead0, ahead1 = second_next(w0, w1)
        back0, back1 = second_prev(w0, w1)
        ahead0, ahead1, back0, back1 = NU * ahead0, NU * ahead1, NU * back0, NU * back1
        if c < 2:
            sign = -1.0 if c == 0 else 1.0
            g0, g1 = sign * flux[1 - c, 0], sign * flux[1 - c, 1]
            d0, d1 = first_next(g0, g1)
            e0, e1 = first_prev(g0, g1)
            ahead0, ahead1, back0, back1 = ahead0 + d0, ahead1 + d1, back0 + e0, back1 + e1
        s["fh_next"][m, c, 0] = ahead0
        s["fh_next"][m, c, 1] = ahead1
        s["fh_prev"][m, c, 0] = back0
        s["fh_prev"][m, c, 1] = back1
        begin(fine_halo(m, c))

    def fine_local(m, c):
        w0, w1 = node[m, c, 0], node[m, c, 1]
        own = [NU * v for v in second_own(w0, w1)]
        if c < 2:
            sign = -1.0 if c == 0 else 1.0
            extra = first_own(sign * flux[1 - c, 0], sign * flux[1 - c, 1])
            own = [own[z] + extra[z] for z in range(2)]
        out = []
        for z in range(2):
            if c == 0:
                curl = first_fine(flux[2, z], 1)
            elif c == 1:
                curl = -first_fine(flux[2, z], 0)
            else:
                curl = first_fine(flux[1, z], 0) - first_fine(flux[0, z], 1)
            out.append(curl + NU * second_fine_xy((w0, w1)[z]) + own[z])
        return out


    def coarse_send(values, i):
        for c, out in enumerate(along_both(values, t, "cf_y")):
            s["cs"][i, pl.ds(c, PARTS, stride=COARSE), :] = out

    def coarse_recv(i):
        return [s["cr"][i, pl.ds(c, PARTS, stride=COARSE), :] for c in range(3)]

    def coarse_modes(i):
        return [z_coarse(x, t) for x in coarse_recv(i)]

    def coarse_velocity(i):
        return along_both(coarse_recv(i), t, "ci_y")

    mine = pl.ds(me, 1)
    wide = lambda name: jnp.broadcast_to(t[name][mine, :], (M, N))

    def coarse_back(hat, i):
        modes = velocity_modes(hat, wide("c_kx"), s["inv_c"][...], t)
        for c in range(3):
            s["cs"][i, pl.ds(c, PARTS, stride=COARSE), :] = z_coarse_back(modes[c], t)

    def coarse_halo(f, w, i):
        g = (-f[1], f[0], None)
        for c in range(3):
            nxt, prv = NU * c_second_next(w[c]), NU * c_second_prev(w[c])
            if g[c] is not None:
                nxt, prv = nxt + c_first_next(g[c]), prv + c_first_prev(g[c])
            s["ch_next"][i, c] = nxt
            s["ch_prev"][i, c] = prv
        begin(coarse_halo_copies(i))

    def coarse_tendency(f, w, i):
        own = [NU * (second_coarse_xy(w[c]) + c_second_own(w[c])) for c in range(3)]
        parts = [
            first_coarse(f[2], False) - c_first_own(f[1]),
            c_first_own(f[0]) - first_coarse(f[2], True),
            first_coarse(f[1], True) - first_coarse(f[0], False),
        ]
        landed(coarse_halo_copies(i))
        return [own[c] + parts[c] + (s["ch_low"][i, c] + s["ch_high"][i, c]) for c in range(3)]

    def keep(i, values):
        for c in range(3):
            co[i, c] = values[c]

    def kept(i):
        return [co[i, c] for c in range(3)]

    def restricted(get):
        return restrict([(get(c, 0), get(c, 1)) for c in range(3)], t)

    for low in range(2):
        at = pl.ds(me * 2 + low, 1)
        kx = jnp.broadcast_to(t["f_kx"][at, :], (N, N))
        mask = t["f_mz"][...] * jnp.broadcast_to(t["f_mx"][at, :], (N, N))
        s["inv_f"][low] = inverse_square(t["f_kk"][...], kx, mask)
    s["inv_c"][...] = inverse_square(t["c_kk"][...], wide("c_kx"), t["c_mz"][...] * wide("c_mx"))

    f0 = lambda c, z: old[0, 0, c, z]
    f1 = lambda c, z: old[0, 1, c, z]
    f2 = lambda c, z: old[0, 2, c, z]

    for c in range(3):
        for z in range(2):
            fine_spread(c, z, jnp.where(has_next, end[0, c, z], init[c, z]))
    pl.semaphore_wait(barrier, 3 * PARTS - 1)

    for m in range(3):
        if m == 0:
            send_z(0, up)
            send_xy(0, up)
        else:
            send_xy(m)
            if m == 1:
                fine_shares(m, 2)
        if m == 1:
            keep(UA0, restricted(lambda c, z: speed[c, z]))
            flux_g0 = cross(kept(UA0), kept(A0))
            coarse_halo(flux_g0, kept(A0), 0)
            keep(G0, coarse_tendency(flux_g0, kept(A0), 0))
        if m == 2:
            keep(A2, restricted(lambda c, z: node[2, c, z]))
        fine_modes(m)
        if m == 0:

            @pl.when(has_next)
            def _():
                start_copy.start()

            @pl.when(is_first)
            def _():
                for c in range(3):
                    for z in range(2):
                        node[0, c, z] = init[c, z]

            @pl.when(jnp.logical_not(is_first))
            def _():
                start_copy.wait_recv()

            fine_shares(0, 2)
            keep(A0, restricted(lambda c, z: node[0, c, z]))
            loads[2].wait()
        fine_velocity(m)
        fine_flux(m)
        if m == 2:
            small = restrict([(flux[c, 0], flux[c, 1]) for c in range(2)], t)
            coarse_halo([*small, None], kept(A2), 4)
            keep(UA2, restricted(lambda c, z: speed[c, z]))
            flux_g2 = cross(kept(UA2), kept(A2))
            coarse_halo(flux_g2, kept(A2), 1)
        weight = (DT / 6.0, DT * 2.0 / 3.0, DT / 6.0)[m]
        if m < 2:
            def advance(c):
                local = fine_local(m, c)
                for z in range(2):
                    total[c, z] = weight * local[z] if m == 0 else total[c, z] + weight * local[z]
                    if m == 0:
                        old_part = (
                            (DT * 5.0 / 24.0 - HALF) * f0(c, z)
                            + (DT / 3.0) * f1(c, z)
                            - (DT / 24.0) * f2(c, z)
                        )
                    else:
                        old_part = (
                            (-DT / 24.0) * f0(c, z)
                            + (DT / 3.0 - HALF) * f1(c, z)
                            + (DT * 5.0 / 24.0) * f2(c, z)
                        )
                    node[m + 1, c, z] = node[m, c, z] + HALF * local[z] + old_part

            def finish(c):
                landed(fine_halo(m, c))
                for z in range(2):
                    share = s["fh_low"][m, c, z] + s["fh_high"][m, c, z]
                    total[c, z] = total[c, z] + weight * share
                    fresh = node[m + 1, c, z] + HALF * share
                    node[m + 1, c, z] = fresh
                    fine_spread(c, z, fresh)

            advance(2)
            finish(2)
            send_z(m + 1)
            for c in range(2):
                advance(c)
            for c in range(2):
                finish(c)
        else:
            for c in range(3):
                local = fine_local(m, c)
                for z in range(2):
                    total[c, z] = total[c, z] + weight * local[z]

    rest = restricted(lambda c, z: total[c, z])
    landed(coarse_halo_copies(4))
    rest = [rest[c] + (DT / 6.0) * (s["ch_low"][4, c] + s["ch_high"][4, c]) for c in range(3)]
    keep(C1, [rest[c] + jnp.where(is_first, co[A0, c], -DT * co[G0, c]) for c in range(3)])
    coarse_send(kept(C1), 0)
    coarse_start(0)
    keep(G2, coarse_tendency(flux_g2, kept(A2), 1))
    keep(
        C2,
        [
            rest[c] - HALF * co[G2, c] + jnp.where(is_first, co[A0, c], -HALF * co[G0, c])
            for c in range(3)
        ],
    )
    coarse_send(kept(C2), 1)
    coarse_start(1)

    coarse_wait(0)
    keep(CM1, coarse_modes(0))
    sx, lx = wide("c_sx"), wide("c_lx")

    def end_shares():
        for c in range(3):
            a, b = speed[c, 0], speed[c, 1]
            s["fh_next"][3, c, 0], s["fh_next"][3, c, 1] = first_next(a, b)
            s["fh_prev"][3, c, 0], s["fh_prev"][3, c, 1] = first_prev(a, b)
            begin(fine_halo(3, c))

    @pl.when(is_first)
    def _():
        keep(BM1, kept(CM1))
        keep(B1, kept(C1))
        keep(S1, kept(C2))
        for c in range(3):
            s["hand_v"][c] = co[A0, c]

    @pl.when(jnp.logical_not(is_first))
    def _():
        coarse_wait(1)
        keep(CM2, coarse_modes(1))
        end_shares()
        v_copy.wait_recv()
        start = [s["hand_v"][c] for c in range(3)]
        coarse_wait(6)
        f = cross(coarse_velocity(6), start)
        coarse_send(f, 2)
        coarse_start(2)
        coarse_halo(f, start, 2)
        early = coarse_tendency(f, start, 2)
        keep(B1, [start[c] + DT * early[c] + co[C1, c] for c in range(3)])
        keep(S1, [start[c] + HALF * early[c] + co[C2, c] for c in range(3)])
        m_copy.wait_recv()
        coarse_wait(2)
        held = [s["hand_m"][c] for c in range(3)]
        early = tendency_modes(coarse_modes(2), held, sx, lx, t)
        keep(BM1, [held[c] + DT * early[c] + co[CM1, c] for c in range(3)])
        keep(SM1, [held[c] + HALF * early[c] + co[CM2, c] for c in range(3)])

    coarse_back(kept(BM1), 3)
    coarse_start(3)

    @pl.when(is_first)
    def _():
        coarse_wait(1)
        keep(SM1, coarse_modes(1))

    coarse_wait(3)
    middle = kept(B1)
    f = cross(coarse_velocity(3), middle)
    coarse_send(f, 4)
    coarse_start(4)
    coarse_halo(f, middle, 3)
    later = coarse_tendency(f, middle, 3)
    for c in range(3):
        s["send_v"][c] = co[S1, c] + HALF * later[c]

    @pl.when(has_next)
    def _():
        v_copy.start()

    coarse_wait(4)
    later = tendency_modes(coarse_modes(4), kept(BM1), sx, lx, t)
    for c in range(3):
        s["send_m"][c] = co[SM1, c] + HALF * later[c]
    final = velocity_modes([s["send_m"][c] for c in range(3)], wide("c_kx"), s["inv_c"][...], t)
    back = [z_coarse_back(x, t) for x in final]

    @pl.when(has_next)
    def _():
        for c in range(3):
            s["cs"][5, pl.ds(c, PARTS, stride=COARSE), :] = back[c]
        transpose_start(s["cs"].at[5], s["cr"].at[6], COARSE, s["c_ssem"].at[6], s["c_rsem"].at[6], up)
        m_copy.start()

    back = back + [z_coarse_back(-turn_back_c(t["c_sz"][...] * x), t) for x in final]
    for c in range(6):
        s["es"][pl.ds(c, PARTS, stride=2 * COARSE), :] = back[c]

    def end_start():
        transpose_start(s["es"], s["er"], 2 * COARSE, s["c_ssem"].at[5], s["c_rsem"].at[5])

    @pl.when(jnp.logical_not(has_next))
    def _():
        end_start()

    @pl.when(is_first)
    def _():
        end_shares()

    zeros = prolong([s["hand_v"][c] - co[A0, c] for c in range(3)], t)
    twos = prolong([s["send_v"][c] - co[A2, c] for c in range(3)], t)
    for c in range(3):
        zero, two = zeros[c], twos[c]
        for z in range(2):
            nodes[0, 0, c, z] = node[0, c, z] + zero[z]
            nodes[0, 1, c, z] = node[1, c, z] + 0.5 * (zero[z] + two[z])
            nodes[0, 2, c, z] = node[2, c, z] + two[z]

    @pl.when(has_next)
    def _():
        end_start()

    slope = s["slope"]
    for c in range(3):
        landed(fine_halo(3, c))
        own = first_own(speed[c, 0], speed[c, 1])
        for z in range(2):
            slope[c, z] = own[z] + (s["fh_low"][3, c, z] + s["fh_high"][3, c, z])

    turned = restricted(lambda c, z: slope[c, z])
    arrived(s["er"], s["c_rsem"].at[5])

    out = along_both([s["er"][pl.ds(c, PARTS, stride=2 * COARSE), :] for c in range(6)], t, "ci_y")
    change = [out[c] - co[UA2, c] for c in range(3)] + [out[3 + c] - turned[c] for c in range(3)]
    put = prolong(change, t)
    for c in range(3):
        for z in range(2):
            speed[c, z] = speed[c, z] + put[c][z]
            slope[c, z] = slope[c, z] + put[3 + c][z]
    for z in range(2):
        gx = [first_fine(speed[c, z], 0) for c in range(3)]
        gy = [first_fine(speed[c, z], 1) for c in range(3)]
        gz = [slope[c, z] for c in range(3)]
        diagonal = gx[0] * gx[0] + gy[1] * gy[1] + gz[2] * gz[2]
        mixed = gx[1] * gy[0] + gx[2] * gz[0] + gy[2] * gz[1]
        q_out[0, z] = -0.5 * diagonal - mixed

    for i in range(9):
        left(s["gs"].at[i], THIRD, s["g_ssem"].at[i], PARTS if i < 3 else PARTS - 1)
    for i in range(6):
        left(s["fs"].at[i], FINE, s["f_ssem"].at[i])
    for i in (0, 1, 3, 4):
        left(s["cs"].at[i], COARSE, s["c_ssem"].at[i])
    left(s["es"], 2 * COARSE, s["c_ssem"].at[5])

    @pl.when(jnp.logical_not(is_first))
    def _():
        left(s["cs"].at[2], COARSE, s["c_ssem"].at[2])
        gone(coarse_halo_copies(2))

    for i in (0, 1, 3):
        for c in range(3):
            gone(fine_halo(i, c))
    for i in (0, 1, 3, 4):
        gone(coarse_halo_copies(i))

    @pl.when(has_next)
    def _():
        left(s["cs"].at[5], COARSE, s["c_ssem"].at[6], PARTS)
        for copy in (start_copy, v_copy, m_copy):
            copy.wait_send()


def body(initial_state, end_states, old_tendencies):
    vmem = pl.BlockSpec(memory_space=pltpu.VMEM)
    operands = [initial_state, end_states, old_tendencies, jnp.asarray(PACKED_32), jnp.asarray(PACKED_16)]
    return pl.pallas_call(
        kernel,
        out_shape=(
            jax.ShapeDtypeStruct((1, 3, 3, 2, N, N), f32),
            jax.ShapeDtypeStruct((1, 2, N, N), f32),
        ),
        in_specs=[pl.BlockSpec(memory_space=pl.ANY)] * len(operands),
        out_specs=(vmem, vmem),
        scratch_shapes=[pltpu.VMEM(x.shape, x.dtype) for x in operands] + list(SCRATCH.values()),
        compiler_params=pltpu.CompilerParams(
            collective_id=0, has_side_effects=True, vmem_limit_bytes=56 * 1024 * 1024
        ),
    )(*operands)


def solution(mesh):
    in_specs = (
        P(None, "space", None, None),
        P("tm", None, "space", None, None),
        P("tm", None, None, "space", None, None),
    )
    out_specs = (P("tm", None, None, "space", None, None), P("tm", "space", None, None))
    return jax.shard_map(body, mesh=mesh, in_specs=in_specs, out_specs=out_specs, check_vma=False)
```

```python
import math

import jax
import jax.numpy as jnp
import numpy as np
from jax import lax
from jax.experimental import pallas as pl
from jax.experimental.pallas import tpu as pltpu
from jax.sharding import PartitionSpec as P

DT = 0.4
HALF = 0.2
NU = 0.1
PARTS = 64
ROWS = 4
N = 128
M = 64
FINE = 6
THIRD = 4
COARSE = 3
f32 = jnp.float32
MESH = pl.DeviceIdType.MESH


def angle_tables(left, right, count):
    angles = (2.0 * math.pi / count) * (np.outer(left, right) % count)
    return np.cos(angles), np.sin(angles)


def restriction_table(count):
    cos_c, sin_c = angle_tables(np.arange(count // 2), np.arange(count // 4), count // 2)
    cos_f, sin_f = angle_tables(np.arange(count), np.arange(count // 4), count)
    weight = np.where(np.arange(count // 4) == 0, 1.0, 2.0)
    return ((cos_c * weight) @ cos_f.T + (sin_c * weight) @ sin_f.T) / count


def twice(block):
    zero = np.zeros_like(block)
    return np.block([[block, zero], [zero, block]])


def wave_symbols(ids, count, spacing):
    theta = 2.0 * math.pi * ids / count
    kappa = theta / spacing
    first = (8.0 * np.sin(theta) - np.sin(2.0 * theta)) / (6.0 * spacing)
    second = (-2.0 * np.cos(2.0 * theta) + 32.0 * np.cos(theta) - 30.0) / (12.0 * spacing**2)
    return kappa, first, second


def signed(ids, count):
    return np.where(ids < count // 2, ids, ids - count)


def build_tables():
    t = {}
    grid = np.arange(N)
    owner = np.concatenate([2 * np.arange(PARTS), 2 * np.arange(PARTS) + 1])
    cos_y, sin_y = angle_tables(grid, np.arange(M), N)
    t["f_y"] = np.hstack([cos_y, -sin_y, -sin_y, -cos_y])
    t["f_x"] = np.hstack(angle_tables(owner, grid, N))
    t["f_z"] = np.hstack(angle_tables(grid, owner, N))
    t["i_z"] = np.hstack(angle_tables(owner, grid, N))
    t["i_x"] = np.hstack(angle_tables(grid, owner, N))
    weight = np.where(np.arange(M) == 0, 1.0, 2.0) / float(N**3)
    wc, ws = (cos_y * weight).T, (sin_y * weight).T
    t["i_y"] = np.hstack([np.vstack([wc, -ws]), np.vstack([-ws, -wc])])
    half = np.arange(M // 2)
    cos_y, sin_y = angle_tables(np.arange(M), half, M)
    t["cf_y"] = np.hstack([twice(np.hstack([cos_y, -sin_y])), twice(np.hstack([-sin_y, -cos_y]))])
    t["c_x"] = np.hstack(angle_tables(np.arange(M), np.arange(M), M))
    weight = np.where(half == 0, 1.0, 2.0) / float(M * M * N)
    wc, ws = (cos_y * weight).T, (sin_y * weight).T
    t["ci_y"] = np.hstack([twice(np.vstack([wc, -ws])), twice(np.vstack([-ws, -wc]))])
    table = restriction_table(N)
    t["r_x"] = table
    t["r_y"] = twice(table.T)
    t["p_x"] = 4.0 * table.T
    t["p_y"] = twice(table)
    kx, _, _ = wave_symbols(signed(grid, N), N, 1.0)
    ky = np.tile(kx[:M], 2)[None, :]
    ones = np.ones((1, N))
    t["f_kx"] = kx[:, None] * ones
    t["f_mx"] = (grid != M)[:, None] * ones
    t["f_ky"] = np.repeat(ky, 8, axis=0)
    t["f_kz"] = kx[:, None] * ones
    t["f_kk"] = ky**2 + kx[:, None] ** 2
    t["f_mz"] = t["f_mx"]
    ckx, sx, lx = wave_symbols(signed(np.arange(M), M), M, 2.0)
    t["c_kx"] = ckx[:, None] * ones
    t["c_mx"] = (np.arange(M) != M // 2)[:, None] * ones
    t["c_sx"] = sx[:, None] * ones
    t["c_lx"] = lx[:, None] * ones
    lane = lambda v: np.tile(v[: M // 2], 4)[None, :]
    cky, sy, ly = lane(ckx), lane(sx), lane(lx)
    zid = np.hstack([np.repeat(np.arange(M)[:, None], M, 1), np.repeat(np.arange(M)[:, None] + M, M, 1)])
    ckz, sz, lz = wave_symbols(signed(zid, N), N, 1.0)
    t["c_ky"] = np.repeat(cky, 8, axis=0)
    t["c_sy"] = np.repeat(sy, 8, axis=0)
    t["c_kz"] = ckz
    t["c_sz"] = sz
    t["c_kk"] = cky**2 + ckz**2
    t["c_mz"] = (zid != M) * 1.0
    t["c_ll"] = ly + lz
    turn = 2.0 * math.pi * np.arange(M)[:, None] / N
    first = (np.arange(N) < M)[None, :]
    t["tw_c"] = np.where(first, 1.0, np.cos(turn))
    t["tw_s"] = np.where(first, 0.0, np.sin(turn))
    made = {}
    for name, value in t.items():
        value = np.asarray(value, np.float32)
        if name in SPLIT:
            high = value.astype(jnp.bfloat16)
            made[name + "_h"] = high
            if name in RIGHT:
                made[name + "_h"] = np.vstack([high, high])
            if name in LEFT:
                made[name + "_h"] = np.hstack([high, high])
            low = (value - high.astype(np.float32)).astype(jnp.bfloat16)
            made[name + "_l"] = np.hstack([low, np.zeros_like(low)]) if name in LEFT else low
        else:
            made[name] = value
    return made


RIGHT = ("f_y", "i_y", "cf_y", "ci_y", "p_y")
LEFT = ("c_x", "r_x", "p_x")
SPLIT = ("r_x", "r_y", "p_x", "p_y", "f_x", "f_y", "f_z", "i_x", "i_y", "i_z", "cf_y", "c_x", "ci_y")
TABLES = build_tables()


def pack(kind, width):
    places, blocks, top = {}, [], 0
    for name in sorted(TABLES):
        value = TABLES[name]
        if value.dtype == kind:
            block = np.zeros((value.shape[0], width), kind)
            block[:, : value.shape[1]] = value
            places[name] = (top, value.shape)
            blocks.append(block)
            top += value.shape[0]
    return places, np.concatenate(blocks)


PLACES_32, PACKED_32 = pack(np.float32, N)
PLACES_16, PACKED_16 = pack(jnp.bfloat16, 2 * N)
OPERANDS = 5


def dot(a, b):
    return jnp.dot(a, b, preferred_element_type=f32)


def split(x):
    high = x.astype(jnp.bfloat16)
    return high, (x - high.astype(f32)).astype(jnp.bfloat16)


def by_table(x, t, name):
    high, low = split(x)
    table = t[name + "_h"][...]
    rest = dot(high, t[name + "_l"][...])
    if name in RIGHT:
        return dot(jnp.concatenate([high, low], axis=1), table) + rest
    return dot(high, table) + (dot(low, table) + rest)


def table_by(t, name, x, rows=slice(None)):
    high, low = split(x)
    table = t[name + "_h"][rows, :]
    if name in LEFT:
        both = jnp.concatenate([high, low], axis=0)
        return dot(table, both) + dot(t[name + "_l"][...], both)
    return dot(table, high) + (dot(table, low) + dot(t[name + "_l"][rows, :], high))


def roll(x, shift, axis):
    return pltpu.roll(x, shift % x.shape[axis], axis)


def lanes(shape):
    return lax.broadcasted_iota(jnp.int32, shape, 1)


def stacked(a, b):
    return jnp.concatenate([a, b], axis=0)


def both_halves(wide):
    return stacked(wide[:, :N], wide[:, N:])


def turn_back(x):
    swapped = roll(x, M, 1)
    return jnp.where(lanes(x.shape) < M, swapped, -swapped)


def turn_back_c(x):
    is_real = (lanes(x.shape) % M) < M // 2
    return jnp.where(is_real, roll(x, -M // 2, 1), -roll(x, M // 2, 1))


def butterfly(x):
    return jnp.where(lanes(x.shape) < M, x, -x) + roll(x, M, 1)


def cross(a, b):
    return (
        a[1] * b[2] - a[2] * b[1],
        a[2] * b[0] - a[0] * b[2],
        a[0] * b[1] - a[1] * b[0],
    )


def first_fine(f, axis):
    return (roll(f, 2, axis) - roll(f, -2, axis) + 8.0 * (roll(f, -1, axis) - roll(f, 1, axis))) * (
        1.0 / 12.0
    )


def second_fine_xy(f):
    near = (roll(f, 1, 0) + roll(f, -1, 0)) + (roll(f, 1, 1) + roll(f, -1, 1))
    far = (roll(f, 2, 0) + roll(f, -2, 0)) + (roll(f, 2, 1) + roll(f, -2, 1))
    return (16.0 * near - far - 60.0 * f) * (1.0 / 12.0)


def roll_half(f, shift):
    place = lanes(f.shape) % M
    keep = place >= shift if shift > 0 else place < M + shift
    return jnp.where(keep, roll(f, shift, 1), roll(f, shift - M if shift > 0 else shift + M, 1))


def first_coarse(f, along_x):
    go = (lambda s: roll(f, s, 0)) if along_x else (lambda s: roll_half(f, s))
    return (go(2) - go(-2) + 8.0 * (go(-1) - go(1))) * (1.0 / 24.0)


def second_coarse_xy(f):
    near = (roll(f, 1, 0) + roll(f, -1, 0)) + (roll_half(f, 1) + roll_half(f, -1))
    far = (roll(f, 2, 0) + roll(f, -2, 0)) + (roll_half(f, 2) + roll_half(f, -2))
    return (16.0 * near - far - 60.0 * f) * (1.0 / 48.0)


def first_next(a, b):
    return (a - 8.0 * b) * (1.0 / 12.0), b * (1.0 / 12.0)


def first_prev(a, b):
    return a * (-1.0 / 12.0), (8.0 * a - b) * (1.0 / 12.0)


def first_own(a, b):
    return b * (8.0 / 12.0), a * (-8.0 / 12.0)


def second_next(a, b):
    return (16.0 * b - a) * (1.0 / 12.0), b * (-1.0 / 12.0)


def second_prev(a, b):
    return a * (-1.0 / 12.0), (16.0 * a - b) * (1.0 / 12.0)


def second_own(a, b):
    return (16.0 * b - 30.0 * a) * (1.0 / 12.0), (16.0 * a - 30.0 * b) * (1.0 / 12.0)


def lane_pair(f, low, high):
    is_low = lanes(f.shape) < M
    own = jnp.where(is_low, low[0], high[0]).astype(f32)
    other = jnp.where(is_low, low[1], high[1]).astype(f32)
    return f * own + roll(f, M, 1) * other


T12 = 1.0 / 12.0


def c_first_next(f):
    return lane_pair(f, (T12, -8 * T12), (T12, 0.0))


def c_first_prev(f):
    return lane_pair(f, (-T12, 0.0), (-T12, 8 * T12))


def c_first_own(f):
    return lane_pair(f, (0.0, 8 * T12), (0.0, -8 * T12))


def c_second_next(f):
    return lane_pair(f, (-T12, 16 * T12), (-T12, 0.0))


def c_second_prev(f):
    return lane_pair(f, (-T12, 0.0), (-T12, 16 * T12))


def c_second_own(f):
    return lane_pair(f, (-30 * T12, 16 * T12), (-30 * T12, 16 * T12))


def along_both(fields, t, name):
    wide = by_table(jnp.concatenate(fields, axis=0), t, name)
    return [table_by(t, "c_x", both_halves(wide[c * M : c * M + M])) for c in range(len(fields))]


def inverse_square(kk, kx, mask):
    squared = kk + kx * kx
    live = squared > 0.0
    return jnp.where(live, mask / jnp.where(live, squared, 1.0), 0.0)


def solve_fine(planes, kx, inverse, t):
    hat = [table_by(t, "f_z", stacked(p, turn_back(p))) for p in planes]
    kz = t["f_kz"][...]
    ky = jnp.broadcast_to(t["f_ky"][0:1, :], kz.shape)
    out = []
    for r in cross((kx, ky, kz), hat):
        r = r * inverse
        out.append(table_by(t, "i_z", stacked(-turn_back(r), -r)))
    return out


def z_coarse(x, t):
    d = table_by(t, "c_x", stacked(x, turn_back_c(x)))
    return butterfly(t["tw_c"][...] * d + t["tw_s"][...] * turn_back_c(d))


def z_coarse_back(a, t):
    b = butterfly(a)
    b = t["tw_c"][...] * b - t["tw_s"][...] * turn_back_c(b)
    return table_by(t, "c_x", stacked(b, -turn_back_c(b)))


def velocity_modes(hat, kx, inverse, t):
    kz = t["c_kz"][...]
    ky = jnp.broadcast_to(t["c_ky"][0:1, :], kz.shape)
    return [-turn_back_c(r * inverse) for r in cross((kx, ky, kz), hat)]


def tendency_modes(flux, w, sx, lx, t):
    sz = t["c_sz"][...]
    sy = jnp.broadcast_to(t["c_sy"][0:1, :], sz.shape)
    spread = NU * (t["c_ll"][...] + lx)
    return [-turn_back_c(r) + spread * w[i] for i, r in enumerate(cross((sx, sy, sz), flux))]


def restrict(pairs, t):
    wide = by_table(jnp.concatenate([jnp.concatenate(pair, axis=1) for pair in pairs], axis=0), t, "r_y")
    return [table_by(t, "r_x", wide[c * N : c * N + N]) for c in range(len(pairs))]


def prolong(pairs, t):
    wide = by_table(jnp.concatenate([table_by(t, "p_x", pair) for pair in pairs], axis=0), t, "p_y")
    return [(wide[c * N : c * N + N, :N], wide[c * N : c * N + N, N:]) for c in range(len(pairs))]


SCRATCH = dict(
    node=pltpu.VMEM((3, 3, 2, N, N), f32),
    speed=pltpu.VMEM((3, 2, N, N), f32),
    flux=pltpu.VMEM((3, 2, N, N), f32),
    total=pltpu.VMEM((3, 2, N, N), f32),
    slope=pltpu.VMEM((3, 2, N, N), f32),
    half=pltpu.VMEM((3, 2, 2 * N, N), f32),
    gs=pltpu.VMEM((9, PARTS * THIRD, N), f32),
    gr=pltpu.VMEM((9, PARTS * THIRD, N), f32),
    fs=pltpu.VMEM((6, PARTS * FINE, N), f32),
    fr=pltpu.VMEM((6, PARTS * FINE, N), f32),
    cs=pltpu.VMEM((6, PARTS * COARSE, N), f32),
    cr=pltpu.VMEM((7, PARTS * COARSE, N), f32),
    fh_next=pltpu.VMEM((4, 3, 2, N, N), f32),
    fh_prev=pltpu.VMEM((4, 3, 2, N, N), f32),
    fh_low=pltpu.VMEM((4, 3, 2, N, N), f32),
    fh_high=pltpu.VMEM((4, 3, 2, N, N), f32),
    es=pltpu.VMEM((PARTS * 2 * COARSE, N), f32),
    er=pltpu.VMEM((PARTS * 2 * COARSE, N), f32),
    ch_next=pltpu.VMEM((5, 3, M, N), f32),
    ch_prev=pltpu.VMEM((5, 3, M, N), f32),
    ch_low=pltpu.VMEM((5, 3, M, N), f32),
    ch_high=pltpu.VMEM((5, 3, M, N), f32),
    hand_v=pltpu.VMEM((3, M, N), f32),
    hand_m=pltpu.VMEM((3, M, N), f32),
    send_v=pltpu.VMEM((3, M, N), f32),
    send_m=pltpu.VMEM((3, M, N), f32),
    co=pltpu.VMEM((14, 3, M, N), f32),
    inv_f=pltpu.VMEM((2, N, N), f32),
    inv_c=pltpu.VMEM((M, N), f32),
    g_ssem=pltpu.SemaphoreType.DMA((9,)),
    g_rsem=pltpu.SemaphoreType.DMA((9,)),
    f_ssem=pltpu.SemaphoreType.DMA((6,)),
    f_rsem=pltpu.SemaphoreType.DMA((6,)),
    c_ssem=pltpu.SemaphoreType.DMA((7,)),
    c_rsem=pltpu.SemaphoreType.DMA((7,)),
    h_ssem=pltpu.SemaphoreType.DMA((17, 2)),
    h_rsem=pltpu.SemaphoreType.DMA((17, 2)),
    y_ssem=pltpu.SemaphoreType.DMA((3,)),
    y_rsem=pltpu.SemaphoreType.DMA((3,)),
    in_sem=pltpu.SemaphoreType.DMA((OPERANDS,)),
)
A0, A2, UA0, UA2, G0, G2, C1, C2, CM1, CM2, B1, S1, BM1, SM1 = range(14)


def kernel(*refs):
    nodes, q_out = refs[OPERANDS : OPERANDS + 2]
    staged = refs[OPERANDS + 2 : 2 * OPERANDS + 2]
    init, end, old = staged[:3]
    s = dict(zip(SCRATCH, refs[2 * OPERANDS + 2 :]))
    t = {}
    for places, packed in ((PLACES_32, staged[3]), (PLACES_16, staged[4])):
        for name, (top, shape) in places.items():
            t[name] = packed.at[pl.ds(top, shape[0]), pl.ds(0, shape[1])]
    loads = [
        pltpu.make_async_copy(source, target, s["in_sem"].at[i])
        for i, (source, target) in enumerate(zip(refs[:OPERANDS], staged))
    ]
    co = s["co"]
    row = lax.axis_index("tm")
    me = lax.axis_index("space")
    ahead = lax.rem(me + 1, PARTS)
    behind = lax.rem(me + PARTS - 1, PARTS)
    up = lax.rem(row + 1, ROWS)
    down = lax.rem(row + ROWS - 1, ROWS)

    barrier = pltpu.get_barrier_semaphore()

    place_x, place_z, core = me // 16, lax.rem(me // 2, 8), lax.rem(me, 2)

    def partner(z, x, c):
        return (lax.rem(place_x + x, 4) * 8 + lax.rem(place_z + z, 8)) * 2 + lax.rem(core + c, 2)

    def greet(z, x, c, rows):
        for other in rows:
            pl.semaphore_signal(barrier, inc=1, device_id=(other, partner(z, x, c)), device_id_type=MESH)

    def greet_far(j, carry):
        z = 4 + ((j + 1) // 2) * (1 - 2 * lax.rem(j, 2))
        for x in (2, 1, 3, 0):
            for c in (1, 0):
                greet(z, x, c, (down, row))
        return carry

    for i in (0, 1, 4, 3, 2):
        loads[i].start()
    lax.fori_loop(0, 7, greet_far, 0)
    for x in (2, 1, 3, 0):
        for c in (1, 0):
            greet(0, x, c, (down, row) if x or c else (down,))
    for i in (0, 1, 3, 4):
        loads[i].wait()


    def transpose_start(send, recv, depth, ssem, rsem, to_row=None):
        mine = pl.ds(me * depth, depth)

        def post(z, x, c):
            to = partner(z, x, c)
            pltpu.make_async_remote_copy(
                src_ref=send.at[pl.ds(to * depth, depth)],
                dst_ref=recv.at[mine],
                send_sem=ssem,
                recv_sem=rsem,
                device_id=(row if to_row is None else to_row, to),
                device_id_type=MESH,
            ).start()

        def step(j, carry):
            z = 4 + ((j + 1) // 2) * (1 - 2 * lax.rem(j, 2))
            for x in (2, 1, 3, 0):
                for c in (1, 0):
                    post(z, x, c)
            return carry

        lax.fori_loop(0, 7, step, 0)
        for x in (2, 1, 3, 0):
            for c in (1, 0):
                if x or c or to_row is not None:
                    post(0, x, c)
        if to_row is None:
            pltpu.make_async_copy(send.at[mine], recv.at[mine], rsem).start()

    def arrived(ref, sem):
        pltpu.make_async_copy(ref, ref, sem).wait()

    def left(ref, depth, sem, parts=PARTS - 1):
        part = ref.at[pl.ds(0, parts * depth)]
        pltpu.make_async_copy(part, part, sem).wait()

    def third_start(i, to_row):
        transpose_start(s["gs"].at[i], s["gr"].at[i], THIRD, s["g_ssem"].at[i], s["g_rsem"].at[i], to_row)

    def third_wait(i):
        arrived(s["gr"].at[i], s["g_rsem"].at[i])

    def fine_start(i):
        transpose_start(s["fs"].at[i], s["fr"].at[i], FINE, s["f_ssem"].at[i], s["f_rsem"].at[i])

    def coarse_start(i):
        transpose_start(s["cs"].at[i], s["cr"].at[i], COARSE, s["c_ssem"].at[i], s["c_rsem"].at[i])

    def fine_wait(i):
        arrived(s["fr"].at[i], s["f_rsem"].at[i])

    def coarse_wait(i):
        arrived(s["cr"].at[i], s["c_rsem"].at[i])

    def halo_copies(kind, at, sem):
        def copy(out, into, side, to):
            return pltpu.make_async_remote_copy(
                src_ref=s[kind + out].at[at],
                dst_ref=s[kind + into].at[at],
                send_sem=s["h_ssem"].at[sem, side],
                recv_sem=s["h_rsem"].at[sem, side],
                device_id=(row, to),
                device_id_type=MESH,
            )

        return copy("h_next", "h_low", 0, ahead), copy("h_prev", "h_high", 1, behind)

    def fine_halo(m, c):
        return halo_copies("f", (m, c), 3 * m + c)

    def coarse_halo_copies(i):
        return halo_copies("c", i, 12 + i)

    def begin(copies):
        for copy in copies:
            copy.start()

    def landed(copies):
        for copy in copies:
            copy.wait_recv()

    def gone(copies):
        for copy in copies:
            copy.wait_send()

    def hand_copy(src, dst, sem):
        return pltpu.make_async_remote_copy(
            src_ref=src,
            dst_ref=dst,
            send_sem=s["y_ssem"].at[sem],
            recv_sem=s["y_rsem"].at[sem],
            device_id=(up, me),
            device_id_type=MESH,
        )

    start_copy = hand_copy(end.at[0], s["node"].at[0], 0)
    v_copy = hand_copy(s["send_v"], s["hand_v"], 1)
    m_copy = hand_copy(s["send_m"], s["hand_m"], 2)
    is_first = row == 0
    has_next = row < ROWS - 1


    def fine_spread(c, z, plane):
        s["half"][c, z] = both_halves(by_table(plane, t, "f_y"))


    def send_z(m, to_row=None):
        for z in range(2):
            out = table_by(t, "f_x", s["half"][2, z])
            for low in range(2):
                s["gs"][3 * m, pl.ds(2 * low + z, PARTS, stride=THIRD), :] = out[low * M : low * M + M]
        third_start(3 * m, to_row)

    def send_xy(m, to_row=None):
        for low in range(2):
            for c in range(2):
                for z in range(2):
                    s["gs"][3 * m + 1 + low, pl.ds(2 * c + z, PARTS, stride=THIRD), :] = table_by(
                        t, "f_x", s["half"][c, z], slice(low * M, low * M + M)
                    )
            third_start(3 * m + 1 + low, to_row)

    def fine_modes(m):
        third_wait(3 * m)
        for low in range(2):
            third_wait(3 * m + 1 + low)
            places = [(1 + low, 0), (1 + low, 2), (0, 2 * low)]
            planes = [
                stacked(*[s["gr"][3 * m + part, pl.ds(at + z, PARTS, stride=THIRD), :] for z in range(2)])
                for part, at in places
            ]
            kx = jnp.broadcast_to(t["f_kx"][pl.ds(me * 2 + low, 1), :], (N, N))
            for c, out in enumerate(solve_fine(planes, kx, s["inv_f"][low], t)):
                for z in range(2):
                    s["fs"][2 * m + low, pl.ds(c * 2 + z, PARTS, stride=FINE), :] = out[z * M : z * M + M]
            fine_start(2 * m + low)

    def fine_velocity(m):
        for low in range(2):
            fine_wait(2 * m + low)
            for c in range(3):
                modes = stacked(*[s["fr"][2 * m + low, pl.ds(c * 2 + z, PARTS, stride=FINE), :] for z in range(2)])
                wide = by_table(modes, t, "i_y")
                for z in range(2):
                    part = wide[z * M : z * M + M]
                    s["half"][c, z, low * M : low * M + M, :] = part[:, :N]
                    s["half"][c, z, N + low * M : N + low * M + M, :] = part[:, N:]
        for c in range(3):
            for z in range(2):
                s["speed"][c, z] = table_by(t, "i_x", s["half"][c, z])

    node, speed, flux, total = s["node"], s["speed"], s["flux"], s["total"]

    def fine_flux(m):
        for z in range(2):
            parts = cross([speed[c, z] for c in range(3)], [node[m, c, z] for c in range(3)])
            for c in range(3):
                flux[c, z] = parts[c]
        if m < 2:
            for c in range(2):
                fine_shares(m, c)

    def fine_shares(m, c):
        w0, w1 = node[m, c, 0], node[m, c, 1]
        ahead0, ahead1 = second_next(w0, w1)
        back0, back1 = second_prev(w0, w1)
        ahead0, ahead1, back0, back1 = NU * ahead0, NU * ahead1, NU * back0, NU * back1
        if c < 2:
            sign = -1.0 if c == 0 else 1.0
            g0, g1 = sign * flux[1 - c, 0], sign * flux[1 - c, 1]
            d0, d1 = first_next(g0, g1)
            e0, e1 = first_prev(g0, g1)
            ahead0, ahead1, back0, back1 = ahead0 + d0, ahead1 + d1, back0 + e0, back1 + e1
        s["fh_next"][m, c, 0] = ahead0
        s["fh_next"][m, c, 1] = ahead1
        s["fh_prev"][m, c, 0] = back0
        s["fh_prev"][m, c, 1] = back1
        begin(fine_halo(m, c))

    def fine_local(m, c):
        w0, w1 = node[m, c, 0], node[m, c, 1]
        own = [NU * v for v in second_own(w0, w1)]
        if c < 2:
            sign = -1.0 if c == 0 else 1.0
            extra = first_own(sign * flux[1 - c, 0], sign * flux[1 - c, 1])
            own = [own[z] + extra[z] for z in range(2)]
        out = []
        for z in range(2):
            if c == 0:
                curl = first_fine(flux[2, z], 1)
            elif c == 1:
                curl = -first_fine(flux[2, z], 0)
            else:
                curl = first_fine(flux[1, z], 0) - first_fine(flux[0, z], 1)
            out.append(curl + NU * second_fine_xy((w0, w1)[z]) + own[z])
        return out


    def coarse_send(values, i):
        for c, out in enumerate(along_both(values, t, "cf_y")):
            s["cs"][i, pl.ds(c, PARTS, stride=COARSE), :] = out

    def coarse_recv(i):
        return [s["cr"][i, pl.ds(c, PARTS, stride=COARSE), :] for c in range(3)]

    def coarse_modes(i):
        return [z_coarse(x, t) for x in coarse_recv(i)]

    def coarse_velocity(i):
        return along_both(coarse_recv(i), t, "ci_y")

    mine = pl.ds(me, 1)
    wide = lambda name: jnp.broadcast_to(t[name][mine, :], (M, N))

    def coarse_back(hat, i):
        modes = velocity_modes(hat, wide("c_kx"), s["inv_c"][...], t)
        for c in range(3):
            s["cs"][i, pl.ds(c, PARTS, stride=COARSE), :] = z_coarse_back(modes[c], t)

    def coarse_halo(f, w, i):
        g = (-f[1], f[0], None)
        for c in range(3):
            nxt, prv = NU * c_second_next(w[c]), NU * c_second_prev(w[c])
            if g[c] is not None:
                nxt, prv = nxt + c_first_next(g[c]), prv + c_first_prev(g[c])
            s["ch_next"][i, c] = nxt
            s["ch_prev"][i, c] = prv
        begin(coarse_halo_copies(i))

    def coarse_tendency(f, w, i):
        own = [NU * (second_coarse_xy(w[c]) + c_second_own(w[c])) for c in range(3)]
        parts = [
            first_coarse(f[2], False) - c_first_own(f[1]),
            c_first_own(f[0]) - first_coarse(f[2], True),
            first_coarse(f[1], True) - first_coarse(f[0], False),
        ]
        landed(coarse_halo_copies(i))
        return [own[c] + parts[c] + (s["ch_low"][i, c] + s["ch_high"][i, c]) for c in range(3)]

    def keep(i, values):
        for c in range(3):
            co[i, c] = values[c]

    def kept(i):
        return [co[i, c] for c in range(3)]

    def restricted(get):
        return restrict([(get(c, 0), get(c, 1)) for c in range(3)], t)

    for low in range(2):
        at = pl.ds(me * 2 + low, 1)
        kx = jnp.broadcast_to(t["f_kx"][at, :], (N, N))
        mask = t["f_mz"][...] * jnp.broadcast_to(t["f_mx"][at, :], (N, N))
        s["inv_f"][low] = inverse_square(t["f_kk"][...], kx, mask)
    s["inv_c"][...] = inverse_square(t["c_kk"][...], wide("c_kx"), t["c_mz"][...] * wide("c_mx"))

    f0 = lambda c, z: old[0, 0, c, z]
    f1 = lambda c, z: old[0, 1, c, z]
    f2 = lambda c, z: old[0, 2, c, z]

    for c in range(3):
        for z in range(2):
            fine_spread(c, z, jnp.where(has_next, end[0, c, z], init[c, z]))
    pl.semaphore_wait(barrier, 2 * PARTS - 1)

    for m in range(3):
        if m == 0:
            send_z(0, up)
            send_xy(0, up)
        else:
            send_xy(m)
            if m == 1:
                fine_shares(m, 2)
        if m == 1:
            keep(UA0, restricted(lambda c, z: speed[c, z]))
            flux_g0 = cross(kept(UA0), kept(A0))
            coarse_halo(flux_g0, kept(A0), 0)
            keep(G0, coarse_tendency(flux_g0, kept(A0), 0))
        if m == 2:
            keep(A2, restricted(lambda c, z: node[2, c, z]))
        fine_modes(m)
        if m == 0:

            @pl.when(has_next)
            def _():
                start_copy.start()

            @pl.when(is_first)
            def _():
                for c in range(3):
                    for z in range(2):
                        node[0, c, z] = init[c, z]

            @pl.when(jnp.logical_not(is_first))
            def _():
                start_copy.wait_recv()

            fine_shares(0, 2)
            keep(A0, restricted(lambda c, z: node[0, c, z]))
            loads[2].wait()
        fine_velocity(m)
        fine_flux(m)
        if m == 2:
            small = restrict([(flux[c, 0], flux[c, 1]) for c in range(2)], t)
            coarse_halo([*small, None], kept(A2), 4)
            keep(UA2, restricted(lambda c, z: speed[c, z]))
            flux_g2 = cross(kept(UA2), kept(A2))
            coarse_halo(flux_g2, kept(A2), 1)
        weight = (DT / 6.0, DT * 2.0 / 3.0, DT / 6.0)[m]
        if m < 2:
            def advance(c):
                local = fine_local(m, c)
                for z in range(2):
                    total[c, z] = weight * local[z] if m == 0 else total[c, z] + weight * local[z]
                    if m == 0:
                        old_part = (
                            (DT * 5.0 / 24.0 - HALF) * f0(c, z)
                            + (DT / 3.0) * f1(c, z)
                            - (DT / 24.0) * f2(c, z)
                        )
                    else:
                        old_part = (
                            (-DT / 24.0) * f0(c, z)
                            + (DT / 3.0 - HALF) * f1(c, z)
                            + (DT * 5.0 / 24.0) * f2(c, z)
                        )
                    node[m + 1, c, z] = node[m, c, z] + HALF * local[z] + old_part

            def finish(c):
                landed(fine_halo(m, c))
                for z in range(2):
                    share = s["fh_low"][m, c, z] + s["fh_high"][m, c, z]
                    total[c, z] = total[c, z] + weight * share
                    fresh = node[m + 1, c, z] + HALF * share
                    node[m + 1, c, z] = fresh
                    fine_spread(c, z, fresh)

            advance(2)
            finish(2)
            send_z(m + 1)
            for c in range(2):
                advance(c)
            for c in range(2):
                finish(c)
        else:
            for c in range(3):
                local = fine_local(m, c)
                for z in range(2):
                    total[c, z] = total[c, z] + weight * local[z]

    rest = restricted(lambda c, z: total[c, z])
    landed(coarse_halo_copies(4))
    rest = [rest[c] + (DT / 6.0) * (s["ch_low"][4, c] + s["ch_high"][4, c]) for c in range(3)]
    keep(C1, [rest[c] + jnp.where(is_first, co[A0, c], -DT * co[G0, c]) for c in range(3)])
    coarse_send(kept(C1), 0)
    coarse_start(0)
    keep(G2, coarse_tendency(flux_g2, kept(A2), 1))
    keep(
        C2,
        [
            rest[c] - HALF * co[G2, c] + jnp.where(is_first, co[A0, c], -HALF * co[G0, c])
            for c in range(3)
        ],
    )
    coarse_send(kept(C2), 1)
    coarse_start(1)

    coarse_wait(0)
    keep(CM1, coarse_modes(0))
    sx, lx = wide("c_sx"), wide("c_lx")

    def end_shares():
        for c in range(3):
            a, b = speed[c, 0], speed[c, 1]
            s["fh_next"][3, c, 0], s["fh_next"][3, c, 1] = first_next(a, b)
            s["fh_prev"][3, c, 0], s["fh_prev"][3, c, 1] = first_prev(a, b)
            begin(fine_halo(3, c))

    @pl.when(is_first)
    def _():
        keep(BM1, kept(CM1))
        keep(B1, kept(C1))
        keep(S1, kept(C2))
        for c in range(3):
            s["hand_v"][c] = co[A0, c]

    @pl.when(jnp.logical_not(is_first))
    def _():
        coarse_wait(1)
        keep(CM2, coarse_modes(1))
        end_shares()
        v_copy.wait_recv()
        start = [s["hand_v"][c] for c in range(3)]
        coarse_wait(6)
        f = cross(coarse_velocity(6), start)
        coarse_send(f, 2)
        coarse_start(2)
        coarse_halo(f, start, 2)
        early = coarse_tendency(f, start, 2)
        keep(B1, [start[c] + DT * early[c] + co[C1, c] for c in range(3)])
        keep(S1, [start[c] + HALF * early[c] + co[C2, c] for c in range(3)])
        m_copy.wait_recv()
        coarse_wait(2)
        held = [s["hand_m"][c] for c in range(3)]
        early = tendency_modes(coarse_modes(2), held, sx, lx, t)
        keep(BM1, [held[c] + DT * early[c] + co[CM1, c] for c in range(3)])
        keep(SM1, [held[c] + HALF * early[c] + co[CM2, c] for c in range(3)])

    coarse_back(kept(BM1), 3)
    coarse_start(3)

    @pl.when(is_first)
    def _():
        coarse_wait(1)
        keep(SM1, coarse_modes(1))

    coarse_wait(3)
    middle = kept(B1)
    f = cross(coarse_velocity(3), middle)
    coarse_send(f, 4)
    coarse_start(4)
    coarse_halo(f, middle, 3)
    later = coarse_tendency(f, middle, 3)
    for c in range(3):
        s["send_v"][c] = co[S1, c] + HALF * later[c]

    @pl.when(has_next)
    def _():
        v_copy.start()

    coarse_wait(4)
    later = tendency_modes(coarse_modes(4), kept(BM1), sx, lx, t)
    for c in range(3):
        s["send_m"][c] = co[SM1, c] + HALF * later[c]
    final = velocity_modes([s["send_m"][c] for c in range(3)], wide("c_kx"), s["inv_c"][...], t)
    back = [z_coarse_back(x, t) for x in final]

    @pl.when(has_next)
    def _():
        for c in range(3):
            s["cs"][5, pl.ds(c, PARTS, stride=COARSE), :] = back[c]
        transpose_start(s["cs"].at[5], s["cr"].at[6], COARSE, s["c_ssem"].at[6], s["c_rsem"].at[6], up)
        m_copy.start()

    back = back + [z_coarse_back(-turn_back_c(t["c_sz"][...] * x), t) for x in final]
    for c in range(6):
        s["es"][pl.ds(c, PARTS, stride=2 * COARSE), :] = back[c]

    def end_start():
        transpose_start(s["es"], s["er"], 2 * COARSE, s["c_ssem"].at[5], s["c_rsem"].at[5])

    @pl.when(jnp.logical_not(has_next))
    def _():
        end_start()

    @pl.when(is_first)
    def _():
        end_shares()

    zeros = prolong([s["hand_v"][c] - co[A0, c] for c in range(3)], t)
    twos = prolong([s["send_v"][c] - co[A2, c] for c in range(3)], t)
    for c in range(3):
        zero, two = zeros[c], twos[c]
        for z in range(2):
            nodes[0, 0, c, z] = node[0, c, z] + zero[z]
            nodes[0, 1, c, z] = node[1, c, z] + 0.5 * (zero[z] + two[z])
            nodes[0, 2, c, z] = node[2, c, z] + two[z]

    @pl.when(has_next)
    def _():
        end_start()

    slope = s["slope"]
    for c in range(3):
        landed(fine_halo(3, c))
        own = first_own(speed[c, 0], speed[c, 1])
        for z in range(2):
            slope[c, z] = own[z] + (s["fh_low"][3, c, z] + s["fh_high"][3, c, z])

    turned = restricted(lambda c, z: slope[c, z])
    arrived(s["er"], s["c_rsem"].at[5])

    out = along_both([s["er"][pl.ds(c, PARTS, stride=2 * COARSE), :] for c in range(6)], t, "ci_y")
    change = [out[c] - co[UA2, c] for c in range(3)] + [out[3 + c] - turned[c] for c in range(3)]
    put = prolong(change, t)
    for c in range(3):
        for z in range(2):
            speed[c, z] = speed[c, z] + put[c][z]
            slope[c, z] = slope[c, z] + put[3 + c][z]
    for z in range(2):
        gx = [first_fine(speed[c, z], 0) for c in range(3)]
        gy = [first_fine(speed[c, z], 1) for c in range(3)]
        gz = [slope[c, z] for c in range(3)]
        diagonal = gx[0] * gx[0] + gy[1] * gy[1] + gz[2] * gz[2]
        mixed = gx[1] * gy[0] + gx[2] * gz[0] + gy[2] * gz[1]
        q_out[0, z] = -0.5 * diagonal - mixed

    for i in range(9):
        left(s["gs"].at[i], THIRD, s["g_ssem"].at[i], PARTS if i < 3 else PARTS - 1)
    for i in range(6):
        left(s["fs"].at[i], FINE, s["f_ssem"].at[i])
    for i in (0, 1, 3, 4):
        left(s["cs"].at[i], COARSE, s["c_ssem"].at[i])
    left(s["es"], 2 * COARSE, s["c_ssem"].at[5])

    @pl.when(jnp.logical_not(is_first))
    def _():
        left(s["cs"].at[2], COARSE, s["c_ssem"].at[2])
        gone(coarse_halo_copies(2))

    for i in (0, 1, 3):
        for c in range(3):
            gone(fine_halo(i, c))
    for i in (0, 1, 3, 4):
        gone(coarse_halo_copies(i))

    @pl.when(has_next)
    def _():
        left(s["cs"].at[5], COARSE, s["c_ssem"].at[6], PARTS)
        for copy in (start_copy, v_copy, m_copy):
            copy.wait_send()


def place(nodes, q, nodes_out, q_out, sems):
    copies = [pltpu.make_async_copy(q, q_out, sems.at[9])]
    for i in range(3):
        for c in range(3):
            copies.append(pltpu.make_async_copy(nodes.at[0, i, c], nodes_out.at[0, i, c], sems.at[3 * i + c]))
    for copy in copies:
        copy.start()
    for copy in copies:
        copy.wait()


def body(initial_state, end_states, old_tendencies):
    vmem = pl.BlockSpec(memory_space=pltpu.VMEM)
    operands = [initial_state, end_states, old_tendencies, jnp.asarray(PACKED_32), jnp.asarray(PACKED_16)]
    shapes = (
        jax.ShapeDtypeStruct((1, 3, 3, 2, N, N), f32),
        jax.ShapeDtypeStruct((1, 2, N, N), f32),
    )
    anywhere = pl.BlockSpec(memory_space=pl.ANY)
    results = pl.pallas_call(
        kernel,
        out_shape=shapes,
        in_specs=[anywhere] * len(operands),
        out_specs=(vmem, vmem),
        scratch_shapes=[pltpu.VMEM(x.shape, x.dtype) for x in operands] + list(SCRATCH.values()),
        compiler_params=pltpu.CompilerParams(
            collective_id=0, has_side_effects=True, vmem_limit_bytes=56 * 1024 * 1024
        ),
    )(*operands)
    return pl.pallas_call(
        place,
        out_shape=shapes,
        in_specs=[anywhere] * 2,
        out_specs=(anywhere, anywhere),
        scratch_shapes=[pltpu.SemaphoreType.DMA((10,))],
        compiler_params=pltpu.CompilerParams(vmem_limit_bytes=63 * 1024 * 1024),
    )(*results)


def solution(mesh):
    in_specs = (
        P(None, "space", None, None),
        P("tm", None, "space", None, None),
        P("tm", None, None, "space", None, None),
    )
    out_specs = (P("tm", None, None, "space", None, None), P("tm", "space", None, None))
    return jax.shard_map(body, mesh=mesh, in_specs=in_specs, out_specs=out_specs, check_vma=False)
```
